32 devices in a mesh: dp: 2 (over core), fsdp: 16 (over z, y, x).
Axes of the slice: x: 2, y: 2, z: 4, core: 2. Of those that a mesh axis runs over, the one named last changes fastest.
Arguments:
- images: bfloat16 [256, 256, 256], P(('dp', 'fsdp')), may hold values from -6 to 6
- timesteps: int32 [256], P(('dp', 'fsdp')), may hold values from 0 to 999
- labels: int32 [256], P(('dp', 'fsdp')), may hold values from 0 to 9
- valid_slot: int32 [256], P(('dp', 'fsdp')), may hold values from 0 to 1
- noise_idx: int32 [256, 256], P(('dp', 'fsdp')), may hold values from 0 to 255
- noise_table: float32 [256, 256], replicated, may hold values from -6 to 6
- params_a: float32 [1646592], P('fsdp')
- params_b: float32 [329728], P('fsdp')
- first_a: float32 [1646592], P('fsdp')
- second_a: float32 [1646592], P('fsdp')
- first_b: float32 [329728], P('fsdp')
- second_b: float32 [329728], P('fsdp')
Outputs:
- new_a: float32 [1646592], P('fsdp')
- moment_one_a: float32 [1646592], P('fsdp')
- moment_two_a: float32 [1646592], P('fsdp')
- copy_a: bfloat16 [1646592], P('fsdp')
- new_b: float32 [329728], P('fsdp')
- moment_one_b: float32 [329728], P('fsdp')
- moment_two_b: float32 [329728], P('fsdp')
- copy_b: bfloat16 [329728], P('fsdp')
- loss_sum: float32 [], replicated
- pixel_count: float32 [], replicated
- grad_norm: float32 [], replicated
The draws below stay inside these ranges and needn't reach their ends.
All inputs are finite; a program needn't handle non-finite values.
Results may differ from the reference program's by a relative error of at most 0.012.
Values may be sent and summed in bfloat16 or wider, within the bound.
A program may use at most 192 MiB of HBM per device.

```python
import math
import jax
import jax.numpy as jnp
import numpy as np
from jax import lax

C = 256
GROUPS = 32
SIDE = 16
POS = 256
TE = 512
SIN = 128
NCLS = 10
NT = 256
T_STEPS = 1000
STEP = 5
IMG_DEV = 8
IMAGES = 256
PA = 1646592
PB = 329728


clip_level = 0.01


def first_segments():
    return [(C, 0.1, 1.0), (C, 0.1, 0.0), (9 * C * C, (9 * C) ** (-0.5), 0.0), (C, 0.1, 0.0), (SIN * TE, SIN ** (-0.5), 0.0), (TE, 0.1, 0.0), (TE * TE, TE ** (-0.5), 0.0), (TE, 0.1, 0.0), (NCLS * TE, 1.0, 0.0), (TE * C, TE ** (-0.5), 0.0), (C, 0.1, 0.0), (C, 0.1, 1.0), (C, 0.1, 0.0), (9 * C * C, (9 * C) ** (-0.5), 0.0), (C, 0.1, 0.0)]


def second_segments():
    return [(C, 0.1, 1.0), (C, 0.1, 0.0), (3 * C * C, 1.4 * C ** (-0.5), 0.0), (2 * C, 0.1, 0.0), (C * C, 4.0 * C ** (-0.5), 0.0), (C, 0.1, 0.0), (C, 0.1, 1.0), (C, 0.1, 0.0), (C * C, C ** (-0.5), 0.0), (C, 0.1, 0.0)]


def flat_draw(key, segments, total_len):
    scale_parts = [np.full(length, value, np.float32) for length, value, _ in segments]
    base_parts = [np.full(length, centre, np.float32) for length, _, centre in segments]
    filled = sum((length for length, _, _ in segments))
    scale_parts.append(np.zeros(total_len - filled, np.float32))
    base_parts.append(np.zeros(total_len - filled, np.float32))
    noise_vec = jax.random.normal(key, (total_len,), jnp.float32)
    return jnp.asarray(np.concatenate(base_parts)) + jnp.asarray(np.concatenate(scale_parts)) * noise_vec


def moment_unit():
    return clip_level / math.sqrt(PA + PB)


def draw_params_a(key, part):
    key = jax.random.fold_in(key, 21)
    return flat_draw(key, first_segments(), PA)


def draw_params_b(key, part):
    key = jax.random.fold_in(key, 22)
    return flat_draw(key, second_segments(), PB)


def draw_first_a(key, part):
    key = jax.random.fold_in(key, 11)
    return jax.random.normal(key, (PA,), jnp.float32) * moment_unit()


def draw_second_a(key, part):
    key = jax.random.fold_in(key, 12)
    return jax.random.uniform(key, (PA,), jnp.float32, 1.0, 4.0) * moment_unit() ** 2


def draw_first_b(key, part):
    key = jax.random.fold_in(key, 13)
    return jax.random.normal(key, (PB,), jnp.float32) * moment_unit()


def draw_second_b(key, part):
    key = jax.random.fold_in(key, 14)
    return jax.random.uniform(key, (PB,), jnp.float32, 1.0, 4.0) * moment_unit() ** 2


def draw_valid_slot(key, part):
    key = jax.random.fold_in(key, 31)
    devices_all = IMAGES // IMG_DEV
    slot_ids = jnp.arange(IMAGES, dtype=jnp.int32)
    owners = slot_ids // IMG_DEV
    levels = 300 + 600 * owners // max(devices_all - 1, 1)
    dice_rolls = jax.random.randint(key, (IMAGES,), 0, 1000, dtype=jnp.int32)
    return jnp.where((dice_rolls < levels) | (slot_ids == 0), 1, 0).astype(jnp.int32)


def place_ends(values, rng, low, high):
    index_at = [jax.random.randint(jax.random.fold_in(rng, axis), (), 0, length) for axis, length in enumerate(values.shape)]
    longest = values.shape.index(max(values.shape))
    neighbour = index_at[:longest] + [(index_at[longest] + 1) % values.shape[longest]] + index_at[longest + 1:]
    return values.at[tuple(index_at)].set(low).at[tuple(neighbour)].set(high)


def level_of(key, shape, cuts, low, top_value):
    level, own = 1.0, jax.random.fold_in(key, 6)
    for dim, parts in cuts:
        steps = jnp.exp(jax.random.uniform(jax.random.fold_in(own, dim), (parts,), jnp.float32, low / len(cuts), top_value / len(cuts)))
        level = level * jnp.repeat(steps, shape[dim] // parts).reshape([-1 if axis == dim else 1 for axis in range(len(shape))])
    return level


def rank_bounds(amount, slope):
    weights = [(1 << 20) // math.isqrt(grade ** slope) + 1 for grade in range(1, amount + 1)]
    width = 1 + sum(weights) // (1 << 30)
    return np.cumsum(np.array([max(1, weight // width) for weight in weights]))


def ranked(key, shape, count, slope):
    grid = rank_bounds(count, slope)
    pick = jax.random.randint(jax.random.fold_in(key, 1), shape, 0, int(grid[count - 1]))
    grade = jnp.searchsorted(jnp.asarray(grid, jnp.int32), pick, side="right")
    return jax.random.permutation(jax.random.fold_in(key, 2), count)[grade].astype(jnp.int32)


def normal_values(own_key, shape, scale, reach, cuts=(), kind=jnp.bfloat16):
    values = scale * jax.random.normal(own_key, shape, jnp.float32)
    if cuts:
        values = values * level_of(own_key, shape, cuts, -0.22, 0.18)
    return jnp.clip(values, -reach, reach).astype(kind)


def setup_inputs(seed: int = 0) -> dict:
    splits = jax.random.split(jax.random.key(seed), 13)
    images = normal_values(splits[0], (IMAGES, POS, C), 1.0, 6.0, ((0, 32),))
    timesteps = place_ends(jax.random.randint(splits[1], (IMAGES,), 0, T_STEPS), jax.random.fold_in(splits[1], 1), 0, T_STEPS - 1).astype(jnp.int32)
    labels = place_ends(ranked(splits[2], (IMAGES,), NCLS, 2), jax.random.fold_in(splits[2], 3), 0, NCLS - 1).astype(jnp.int32)
    valid_slot = draw_valid_slot(jax.random.fold_in(splits[12], 71), 0)
    noise_idx = place_ends(jax.random.randint(splits[4], (IMAGES, POS), 0, NT), jax.random.fold_in(splits[4], 1), 0, NT - 1).astype(jnp.int32)
    noise_table = normal_values(splits[5], (NT, C), 1.0, 6.0, (), jnp.float32)
    params_a = draw_params_a(jax.random.fold_in(splits[12], 71), 0)
    params_b = draw_params_b(jax.random.fold_in(splits[12], 71), 0)
    first_a = draw_first_a(jax.random.fold_in(splits[12], 71), 0)
    second_a = draw_second_a(jax.random.fold_in(splits[12], 71), 0)
    first_b = draw_first_b(jax.random.fold_in(splits[12], 71), 0)
    second_b = draw_second_b(jax.random.fold_in(splits[12], 71), 0)
    return dict(images=images, timesteps=timesteps, labels=labels, valid_slot=valid_slot, noise_idx=noise_idx, noise_table=noise_table, params_a=params_a, params_b=params_b, first_a=first_a, second_a=second_a, first_b=first_b, second_b=second_b)


@jax.custom_vjp
def low(v):
    return lax.optimization_barrier(v.astype(jnp.bfloat16)).astype(jnp.float32)

@jax.custom_vjp
def low_back(v):
    return v

def low_keep(v):
    return (low(v), None)

def low_pass(kept, grad):
    return (grad,)

def back_keep(v):
    return (v, None)

def back_low(kept, grad):
    return (low(grad),)
low.defvjp(low_keep, low_pass)
low_back.defvjp(back_keep, back_low)
eps_norm = 1e-05
beta_one = 0.5
beta_two = 0.5
learn_rate = 0.1
decay_rate = 0.01
adam_eps = 1e-08
clip_level = 0.01
highest = lax.Precision.HIGHEST

def first_shapes():
    return [(2, C), (9 * C, C), (C,), (SIN, TE), (TE,), (TE, TE), (TE,), (NCLS, TE), (TE, C), (C,), (2, C), (9 * C, C), (C,)]

def second_shapes():
    return [(2, C), (C, 3 * C), (2 * C,), (C, C), (C,), (2, C), (C, C), (C,)]

def unpack(vector, shapes):
    result = []
    offset = 0
    for extent in shapes:
        length = math.prod(extent)
        result.append(vector[offset:offset + length].reshape(extent))
        offset += length
    return result

def swish(v):
    return v * jax.nn.sigmoid(v)

def group_norm(values, gain_bias):
    grouped = values.reshape(values.shape[0], values.shape[1], GROUPS, C // GROUPS)
    centre = grouped - lax.optimization_barrier(jnp.mean(grouped, axis=(1, 3), keepdims=True))
    spread = lax.optimization_barrier(jnp.mean(centre * centre, axis=(1, 3), keepdims=True))
    scaled = (centre * lax.rsqrt(spread + eps_norm)).reshape(values.shape)
    return scaled * gain_bias[0] + gain_bias[1]

def sinusoid(steps_in):
    half_dim = SIN // 2
    factor = math.log(10000.0) / (half_dim - 1)
    frequency = jnp.exp(jnp.arange(half_dim, dtype=jnp.float32) * -factor)
    angles = steps_in.astype(jnp.float32)[:, None] * frequency[None, :]
    return jnp.concatenate([jnp.sin(angles), jnp.cos(angles)], axis=1)

def conv_three(values, kernel):
    count_img = values.shape[0]
    planes = values.reshape(count_img, SIDE, SIDE, C)
    padded = jnp.pad(planes, ((0, 0), (1, 1), (1, 1), (0, 0)))
    columns = jnp.concatenate([padded[:, r:r + SIDE, s:s + SIDE, :] for r in range(3) for s in range(3)], axis=3)
    output = jnp.dot(columns.reshape(count_img * POS, 9 * C), kernel, precision=highest, preferred_element_type=jnp.float32)
    return output.reshape(count_img, POS, C)

def group_loss(master_a, master_b, h_zero, steps_in, classes, valid_f, target, total_count):
    norm_one, kernel_one, bias_one, time_w1, time_b1, time_w2, time_b2, class_table, proj_time, proj_bias, norm_two, kernel_two, bias_two = unpack(low(master_a), first_shapes())
    norm_three, triple_weight, qv_bias, out_weight, out_bias, norm_four, head_weight, head_bias = unpack(low(master_b), second_shapes())
    embedding = sinusoid(steps_in)
    hidden_one = swish(jnp.dot(embedding, time_w1, precision=highest) + time_b1)
    time_embed = jnp.dot(hidden_one, time_w2, precision=highest) + time_b2 + class_table[classes]
    time_add = jnp.dot(swish(time_embed), proj_time, precision=highest) + proj_bias
    x_one = low(swish(group_norm(h_zero, norm_one)))
    c_one = low_back(conv_three(x_one, kernel_one)) + bias_one + time_add[:, None, :]
    x_two = low(swish(group_norm(c_one, norm_two)))
    h_one = h_zero + low_back(conv_three(x_two, kernel_two)) + bias_two
    x_three = low(group_norm(h_one, norm_three))
    bias_all = jnp.concatenate([qv_bias[:C], jnp.zeros((C,), jnp.float32), qv_bias[C:]])
    triple = low(low_back(jnp.einsum('npc,cd->npd', x_three, triple_weight, precision=highest) + bias_all))
    queries, attn_keys, attn_values = (triple[..., :C], triple[..., C:2 * C], triple[..., 2 * C:])
    scores = low_back(jnp.einsum('npc,nqc->npq', queries, attn_keys, precision=highest) * C ** (-0.5))
    row_peak = lax.optimization_barrier(jnp.max(scores, axis=2, keepdims=True))
    log_total = row_peak + jnp.log(lax.optimization_barrier(jnp.sum(jnp.exp(scores - row_peak), axis=2, keepdims=True)))
    attn_probs = low(jnp.exp(scores - log_total))
    attn_mixed = low(low_back(jnp.einsum('npq,nqc->npc', attn_probs, attn_values, precision=highest)))
    h_two = h_one + low_back(jnp.einsum('npc,cd->npd', attn_mixed, out_weight, precision=highest)) + out_bias
    x_four = low(swish(group_norm(h_two, norm_four)))
    predict = low_back(jnp.einsum('npc,cd->npd', x_four, head_weight, precision=highest)) + head_bias
    differ = predict - target
    summed = jnp.sum(valid_f[:, None, None] * differ * differ)
    return (summed / total_count, summed)

def adam_update(master, grad_in, first_mom, second, clip_scale):
    clipped = grad_in * clip_scale
    first_new = beta_one * first_mom + (1.0 - beta_one) * clipped
    second_new = beta_two * second + (1.0 - beta_two) * clipped * clipped
    first_hat = first_new / (1.0 - beta_one ** STEP)
    second_hat = second_new / (1.0 - beta_two ** STEP)
    master_new = master - learn_rate * (first_hat / (jnp.sqrt(second_hat) + adam_eps) + decay_rate * master)
    return (master_new, first_new, second_new)

def reference(images, timesteps, labels, valid_slot, noise_idx, noise_table, params_a, params_b, first_a, second_a, first_b, second_b):
    total_count = jnp.sum(valid_slot).astype(jnp.float32) * POS
    group_count = IMAGES // IMG_DEV

    def one_group(running, slot_index):
        row_start = (slot_index * IMG_DEV).astype(jnp.int32)
        h_zero = lax.dynamic_slice_in_dim(images, row_start, IMG_DEV, 0).astype(jnp.float32)
        steps_in = lax.dynamic_slice_in_dim(timesteps, row_start, IMG_DEV, 0)
        classes = lax.dynamic_slice_in_dim(labels, row_start, IMG_DEV, 0)
        valid_f = lax.dynamic_slice_in_dim(valid_slot, row_start, IMG_DEV, 0).astype(jnp.float32)
        noise_rows = lax.dynamic_slice_in_dim(noise_idx, row_start, IMG_DEV, 0)
        target = noise_table[noise_rows]

        def closure(master_a, master_b):
            return group_loss(master_a, master_b, h_zero, steps_in, classes, valid_f, target, total_count)
        _, pullback, summed = jax.vjp(closure, params_a, params_b, has_aux=True)
        grad_a, grad_b = pullback(jnp.ones((), jnp.float32))
        return ((running[0] + grad_a, running[1] + grad_b, running[2] + summed), None)
    initial = (jnp.zeros((PA,), jnp.float32), jnp.zeros((PB,), jnp.float32), jnp.zeros((), jnp.float32))
    (grad_a, grad_b, loss_total), _ = lax.scan(one_group, initial, jnp.arange(group_count, dtype=jnp.int32))
    norm_value = jnp.sqrt(jnp.sum(grad_a * grad_a) + jnp.sum(grad_b * grad_b))
    clip_scale = jnp.minimum(1.0, clip_level / (norm_value + 1e-06))
    new_a, mom_one_a, mom_two_a = adam_update(params_a, grad_a, first_a, second_a, clip_scale)
    new_b, mom_one_b, mom_two_b = adam_update(params_b, grad_b, first_b, second_b, clip_scale)
    return (new_a, mom_one_a, mom_two_a, new_a.astype(jnp.bfloat16), new_b, mom_one_b, mom_two_b, new_b.astype(jnp.bfloat16), loss_total, total_count, norm_value)
```

```python
import functools
import math
import jax
import jax.numpy as jnp
import numpy as np
from jax import lax
from jax.experimental import pallas as pl
from jax.experimental.pallas import tpu as pltpu
from jax.sharding import PartitionSpec as P

C = 256
SIDE = 16
POS = 256
TE = 512
SIN = 128
NCLS = 10
NT = 256
NIMG = 8
bf = jnp.bfloat16
f32 = jnp.float32
eps_norm = 1e-05
CH = 64
TY = 2

A_N1, A_K1, A_B1, A_W1, A_TB1, A_W2, A_TB2, A_CT, A_PT, A_PB, A_N2, A_K2, A_B2 = (
    0, 2, 2306, 2307, 2563, 2565, 3589, 3591, 3611, 4123, 4124, 4126, 6430)
A_ROWS = 6432
B_N3, B_W, B_QV, B_WO, B_BO, B_N4, B_WH, B_BH = (0, 2, 770, 772, 1028, 1029, 1031, 1287)
B_ROWS = 1288


def dot(a, b):
    return jnp.dot(a, b, preferred_element_type=f32)


def dot_nt(a, b):
    return lax.dot_general(a, b, (((1,), (1,)), ((), ())), preferred_element_type=f32)


def dot_tn(a, b):
    return lax.dot_general(a, b, (((0,), (0,)), ((), ())), preferred_element_type=f32)


def split3(x):
    hi = x.astype(bf).astype(f32)
    rest = x - hi
    mid = rest.astype(bf).astype(f32)
    return hi, mid, rest - mid


def wide_dot(x, w, nt=False):
    n = x.shape[0]
    stacked = jnp.concatenate(split3(x), axis=0).astype(bf)
    out = dot_nt(stacked, w) if nt else dot(stacked, w)
    return out[:n] + out[n:2 * n] + out[2 * n:]


def outer_sum(a, b):
    a0, a1, _ = split3(a)
    b0, b1, _ = split3(b)
    return dot_tn(jnp.concatenate([a0, a0, a1], axis=0).astype(bf),
                  jnp.concatenate([b0, b1, b0], axis=0).astype(bf))


def sigm(v):
    return 0.5 * jnp.tanh(0.5 * v) + 0.5


def rowsum(x):
    return jnp.sum(x, axis=0, keepdims=True)


def put_shifts(buf, i, r0, x):
    n = x.shape[0]
    col = lax.broadcasted_iota(jnp.int32, x.shape, 0) & 15
    left = jnp.where(col == 0, 0.0, pltpu.roll(x, 1, 0))
    right = jnp.where(col == 15, 0.0, pltpu.roll(x, n - 1, 0))
    y = n // 16
    for s, v in enumerate((left, x, right)):
        buf[pl.ds(1 + r0 // 16, y), i, :, 256 * s:256 * s + 256] = v.astype(bf).reshape(y, 16, C)


def conv_mm(buf, kmat, y, ty=TY):
    parts = [buf[pl.ds(y + r, ty)].reshape(ty * 128, 3 * C) for r in range(3)]
    return dot(jnp.concatenate(parts, axis=1), kmat[...])


class Refs:
    pass


def ld(f, row, n, stride=1):
    at = pl.ds(row, n, stride=stride) if stride > 1 else pl.ds(row, n)
    return jnp.concatenate([f[0, at, :], f[1, at, :]], axis=1)


def st(f, row, value, stride=1):
    n = value.shape[0]
    at = pl.ds(row, n, stride=stride) if stride > 1 else pl.ds(row, n)
    f[0, at, :] = value[:, :128]
    f[1, at, :] = value[:, 128:]


def unpack_weights(R, fa, fb):
    for kmat, kt, base in ((R.k1, R.k1t, A_K1), (R.k2, R.k2t, A_K2)):
        for t in range(9):
            w = ld(fa, base + 256 * t, 256)
            kmat[256 * t:256 * t + 256, :] = w.astype(bf)
            kt[256 * (8 - t):256 * (8 - t) + 256, :] = w.T.astype(bf)
    for h in range(2):
        R.tw1[:, 256 * h:256 * h + 256] = ld(fa, A_W1 + h, SIN, 2).astype(bf)
        R.tw2[:, 256 * h:256 * h + 256] = ld(fa, A_W2 + h, TE, 2).astype(bf)
    R.pt[...] = ld(fa, A_PT, TE).astype(bf)
    for h in range(3):
        w = ld(fb, B_W + h, C, 3)
        R.wt[:, 256 * h:256 * h + 256] = w.astype(bf)
        R.wtt[256 * h:256 * h + 256, :] = w.T.astype(bf)
    w = ld(fb, B_WO, C)
    R.wo[...] = w.astype(bf)
    R.wot[...] = w.T.astype(bf)
    w = ld(fb, B_WH, C)
    R.wh[...] = w.astype(bf)
    R.wht[...] = w.T.astype(bf)
    for k, row in enumerate((A_N1, A_N1 + 1, A_B1, A_TB1, A_TB1 + 1, A_TB2, A_TB2 + 1, A_PB, A_N2, A_N2 + 1, A_B2)):
        R.vec[k:k + 1, :] = ld(fa, row, 1)
    for k, row in enumerate((B_N3, B_N3 + 1, B_QV, B_QV + 1, B_BO, B_N4, B_N4 + 1, B_BH)):
        R.vec[11 + k:12 + k, :] = ld(fb, row, 1)
    R.ct[0:20, :] = ld(fa, A_CT, 20)


(V_G1, V_C1, V_B1, V_TB1, V_TB1B, V_TB2, V_TB2B, V_PB, V_G2, V_C2, V_B2,
 V_G3, V_C3, V_QB, V_VB, V_BO, V_G4, V_C4, V_BH) = range(19)


def vec(R, k):
    return R.vec[k:k + 1, :]


def group_mean(R, s):
    return wide_dot(s, R.gm[...])


def stats(R, k, load):
    for i in range(NIMG):
        R.tmp[i:i + 1, :] = rowsum(load(i))
    mean = group_mean(R, R.tmp[0:8, :])
    R.mean[k] = mean
    for i in range(NIMG):
        x = load(i) - mean[i:i + 1, :]
        R.tmp[i:i + 1, :] = rowsum(x * x)
    R.inv[k] = lax.rsqrt(group_mean(R, R.tmp[0:8, :]) + eps_norm)


def norm_sums(R, k, gain):
    s1, s2 = R.s1[...], R.s2[...]
    m = group_mean(R, jnp.concatenate([s1 * gain, s2 * gain], axis=0))
    R.m1[...] = m[:8] * R.inv[k]
    R.m2[...] = m[8:] * R.inv[k]
    return rowsum(s2), rowsum(s1)


def first_setup(R):
    row = lax.broadcasted_iota(jnp.int32, (C, C), 0) >> 3
    col = lax.broadcasted_iota(jnp.int32, (C, C), 1) >> 3
    R.gm[...] = jnp.where(row == col, 1.0 / 2048.0, 0.0).astype(bf)
    zero = jnp.zeros((1, NIMG, 16, 3 * C), bf)
    for buf in (R.buf1, R.buf2, R.dbuf):
        buf[0:1] = zero
        buf[17:18] = zero
    hi, mid, lo = split3(R.table[...])
    R.tab3[...] = jnp.concatenate([hi, mid, lo], axis=1).astype(bf)

    @pl.loop(0, NIMG)
    def _(i):
        rows = lax.broadcasted_iota(jnp.int32, (NT, POS), 0)
        hot = jnp.where(rows == R.nidx[pl.ds(i, 1), :], 1.0, 0.0)
        out = dot(hot.T.astype(bf), R.tab3[...])
        R.target[i] = out[:, :C] + out[:, C:2 * C] + out[:, 2 * C:]
    stats(R, 0, lambda i: R.img[i].astype(f32))


def column_of(smem, shape):
    row = lax.broadcasted_iota(jnp.int32, shape, 0)
    out = jnp.zeros(shape, jnp.int32)
    for i in range(NIMG):
        out = jnp.where(row == i, smem[i], out)
    return out


def time_forward(R):
    lane = lax.broadcasted_iota(jnp.int32, (NIMG, SIN), 1)
    factor = math.log(10000.0) / (SIN // 2 - 1)
    freq = jnp.exp((lane & 63).astype(f32) * -factor)
    angle = column_of(R.steps, (NIMG, SIN)).astype(f32) * freq
    e = jnp.where(lane < 64, jnp.sin(angle), jnp.cos(angle))
    R.emb[...] = e
    u = wide_dot(e, R.tw1[...]) + jnp.concatenate([vec(R, V_TB1), vec(R, V_TB1B)], axis=1)
    R.pre[...] = u
    lab = column_of(R.labels, (NIMG, TE))
    te = wide_dot(u * sigm(u), R.tw2[...]) + jnp.concatenate([vec(R, V_TB2), vec(R, V_TB2B)], axis=1)
    for j in range(NCLS):
        row = jnp.concatenate([R.ct[2 * j:2 * j + 1, :], R.ct[2 * j + 1:2 * j + 2, :]], axis=1)
        te = te + jnp.where(lab == j, row, 0.0)
    R.te[...] = te
    add = wide_dot(te * sigm(te), R.pt[...]) + vec(R, V_PB) + vec(R, V_B1)
    for i in range(NIMG):
        R.addb[i] = jnp.broadcast_to(add[i:i + 1, :], (16, C))


def each_chunk(fn):
    @pl.loop(0, NIMG)
    def _(i):
        for c in range(POS // CH):
            fn(i, c * CH)


def normed(R, k, i, x):
    return (x - R.mean[k, pl.ds(i, 1), :]) * R.inv[k, pl.ds(i, 1), :]


def forward_a(R):
    def one(i, r0):
        x = normed(R, 0, i, R.img[i, r0:r0 + CH, :].astype(f32))
        a = x * vec(R, V_G1) + vec(R, V_C1)
        put_shifts(R.buf1, i, r0, a * sigm(a))
    each_chunk(one)

    @pl.loop(0, SIDE // TY)
    def _(t):
        acc = conv_mm(R.buf1, R.k1, t * TY).reshape(TY, NIMG, 16, C)
        for yy in range(TY):
            R.c1[:, pl.ds(pl.multiple_of((t * TY + yy) * 16, 16), 16), :] = acc[yy] + R.addb[...]
    stats(R, 1, lambda i: R.c1[i])

    def two(i, r0):
        x = normed(R, 1, i, R.c1[i, r0:r0 + CH, :])
        a = x * vec(R, V_G2) + vec(R, V_C2)
        put_shifts(R.buf2, i, r0, a * sigm(a))
    each_chunk(two)

    @pl.loop(0, SIDE // TY)
    def _(t):
        acc = conv_mm(R.buf2, R.k2, t * TY).reshape(TY, NIMG, 16, C)
        for yy in range(TY):
            at = pl.ds(pl.multiple_of((t * TY + yy) * 16, 16), 16)
            R.h1[:, at, :] = acc[yy] + R.img[:, at, :].astype(f32) + vec(R, V_B2)
    stats(R, 2, lambda i: R.h1[i])


def forward_b(R):
    bias = jnp.concatenate([vec(R, V_QB), jnp.zeros((1, C), f32), vec(R, V_VB)], axis=1)

    @pl.loop(0, NIMG)
    def _(i):
        x = (normed(R, 2, i, R.h1[i]) * vec(R, V_G3) + vec(R, V_C3)).astype(bf)
        R.x3t[:, pl.ds(pl.multiple_of(i * POS, POS), POS)] = x.T
        R.tri[i] = (dot(x, R.wt[...]) + bias).astype(bf)

    @pl.loop(0, NIMG)
    def _(i):
        k = R.tri[i, :, C:2 * C]
        v = R.tri[i, :, 2 * C:]
        for h in range(2):
            at = slice(128 * h, 128 * h + 128)
            s = dot_nt(R.tri[i, at, 0:C], k) * C ** (-0.5)
            e = jnp.exp(s - jnp.max(s, axis=1, keepdims=True))
            p = e * (1.0 / jnp.sum(e, axis=1, keepdims=True))
            R.p[i, at, :] = p
            o = dot(p.astype(bf), v).astype(bf)
            R.o[i, at, :] = o
            R.h2[i, at, :] = R.h1[i, at, :] + dot(o, R.wo[...]) + vec(R, V_BO)
    stats(R, 3, lambda i: R.h2[i])


def head(R, scale):
    R.loss[...] = jnp.zeros_like(R.loss)
    R.sh[...] = jnp.zeros_like(R.sh)

    @pl.loop(0, NIMG)
    def _(i):
        valid = R.valid[i].astype(f32)
        s1 = jnp.zeros((1, C), f32)
        s2 = jnp.zeros((1, C), f32)
        for h in range(2):
            at = slice(128 * h, 128 * h + 128)
            x = normed(R, 3, i, R.h2[i, at, :])
            a = x * vec(R, V_G4) + vec(R, V_C4)
            sg = sigm(a)
            x4 = (a * sg).astype(bf)
            R.xt[:, pl.ds(pl.multiple_of(i * POS + 128 * h, 128), 128)] = x4.T
            differ = dot(x4, R.wh[...]) + vec(R, V_BH) - R.target[i, at, :]
            dv = valid * differ
            R.loss[...] += rowsum(dv * differ)
            dp = dv * scale
            R.sh[...] += rowsum(dp)
            low = dp.astype(bf)
            R.low[i, at, :] = low
            da = dot(low, R.wht[...]) * (sg * (1.0 + a * (1.0 - sg)))
            R.da[i, at, :] = da
            s1 += rowsum(da)
            s2 += rowsum(da * x)
        R.s1[pl.ds(i, 1), :] = s1
        R.s2[pl.ds(i, 1), :] = s2


def weight_grad(R, xt, low, put):
    put(dot(xt[...], low[...].reshape(NIMG * POS, low.shape[-1])))


def backward_b(R):
    st(R.gb, B_BH, R.sh[...])
    st(R.gb, B_WH, dot(R.xt[...], R.low[...].reshape(NIMG * POS, C)))
    dg, db = norm_sums(R, 3, vec(R, V_G4))
    st(R.gb, B_N4, dg)
    st(R.gb, B_N4 + 1, db)
    R.sh[...] = jnp.zeros_like(R.sh)
    R.sq[...] = jnp.zeros_like(R.sq)

    @pl.loop(0, NIMG)
    def _(i):
        x = normed(R, 3, i, R.h2[i])
        d = (R.inv[3, pl.ds(i, 1), :] * vec(R, V_G4)) * R.da[i] - R.m1[pl.ds(i, 1), :] - x * R.m2[pl.ds(i, 1), :]
        R.dh[i] = d
        R.sh[...] += rowsum(d)
        low = d.astype(bf)
        R.low[i] = low
        R.xt[:, pl.ds(pl.multiple_of(i * POS, POS), POS)] = R.o[i].T
        dm = dot(low, R.wot[...]).astype(bf)
        p = R.p[i]
        q = R.tri[i, :, 0:C]
        k = R.tri[i, :, C:2 * C]
        v = R.tri[i, :, 2 * C:]
        dv = dot_tn(p.astype(bf), dm).astype(bf)
        dpr = dot_nt(dm, v)
        ds = (p * (dpr - jnp.sum(dpr * p, axis=1, keepdims=True))).astype(bf)
        dq = (dot(ds, k) * C ** (-0.5)).astype(bf)
        dk = (dot_tn(ds, q) * C ** (-0.5)).astype(bf)
        R.tri[i, :, 0:C] = dq
        R.tri[i, :, C:2 * C] = dk
        R.tri[i, :, 2 * C:] = dv
        R.sq[:, 0:C] += rowsum(dq.astype(f32))
        R.sq[:, C:2 * C] += rowsum(dv.astype(f32))
    st(R.gb, B_BO, R.sh[...])
    st(R.gb, B_QV, R.sq[:, 0:C])
    st(R.gb, B_QV + 1, R.sq[:, C:2 * C])
    st(R.gb, B_WO, dot(R.xt[...], R.low[...].reshape(NIMG * POS, C)))

    @pl.loop(0, NIMG)
    def _(i):
        da = dot(R.tri[i], R.wtt[...])
        R.da[i] = da
        R.s1[pl.ds(i, 1), :] = rowsum(da)
        R.s2[pl.ds(i, 1), :] = rowsum(da * normed(R, 2, i, R.h1[i]))
    for h in range(3):
        st(R.gb, B_W + h, dot(
            R.x3t[...], R.tri[:, :, 256 * h:256 * h + 256].reshape(NIMG * POS, C)), 3)
    dg, db = norm_sums(R, 2, vec(R, V_G3))
    st(R.gb, B_N3, dg)
    st(R.gb, B_N3 + 1, db)


def kernel_grad(R, buf, row):
    @pl.loop(0, SIDE // 2)
    def _(t):
        x = buf[pl.ds(1 + 2 * t, 2), :, :, C:2 * C].reshape(256, C)
        R.xt[:, pl.ds(pl.multiple_of(t * 256, 256), 256)] = x.T
    for r in range(3):
        for s in range(3):
            d = R.dbuf[2 - r:18 - r, :, :, 256 * (2 - s):256 * (3 - s)].reshape(NIMG * POS, C)
            at = row + (3 * r + s) * 256
            st(R.ga, at, dot(R.xt[...], d))


def conv_back(R, kt):
    @pl.loop(0, SIDE // TY)
    def _(t):
        acc = conv_mm(R.dbuf, kt, t * TY).reshape(TY, NIMG, 16, C)
        for yy in range(TY):
            R.da[:, pl.ds(pl.multiple_of((t * TY + yy) * 16, 16), 16), :] = acc[yy]


def swish_back(R, k, load, vg, vc, keep):
    R.s1[...] = jnp.zeros_like(R.s1)
    R.s2[...] = jnp.zeros_like(R.s2)

    def one(i, r0):
        x = normed(R, k, i, load(i, r0))
        a = x * vec(R, vg) + vec(R, vc)
        sg = sigm(a)
        da = R.da[i, r0:r0 + CH, :] * (sg * (1.0 + a * (1.0 - sg)))
        if keep:
            R.da[i, r0:r0 + CH, :] = da
        R.s1[pl.ds(i, 1), :] += rowsum(da)
        R.s2[pl.ds(i, 1), :] += rowsum(da * x)
    each_chunk(one)


def backward_a(R):
    R.sh[...] = jnp.zeros_like(R.sh)

    def one(i, r0):
        at = slice(r0, r0 + CH)
        x = normed(R, 2, i, R.h1[i, at, :])
        d = (R.dh[i, at, :] + (R.inv[2, pl.ds(i, 1), :] * vec(R, V_G3)) * R.da[i, at, :]
             - R.m1[pl.ds(i, 1), :] - x * R.m2[pl.ds(i, 1), :])
        R.sh[...] += rowsum(d)
        put_shifts(R.dbuf, i, r0, d)
    each_chunk(one)
    st(R.ga, A_B2, R.sh[...])
    kernel_grad(R, R.buf2, A_K2)
    conv_back(R, R.k2t)
    swish_back(R, 1, lambda i, r0: R.c1[i, r0:r0 + CH, :], V_G2, V_C2, True)
    dg, db = norm_sums(R, 1, vec(R, V_G2))
    st(R.ga, A_N2, dg)
    st(R.ga, A_N2 + 1, db)
    R.tmp[...] = jnp.zeros_like(R.tmp)

    def two(i, r0):
        at = slice(r0, r0 + CH)
        x = normed(R, 1, i, R.c1[i, at, :])
        d = ((R.inv[1, pl.ds(i, 1), :] * vec(R, V_G2)) * R.da[i, at, :]
             - R.m1[pl.ds(i, 1), :] - x * R.m2[pl.ds(i, 1), :])
        R.tmp[pl.ds(i, 1), :] += rowsum(d)
        put_shifts(R.dbuf, i, r0, d)
    each_chunk(two)
    time_backward(R)
    kernel_grad(R, R.buf1, A_K1)
    conv_back(R, R.k1t)
    swish_back(R, 0, lambda i, r0: R.img[i, r0:r0 + CH, :].astype(f32), V_G1, V_C1, False)
    st(R.ga, A_N1, rowsum(R.s2[...]))
    st(R.ga, A_N1 + 1, rowsum(R.s1[...]))


def swish_slope(v):
    s = sigm(v)
    return s * (1.0 + v * (1.0 - s))


def time_backward(R):
    d_add = R.tmp[0:8, :]
    total = rowsum(d_add)
    st(R.ga, A_B1, total)
    st(R.ga, A_PB, total)
    te = R.te[...]
    st(R.ga, A_PT, outer_sum(te * sigm(te), d_add))
    d_te = wide_dot(d_add, R.pt[...], nt=True) * swish_slope(te)
    lab = column_of(R.labels, (NIMG, TE))
    for j in range(NCLS):
        row = rowsum(jnp.where(lab == j, d_te, 0.0))
        for h in range(2):
            st(R.ga, A_CT + 2 * j + h, row[:, 256 * h:256 * h + 256])
    row = rowsum(d_te)
    u = R.pre[...]
    dw2 = outer_sum(u * sigm(u), d_te)
    d_u = wide_dot(d_te, R.tw2[...], nt=True) * swish_slope(u)
    row1 = rowsum(d_u)
    dw1 = outer_sum(R.emb[...], d_u)
    for h in range(2):
        st(R.ga, A_TB2 + h, row[:, 256 * h:256 * h + 256])
        st(R.ga, A_TB1 + h, row1[:, 256 * h:256 * h + 256])
        st(R.ga, A_W2 + h, dw2[:, 256 * h:256 * h + 256], 2)
        st(R.ga, A_W1 + h, dw1[:, 256 * h:256 * h + 256], 2)


SCRATCH = dict(
    k1=((2304, C), bf), k1t=((2304, C), bf), k2=((2304, C), bf), k2t=((2304, C), bf),
    tw1=((SIN, TE), bf), tw2=((TE, TE), bf), pt=((TE, C), bf),
    wt=((C, 3 * C), bf), wtt=((3 * C, C), bf), wo=((C, C), bf), wot=((C, C), bf), wh=((C, C), bf), wht=((C, C), bf),
    vec=((24, C), f32), ct=((24, C), f32),
    gm=((C, C), bf), tab3=((NT, 3 * C), bf), target=((NIMG, POS, C), f32),
    tmp=((8, C), f32), mean=((4, 8, C), f32), inv=((4, 8, C), f32),
    s1=((8, C), f32), s2=((8, C), f32), m1=((8, C), f32), m2=((8, C), f32),
    sh=((1, C), f32), sq=((1, 2 * C), f32),
    emb=((8, SIN), f32), pre=((8, TE), f32), te=((8, TE), f32), addb=((8, 16, C), f32),
    buf1=((18, 8, 16, 3 * C), bf), buf2=((18, 8, 16, 3 * C), bf), dbuf=((18, 8, 16, 3 * C), bf),
    c1=((8, POS, C), f32), h1=((8, POS, C), f32), h2=((8, POS, C), f32), da=((8, POS, C), f32), dh=((8, POS, C), f32),
    p=((8, POS, POS), f32), o=((8, POS, C), bf), low=((8, POS, C), bf),
    tri=((8, POS, 3 * C), bf),
    x3t=((C, 8 * POS), bf), xt=((C, 8 * POS), bf),
)


def main_kernel(names_in, *refs):
    R = Refs()
    n_in = len(names_in)
    for name, r in zip(names_in, refs):
        setattr(R, name, r)
    R.ga, R.gb, R.loss = refs[n_in:n_in + 3]
    for name, r in zip(list(SCRATCH), refs[n_in + 3:]):
        setattr(R, name, r)
    fa, fb = R.ga, R.gb
    for c in range(0, A_ROWS, 402):
        st(fa, c, R.wa[c:c + 402, :].astype(f32))
    st(fb, 0, R.wb[...].astype(f32))
    first_setup(R)
    unpack_weights(R, fa, fb)
    time_forward(R)
    forward_a(R)
    forward_b(R)
    head(R, R.scale[0])
    backward_b(R)
    backward_a(R)


def compute(img, steps, labels, valid, scale, nidx, table, wa, wb):
    smem = pl.BlockSpec(memory_space=pltpu.SMEM)
    vmem = pl.BlockSpec(memory_space=pltpu.VMEM)
    names = ("img", "steps", "labels", "valid", "scale", "nidx", "table", "wa", "wb")
    return pl.pallas_call(
        functools.partial(main_kernel, names),
        out_shape=(jax.ShapeDtypeStruct((2, A_ROWS, 128), f32), jax.ShapeDtypeStruct((2, B_ROWS, 128), f32),
                   jax.ShapeDtypeStruct((1, C), f32)),
        in_specs=[vmem, smem, smem, smem, smem, vmem, vmem, vmem, vmem],
        out_specs=(vmem, vmem, vmem),
        scratch_shapes=[pltpu.VMEM(s, d) for s, d in SCRATCH.values()],
        compiler_params=pltpu.CompilerParams(vmem_limit_bytes=63 * 1024 * 1024),
    )(img, steps, labels, valid, scale, nidx, table, wa, wb)


beta_one = 0.5
beta_two = 0.5
learn_rate = 0.1
decay_rate = 0.01
adam_eps = 1e-08
clip_level = 0.01
STEP = 5
PA = A_ROWS * C
PB = B_ROWS * C
MESH = pl.DeviceIdType.MESH
ORDER = (0, 1, 3, 2)
HALF_A, HALF_B, PIECE = 201, 48, 256
B_AT = 208


class Place:
    def __init__(self, chips):
        self.me = lax.axis_index("fsdp")
        self.core = lax.axis_index("dp")
        self.depth = chips // 4

    def z(self, k, d):
        return lax.rem(lax.div(k, 4) + d + self.depth, self.depth) * 4 + lax.rem(k, 4)

    def flip_x(self, k):
        return k + 1 - 2 * lax.rem(k, 2)

    def flip_y(self, k):
        return k + 2 - 4 * lax.rem(lax.div(k, 2), 2)

    def s(self, k):
        return self.core * self.flip_x(k) + (1 - self.core) * self.flip_y(k)

    def t(self, k):
        return self.core * self.flip_y(k) + (1 - self.core) * self.flip_x(k)

    def pieces(self):
        line = [self.z(self.me, -j) for j in range(4)]
        near = line + [self.s(k) for k in line]
        return near + [self.t(k) for k in near]


def send(src, dst, sems, at, core, chip):
    copy = pltpu.make_async_remote_copy(
        src_ref=src, dst_ref=dst, send_sem=sems[0].at[at], recv_sem=sems[1].at[at],
        device_id=(core, chip), device_id_type=MESH)
    copy.start()
    return copy


def greet(R, place, chips):
    barrier = pltpu.get_barrier_semaphore()
    for d in range(1, chips):
        pl.semaphore_signal(barrier, inc=1, device_id=(place.core, lax.rem(place.me + d, chips)), device_id_type=MESH)
    pl.semaphore_signal(barrier, inc=1, device_id=(1 - place.core, place.me), device_id_type=MESH)
    return barrier


def own_piece(R, place):
    count = R.valid[0]
    for i in range(1, NIMG):
        count = count + R.valid[i]
    count = count.astype(f32)
    odd = lax.rem(place.me, 2) == 1
    R.flat[0:8, :] = jnp.zeros((8, 128), f32)
    R.flat[168:184, :] = jnp.zeros((16, 128), f32)
    R.flat[8:169, :] = R.pb[...]
    for h in range(2):
        for lane in range(2):
            R.piece[lane, 0:201, :] = R.pa[pl.ds(402 * h + lane, 201, stride=2), :]
            even_rows = R.flat[pl.ds(8 + lane + 96 * h, 48 - 8 * h, stride=2), :]
            odd_rows = R.flat[pl.ds(7 + lane + 96 * h, 48 - 8 * h, stride=2), :]
            R.piece[lane, 208:256 - 8 * h, :] = jnp.where(odd, odd_rows, even_rows)
        R.piece[:, 201:208, :] = jnp.full((2, 7, 128), count)

        @pl.when(place.core == h)
        def _():
            R.w[place.me, h] = jnp.concatenate([R.piece[0], R.piece[1]], axis=1).astype(bf)


def gather_weights(R, place):
    me, core = place.me, place.core
    got = place.pieces()
    put = lambda k: R.w.at[k, core]
    over_s, over_t = place.s(me), place.t(me)
    zc = {d: send(put(me), put(me), R.zsem, d - 1, core, place.z(me, d)) for d in (1, 3, 2)}
    sc, tc, sib = {}, {}, {}
    for j in ORDER:
        if j:
            zc[j].wait_recv()
        sc[j] = send(put(got[j]), put(got[j]), R.ssem, j, core, over_s)
        tc[j] = send(put(got[j]), put(got[j]), R.tsem, j, core, over_t)
        sib[j] = send(put(got[j]), put(got[j]), R.csem, j, 1 - core, me)
    for j in ORDER:
        sc[j].wait_recv()
        q = 4 + j
        tc[q] = send(put(got[q]), put(got[q]), R.tsem, q, core, over_t)
        sib[q] = send(put(got[q]), put(got[q]), R.csem, q, 1 - core, me)
    for half in (0, 4):
        for j in ORDER:
            q = half + j
            tc[q].wait_recv()
            sib[8 + q] = send(put(got[8 + q]), put(got[8 + q]), R.csem, 8 + q, 1 - core, me)
    for c in sib.values():
        c.wait_recv()
    for group in (zc, sc, tc, sib):
        for c in group.values():
            c.wait_send()


def spread_rows(R, chips):
    count = jnp.zeros((1, 128), f32)
    for k in range(chips):
        base = (161 * k) // 2
        odd = k % 2
        for h in range(2):
            a = R.w[k, h, 0:208, :].astype(f32)
            row = 402 * k + 201 * h
            R.ga[0, row:row + 208, :] = a[:, :128]
            R.ga[1, row:row + 208, :] = a[:, 128:]
            count = count + a[201:202, :128]
            b = R.w[k, h, 208:256, :].astype(f32)
            if h == 0:
                R.gb[0, base + odd:base + 48, :] = b[odd:, :128]
                R.gb[1, base:base + 48, :] = b[:, 128:]
            else:
                R.gb[0, base + 48:base + 81, :] = b[:33, :128]
                R.gb[1, base + 48:base + 80 + odd, :] = b[:32 + odd, 128:]
    return count


def pack_gradients(R, chips):
    for k in range(chips):
        base = (161 * k) // 2
        for h in range(2):
            R.w[k, h, 0:208, :] = ld(R.ga, 402 * k + 201 * h, 208).astype(bf)
            R.w[k, h, 208:256, :] = ld(R.gb, base + 48 * h, 48).astype(bf)


def reduce_gradients(R, place):
    me, core = place.me, place.core
    got = place.pieces()
    over_s, over_t = place.s(me), place.t(me)
    order = [12 + j for j in ORDER] + [8 + j for j in ORDER]
    sib = {}
    for q in order[:4] + [4 + j for j in ORDER] + order[4:] + [1, 3, 2, 0]:
        there = q + 4 if 4 <= q < 8 else q - 4 if 8 <= q < 12 else q
        copy = pltpu.make_async_remote_copy(
            src_ref=R.w.at[got[q], 1 - core], dst_ref=R.r1.at[there], send_sem=R.gcsem[0].at[q],
            recv_sem=R.gcsem[1].at[there], device_id=(1 - core, me), device_id_type=MESH)
        copy.start()
        sib[there] = copy

    def total(q):
        return R.w[got[q], core].astype(f32) + R.r1[q].astype(f32)
    tc, sc, zc = {}, {}, {}
    for q in order:
        sib[q].wait_recv()
        R.t2[q - 8] = total(q).astype(bf)
        tc[q - 8] = send(R.t2.at[q - 8], R.r2.at[q - 8], R.gtsem, q - 8, core, over_t)
    for j in ORDER:
        q = 4 + j
        sib[q].wait_recv()
        tc[q].wait_recv()
        R.t3[j] = (total(q) + R.r2[q].astype(f32)).astype(bf)
        sc[j] = send(R.t3.at[j], R.r3.at[j], R.gssem, j, core, over_s)
    for j in (1, 3, 2):
        sib[j].wait_recv()
        tc[j].wait_recv()
        sc[j].wait_recv()
        R.t4[j - 1] = (total(j) + R.r2[j].astype(f32) + R.r3[j].astype(f32)).astype(bf)
        zc[j] = send(R.t4.at[j - 1], R.r4.at[j - 1], R.gzsem, j - 1, core, place.z(me, -j))
    sib[0].wait_recv()
    tc[0].wait_recv()
    sc[0].wait_recv()
    own = total(0) + R.r2[0].astype(f32) + R.r3[0].astype(f32)
    for j in (1, 3, 2):
        zc[j].wait_recv()
        own = own + R.r4[j - 1].astype(f32)
    R.half[core, 0] = own[:, :128]
    R.half[core, 1] = own[:, 128:]
    for group in (sib, tc, sc, zc):
        for c in group.values():
            c.wait_send()


def finish(R, place, chips):
    me, core = place.me, place.core
    loss = jnp.sum(R.loss[...], axis=1, keepdims=True)
    R.half[core, :, 201:208, :] = jnp.broadcast_to(loss, (2, 7, 128))
    both = send(R.half.at[core], R.half.at[core], R.hsem, 0, 1 - core, me)
    both.wait_recv()
    odd = lax.rem(me, 2)
    row = lax.broadcasted_iota(jnp.int32, (256, 128), 0)
    squares = jnp.zeros((1, 128), f32)
    for h in range(2):
        for lane in range(2):
            g = R.half[h, lane]
            keep = row < 201
            if h == 0:
                b_in = row >= 208 + (odd if lane == 0 else 0)
            else:
                b_in = jnp.logical_and(row >= 208, row < 208 + (33 if lane == 0 else 32 + odd))
            g = jnp.where(jnp.logical_or(keep, b_in), g, 0.0)
            squares = squares + rowsum(g * g)
    R.msg[0] = jnp.broadcast_to(jnp.sum(squares, axis=1, keepdims=True), (8, 128))
    R.msg[1] = R.half[0, 0, 200:208, :] + R.half[1, 0, 200:208, :]
    R.news[0] = R.msg[...]
    sent = []
    for d in range(1, chips):
        sent.append(send(R.msg, R.news.at[d], R.nsem, d - 1, core, lax.rem(me + d, chips)))
    for lane in range(2):
        for h in range(2):
            R.flat_a[pl.ds(402 * h + lane, 201, stride=2), :] = R.half[h, lane, 0:201, :]
            R.flat[pl.ds(8 + 96 * h + lane, 48 - 8 * h, stride=2), :] = R.half[h, lane, 208:256 - 8 * h, :]
    grad_b = jnp.where(odd == 1, R.flat[9:170, :], R.flat[8:169, :])
    for c in sent:
        c.wait_recv()
    total = R.news[0]
    for d in range(1, chips):
        total = total + R.news[d]
    norm = jnp.sqrt(total[0, 0:1, :])
    R.scalars[0:1, :] = total[1, 7:8, :]
    R.scalars[2:3, :] = norm
    clip = jnp.minimum(1.0, clip_level / (norm + 1e-06))
    for grad, p, m, v, outs in ((R.flat_a[0:804, :], R.pa, R.ma, R.va, R.outs_a), (grad_b, R.pb, R.mb, R.vb, R.outs_b)):
        g = grad * clip
        first = beta_one * m[...] + (1.0 - beta_one) * g
        second = beta_two * v[...] + (1.0 - beta_two) * g * g
        step = (first * (1.0 / (1.0 - beta_one ** STEP))) / (
            jnp.sqrt(second * (1.0 / (1.0 - beta_two ** STEP))) + adam_eps)
        old = p[...]
        new = old - learn_rate * (step + decay_rate * old)
        outs[0][...] = new
        outs[1][...] = first
        outs[2][...] = second
        outs[3][...] = new.astype(bf)
    for c in sent:
        c.wait_send()
    both.wait_send()


IN_ALL = ("img", "steps", "labels", "valid", "nidx", "table", "pa", "pb", "ma", "va", "mb", "vb")


def comm_scratch(chips):
    return dict(
        w=((chips, 2, PIECE, C), bf), flat=((184, 128), f32), piece=((2, PIECE, 128), f32),
        ga=((2, A_ROWS + 16, 128), f32), gb=((2, B_ROWS + 16, 128), f32), loss=((1, C), f32),
        r1=((chips, PIECE, C), bf), r2=((8, PIECE, C), bf), r3=((4, PIECE, C), bf), r4=((3, PIECE, C), bf),
        t2=((8, PIECE, C), bf), t3=((4, PIECE, C), bf), t4=((3, PIECE, C), bf),
        half=((2, 2, PIECE, 128), f32), flat_a=((808, 128), f32), msg=((2, 8, 128), f32), news=((chips, 2, 8, 128), f32))


def sem_counts(chips):
    return dict(zsem=3, ssem=4, tsem=8, csem=16, gcsem=16, gtsem=8, gssem=4, gzsem=3, hsem=1, nsem=chips - 1)


def whole_kernel(chips, *refs):
    R = Refs()
    refs = list(refs)
    for name in IN_ALL:
        setattr(R, name, refs.pop(0))
    R.outs_a = [refs.pop(0) for _ in range(4)]
    R.outs_b = [refs.pop(0) for _ in range(4)]
    R.scalars = refs.pop(0)
    for name in list(SCRATCH) + list(comm_scratch(chips)):
        setattr(R, name, refs.pop(0))
    for name in sem_counts(chips):
        setattr(R, name, (refs.pop(0), refs.pop(0)))
    place = Place(chips)
    barrier = greet(R, place, chips)
    own_piece(R, place)
    pl.semaphore_wait(barrier, chips)
    gather_weights(R, place)
    count = spread_rows(R, chips) * POS
    R.scalars[...] = jnp.zeros((8, 128), f32)
    R.scalars[1:2, :] = count
    first_setup(R)
    unpack_weights(R, R.ga, R.gb)
    time_forward(R)
    forward_a(R)
    forward_b(R)
    head(R, 2.0 / jnp.concatenate([count, count], axis=1))
    backward_b(R)
    backward_a(R)
    st(R.ga, A_ROWS - 1, jnp.zeros((1, C), f32))
    pack_gradients(R, chips)
    reduce_gradients(R, place)
    finish(R, place, chips)


def whole_step(chips, images, timesteps, labels, valid_slot, noise_idx, noise_table,
               params_a, params_b, first_a, second_a, first_b, second_b):
    smem = pl.BlockSpec(memory_space=pltpu.SMEM)
    vmem = pl.BlockSpec(memory_space=pltpu.VMEM)
    rows = lambda v: v.reshape(-1, 128)
    shapes = [jax.ShapeDtypeStruct((n, 128), d) for n in (804, 161) for d in (f32, f32, f32, bf)]
    scratch = [pltpu.VMEM(s, d) for s, d in SCRATCH.values()] + [pltpu.VMEM(s, d) for s, d in comm_scratch(chips).values()]
    for n in sem_counts(chips).values():
        scratch += [pltpu.SemaphoreType.DMA((n,)), pltpu.SemaphoreType.DMA((n,))]
    outs = pl.pallas_call(
        functools.partial(whole_kernel, chips),
        out_shape=shapes + [jax.ShapeDtypeStruct((8, 128), f32)],
        in_specs=[vmem, smem, smem, smem] + [vmem] * 8,
        out_specs=[vmem] * 9,
        scratch_shapes=scratch,
        compiler_params=pltpu.CompilerParams(
            collective_id=0, has_side_effects=True, vmem_limit_bytes=63 * 1024 * 1024),
    )(images, timesteps, labels, valid_slot, noise_idx, noise_table, rows(params_a), rows(params_b),
      rows(first_a), rows(second_a), rows(first_b), rows(second_b))
    flat = [v.reshape(-1) for v in outs[:8]]
    return (*flat, outs[8][0, 0], outs[8][1, 0], outs[8][2, 0])


def adam_update(master, grad_in, first_mom, second, clip_scale):
    clipped = grad_in * clip_scale
    first_new = beta_one * first_mom + (1.0 - beta_one) * clipped
    second_new = beta_two * second + (1.0 - beta_two) * clipped * clipped
    first_hat = first_new / (1.0 - beta_one**STEP)
    second_hat = second_new / (1.0 - beta_two**STEP)
    master_new = master - learn_rate * (
        first_hat / (jnp.sqrt(second_hat) + adam_eps) + decay_rate * master
    )
    return (master_new, first_new, second_new)


def plain_step(images, timesteps, labels, valid_slot, noise_idx, noise_table,
               params_a, params_b, first_a, second_a, first_b, second_b):
    gather = lambda v: lax.all_gather(v.astype(bf), "fsdp", axis=0, tiled=True).reshape(-1, C)
    count = lax.psum(jnp.sum(valid_slot).astype(f32) * POS, ("dp", "fsdp"))
    ga, gb, loss = compute(images, timesteps, labels, valid_slot, (2.0 / count).reshape(1), noise_idx, noise_table,
                           gather(params_a), gather(params_b))
    flat = lambda g: jnp.concatenate([g[0], g[1]], axis=1).reshape(-1)
    shard = lambda g: lax.psum_scatter(flat(g), "fsdp", scatter_dimension=0, tiled=True)
    part_a, part_b, loss = lax.psum((shard(ga), shard(gb), jnp.sum(loss)), "dp")
    loss, squares = lax.psum((loss, jnp.sum(part_a * part_a) + jnp.sum(part_b * part_b)), "fsdp")
    norm = jnp.sqrt(squares)
    clip = jnp.minimum(1.0, clip_level / (norm + 1e-06))
    new_a = adam_update(params_a, part_a, first_a, second_a, clip)
    new_b = adam_update(params_b, part_b, first_b, second_b, clip)
    return (*new_a, new_a[0].astype(bf), *new_b, new_b[0].astype(bf), loss, count, norm)


def solution(mesh):
    chips = mesh.shape["fsdp"]
    if chips == 16 and mesh.shape["dp"] == 2:
        step = functools.partial(whole_step, chips)
    else:
        step = plain_step
    both = P(("dp", "fsdp"))
    return jax.shard_map(
        step, mesh=mesh,
        in_specs=(both, both, both, both, both, P()) + (P("fsdp"),) * 6,
        out_specs=(P("fsdp"),) * 8 + (P(),) * 3,
        check_vma=False)
```

```python
import functools
import math
import jax
import jax.numpy as jnp
import numpy as np
from jax import lax
from jax.experimental import pallas as pl
from jax.experimental.pallas import tpu as pltpu
from jax.sharding import PartitionSpec as P

C = 256
SIDE = 16
POS = 256
TE = 512
SIN = 128
NCLS = 10
NT = 256
NIMG = 8
bf = jnp.bfloat16
f32 = jnp.float32
eps_norm = 1e-05
CH = 64
TY = 2
U = dict(conv=8, cback=8, triple=8, attn=8, head=8, aback=8, dx3=8, chunk=8, setup=8)

A_N1, A_K1, A_B1, A_W1, A_TB1, A_W2, A_TB2, A_CT, A_PT, A_PB, A_N2, A_K2, A_B2 = (
    0, 2, 2306, 2307, 2563, 2565, 3589, 3591, 3611, 4123, 4124, 4126, 6430)
A_ROWS = 6432
B_N3, B_W, B_QV, B_WO, B_BO, B_N4, B_WH, B_BH = (0, 2, 770, 772, 1028, 1029, 1031, 1287)
B_ROWS = 1288


def dot(a, b):
    return jnp.dot(a, b, preferred_element_type=f32)


def dot_nt(a, b):
    return lax.dot_general(a, b, (((1,), (1,)), ((), ())), preferred_element_type=f32)


def dot_tn(a, b):
    return lax.dot_general(a, b, (((0,), (0,)), ((), ())), preferred_element_type=f32)


def split3(x):
    hi = x.astype(bf).astype(f32)
    rest = x - hi
    mid = rest.astype(bf).astype(f32)
    return hi, mid, rest - mid


def wide_dot(x, w, nt=False):
    n = x.shape[0]
    stacked = jnp.concatenate(split3(x), axis=0).astype(bf)
    out = dot_nt(stacked, w) if nt else dot(stacked, w)
    return out[:n] + out[n:2 * n] + out[2 * n:]


def outer_sum(a, b):
    a0, a1, _ = split3(a)
    b0, b1, _ = split3(b)
    return dot_tn(jnp.concatenate([a0, a0, a1], axis=0).astype(bf),
                  jnp.concatenate([b0, b1, b0], axis=0).astype(bf))


def sigm(v):
    return 0.5 * jnp.tanh(0.5 * v) + 0.5


def rowsum(x):
    return jnp.sum(x, axis=0, keepdims=True)


def put_shifts(buf, i, r0, x):
    n = x.shape[0]
    col = lax.broadcasted_iota(jnp.int32, x.shape, 0) & 15
    left = jnp.where(col == 0, 0.0, pltpu.roll(x, 1, 0))
    right = jnp.where(col == 15, 0.0, pltpu.roll(x, n - 1, 0))
    y = n // 16
    for s, v in enumerate((left, x, right)):
        buf[pl.ds(1 + r0 // 16, y), i, :, 256 * s:256 * s + 256] = v.astype(bf).reshape(y, 16, C)


def conv_mm(buf, kmat, y):
    ty = TY
    parts = [buf[pl.ds(y + r, ty)].reshape(ty * 128, 3 * C) for r in range(3)]
    return dot(jnp.concatenate(parts, axis=1), kmat[...])


class Refs:
    pass


def ld(f, row, n, stride=1):
    at = pl.ds(row, n, stride=stride) if stride > 1 else pl.ds(row, n)
    return jnp.concatenate([f[0, at, :], f[1, at, :]], axis=1)


def st(f, row, value, stride=1):
    n = value.shape[0]
    at = pl.ds(row, n, stride=stride) if stride > 1 else pl.ds(row, n)
    f[0, at, :] = value[:, :128]
    f[1, at, :] = value[:, 128:]


def unpack_weights(R, fa, fb):
    for kmat, kt, base in ((R.k1, R.k1t, A_K1), (R.k2, R.k2t, A_K2)):
        for t in range(9):
            w = ld(fa, base + 256 * t, 256)
            kmat[256 * t:256 * t + 256, :] = w.astype(bf)
            kt[256 * (8 - t):256 * (8 - t) + 256, :] = w.T.astype(bf)
    for h in range(2):
        R.tw1[:, 256 * h:256 * h + 256] = ld(fa, A_W1 + h, SIN, 2).astype(bf)
        R.tw2[:, 256 * h:256 * h + 256] = ld(fa, A_W2 + h, TE, 2).astype(bf)
    R.pt[...] = ld(fa, A_PT, TE).astype(bf)
    for h in range(3):
        w = ld(fb, B_W + h, C, 3)
        R.wt[:, 256 * h:256 * h + 256] = w.astype(bf)
        R.wtt[256 * h:256 * h + 256, :] = w.T.astype(bf)
    w = ld(fb, B_WO, C)
    R.wo[...] = w.astype(bf)
    R.wot[...] = w.T.astype(bf)
    w = ld(fb, B_WH, C)
    R.wh[...] = w.astype(bf)
    R.wht[...] = w.T.astype(bf)
    for k, row in enumerate((A_N1, A_N1 + 1, A_B1, A_TB1, A_TB1 + 1, A_TB2, A_TB2 + 1, A_PB, A_N2, A_N2 + 1, A_B2)):
        R.vec[k:k + 1, :] = ld(fa, row, 1)
    for k, row in enumerate((B_N3, B_N3 + 1, B_QV, B_QV + 1, B_BO, B_N4, B_N4 + 1, B_BH)):
        R.vec[11 + k:12 + k, :] = ld(fb, row, 1)
    R.ct[0:20, :] = ld(fa, A_CT, 20)


(V_G1, V_C1, V_B1, V_TB1, V_TB1B, V_TB2, V_TB2B, V_PB, V_G2, V_C2, V_B2,
 V_G3, V_C3, V_QB, V_VB, V_BO, V_G4, V_C4, V_BH) = range(19)


def vec(R, k):
    return R.vec[k:k + 1, :]


def group_mean(R, s):
    return wide_dot(s, R.gm[...])


def stats(R, k, load):
    for i in range(NIMG):
        R.tmp[i:i + 1, :] = rowsum(load(i))
    mean = group_mean(R, R.tmp[0:8, :])
    R.mean[k] = mean
    for i in range(NIMG):
        x = load(i) - mean[i:i + 1, :]
        R.tmp[i:i + 1, :] = rowsum(x * x)
    R.inv[k] = lax.rsqrt(group_mean(R, R.tmp[0:8, :]) + eps_norm)


def norm_sums(R, k, gain):
    s1, s2 = R.s1[...], R.s2[...]
    m = group_mean(R, jnp.concatenate([s1 * gain, s2 * gain], axis=0))
    R.m1[...] = m[:8] * R.inv[k]
    R.m2[...] = m[8:] * R.inv[k]
    return rowsum(s2), rowsum(s1)


def first_setup(R):
    row = lax.broadcasted_iota(jnp.int32, (C, C), 0) >> 3
    col = lax.broadcasted_iota(jnp.int32, (C, C), 1) >> 3
    R.gm[...] = jnp.where(row == col, 1.0 / 2048.0, 0.0).astype(bf)
    zero = jnp.zeros((1, NIMG, 16, 3 * C), bf)
    for buf in (R.buf1, R.buf2, R.dbuf):
        buf[0:1] = zero
        buf[17:18] = zero
    hi, mid, lo = split3(R.table[...])
    R.tab3[...] = jnp.concatenate([hi, mid, lo], axis=1).astype(bf)

    @pl.loop(0, NIMG, unroll=U["setup"])
    def _(i):
        rows = lax.broadcasted_iota(jnp.int32, (NT, POS), 0)
        hot = jnp.where(rows == R.nidx[pl.ds(i, 1), :], 1.0, 0.0)
        out = dot(hot.T.astype(bf), R.tab3[...])
        R.target[i] = out[:, :C] + out[:, C:2 * C] + out[:, 2 * C:]
    stats(R, 0, lambda i: R.img[i].astype(f32))


def column_of(smem, shape):
    row = lax.broadcasted_iota(jnp.int32, shape, 0)
    out = jnp.zeros(shape, jnp.int32)
    for i in range(NIMG):
        out = jnp.where(row == i, smem[i], out)
    return out


def time_forward(R):
    lane = lax.broadcasted_iota(jnp.int32, (NIMG, SIN), 1)
    factor = math.log(10000.0) / (SIN // 2 - 1)
    freq = jnp.exp((lane & 63).astype(f32) * -factor)
    angle = column_of(R.steps, (NIMG, SIN)).astype(f32) * freq
    e = jnp.where(lane < 64, jnp.sin(angle), jnp.cos(angle))
    R.emb[...] = e
    u = wide_dot(e, R.tw1[...]) + jnp.concatenate([vec(R, V_TB1), vec(R, V_TB1B)], axis=1)
    R.pre[...] = u
    lab = column_of(R.labels, (NIMG, TE))
    te = wide_dot(u * sigm(u), R.tw2[...]) + jnp.concatenate([vec(R, V_TB2), vec(R, V_TB2B)], axis=1)
    for j in range(NCLS):
        row = jnp.concatenate([R.ct[2 * j:2 * j + 1, :], R.ct[2 * j + 1:2 * j + 2, :]], axis=1)
        te = te + jnp.where(lab == j, row, 0.0)
    R.te[...] = te
    add = wide_dot(te * sigm(te), R.pt[...]) + vec(R, V_PB) + vec(R, V_B1)
    for i in range(NIMG):
        R.addb[i] = jnp.broadcast_to(add[i:i + 1, :], (16, C))


def each_chunk(fn):
    @pl.loop(0, NIMG, unroll=U["chunk"])
    def _(i):
        for c in range(POS // CH):
            fn(i, c * CH)


def normed(R, k, i, x):
    return (x - R.mean[k, pl.ds(i, 1), :]) * R.inv[k, pl.ds(i, 1), :]


def step_x1(R):
    def one(i, r0):
        x = normed(R, 0, i, R.img[i, r0:r0 + CH, :].astype(f32))
        a = x * vec(R, V_G1) + vec(R, V_C1)
        put_shifts(R.buf1, i, r0, a * sigm(a))
    each_chunk(one)


def step_conv1(R):
    @pl.loop(0, SIDE // TY, unroll=U["conv"])
    def _(t):
        acc = conv_mm(R.buf1, R.k1, t * TY).reshape(TY, NIMG, 16, C)
        for yy in range(TY):
            R.c1[:, pl.ds(pl.multiple_of((t * TY + yy) * 16, 16), 16), :] = acc[yy] + R.addb[...]


def step_stats1(R):
    stats(R, 1, lambda i: R.c1[i])


def step_x2(R):
    def two(i, r0):
        x = normed(R, 1, i, R.c1[i, r0:r0 + CH, :])
        a = x * vec(R, V_G2) + vec(R, V_C2)
        put_shifts(R.buf2, i, r0, a * sigm(a))
    each_chunk(two)


def step_conv2(R):
    @pl.loop(0, SIDE // TY, unroll=U["conv"])
    def _(t):
        acc = conv_mm(R.buf2, R.k2, t * TY).reshape(TY, NIMG, 16, C)
        for yy in range(TY):
            at = pl.ds(pl.multiple_of((t * TY + yy) * 16, 16), 16)
            R.h1[:, at, :] = acc[yy] + R.img[:, at, :].astype(f32) + vec(R, V_B2)


def step_stats2(R):
    stats(R, 2, lambda i: R.h1[i])


def step_triple(R):
    bias = jnp.concatenate([vec(R, V_QB), jnp.zeros((1, C), f32), vec(R, V_VB)], axis=1)

    @pl.loop(0, NIMG, unroll=U["triple"])
    def _(i):
        x = (normed(R, 2, i, R.h1[i]) * vec(R, V_G3) + vec(R, V_C3)).astype(bf)
        R.x3t[:, pl.ds(pl.multiple_of(i * POS, POS), POS)] = x.T
        R.tri[i] = (dot(x, R.wt[...]) + bias).astype(bf)


def step_attn(R):
    @pl.loop(0, NIMG, unroll=U["attn"])
    def _(i):
        k = R.tri[i, :, C:2 * C]
        v = R.tri[i, :, 2 * C:]
        for h in range(2):
            at = slice(128 * h, 128 * h + 128)
            s = dot_nt(R.tri[i, at, 0:C], k) * C ** (-0.5)
            e = jnp.exp(s - jnp.max(s, axis=1, keepdims=True))
            p = e * (1.0 / jnp.sum(e, axis=1, keepdims=True))
            R.p[i, at, :] = p
            o = dot(p.astype(bf), v).astype(bf)
            R.o[i, at, :] = o
            R.h2[i, at, :] = R.h1[i, at, :] + dot(o, R.wo[...]) + vec(R, V_BO)


def step_stats3(R):
    stats(R, 3, lambda i: R.h2[i])


def step_head(R):
    scale = R.scale_row[...]
    R.loss[...] = jnp.zeros_like(R.loss)
    R.sh[...] = jnp.zeros_like(R.sh)

    @pl.loop(0, NIMG, unroll=U["head"])
    def _(i):
        valid = R.valid[i].astype(f32)
        s1 = jnp.zeros((1, C), f32)
        s2 = jnp.zeros((1, C), f32)
        for h in range(2):
            at = slice(128 * h, 128 * h + 128)
            x = normed(R, 3, i, R.h2[i, at, :])
            a = x * vec(R, V_G4) + vec(R, V_C4)
            sg = sigm(a)
            x4 = (a * sg).astype(bf)
            R.xt[:, pl.ds(pl.multiple_of(i * POS + 128 * h, 128), 128)] = x4.T
            differ = dot(x4, R.wh[...]) + vec(R, V_BH) - R.target[i, at, :]
            dv = valid * differ
            R.loss[...] += rowsum(dv * differ)
            dp = dv * scale
            R.sh[...] += rowsum(dp)
            low = dp.astype(bf)
            R.low[i, at, :] = low
            da = dot(low, R.wht[...]) * (sg * (1.0 + a * (1.0 - sg)))
            R.da[i, at, :] = da
            s1 += rowsum(da)
            s2 += rowsum(da * x)
        R.s1[pl.ds(i, 1), :] = s1
        R.s2[pl.ds(i, 1), :] = s2


def step_head_grads(R):
    st(R.gb, B_BH, R.sh[...])
    st(R.gb, B_WH, dot(R.xt[...], R.low[...].reshape(NIMG * POS, C)))
    dg, db = norm_sums(R, 3, vec(R, V_G4))
    st(R.gb, B_N4, dg)
    st(R.gb, B_N4 + 1, db)


def step_attn_back(R):
    R.sh[...] = jnp.zeros_like(R.sh)
    R.sq[...] = jnp.zeros_like(R.sq)

    @pl.loop(0, NIMG, unroll=U["aback"])
    def _(i):
        x = normed(R, 3, i, R.h2[i])
        d = (R.inv[3, pl.ds(i, 1), :] * vec(R, V_G4)) * R.da[i] - R.m1[pl.ds(i, 1), :] - x * R.m2[pl.ds(i, 1), :]
        R.dh[i] = d
        R.sh[...] += rowsum(d)
        low = d.astype(bf)
        R.low[i] = low
        R.xt[:, pl.ds(pl.multiple_of(i * POS, POS), POS)] = R.o[i].T
        dm = dot(low, R.wot[...]).astype(bf)
        p = R.p[i]
        q = R.tri[i, :, 0:C]
        k = R.tri[i, :, C:2 * C]
        v = R.tri[i, :, 2 * C:]
        dv = dot_tn(p.astype(bf), dm).astype(bf)
        dpr = dot_nt(dm, v)
        ds = (p * (dpr - jnp.sum(dpr * p, axis=1, keepdims=True))).astype(bf)
        dq = (dot(ds, k) * C ** (-0.5)).astype(bf)
        dk = (dot_tn(ds, q) * C ** (-0.5)).astype(bf)
        R.tri[i, :, 0:C] = dq
        R.tri[i, :, C:2 * C] = dk
        R.tri[i, :, 2 * C:] = dv
        R.sq[:, 0:C] += rowsum(dq.astype(f32))
        R.sq[:, C:2 * C] += rowsum(dv.astype(f32))
    st(R.gb, B_BO, R.sh[...])
    st(R.gb, B_QV, R.sq[:, 0:C])
    st(R.gb, B_QV + 1, R.sq[:, C:2 * C])


def step_out_grads(R):
    st(R.gb, B_WO, dot(R.xt[...], R.low[...].reshape(NIMG * POS, C)))


def step_dx3(R):
    @pl.loop(0, NIMG, unroll=U["dx3"])
    def _(i):
        da = dot(R.tri[i], R.wtt[...])
        R.da[i] = da
        R.s1[pl.ds(i, 1), :] = rowsum(da)
        R.s2[pl.ds(i, 1), :] = rowsum(da * normed(R, 2, i, R.h1[i]))


def step_triple_grads(R):
    for h in range(3):
        st(R.gb, B_W + h, dot(
            R.x3t[...], R.tri[:, :, 256 * h:256 * h + 256].reshape(NIMG * POS, C)), 3)
    dg, db = norm_sums(R, 2, vec(R, V_G3))
    st(R.gb, B_N3, dg)
    st(R.gb, B_N3 + 1, db)


def kernel_grad(R, buf, row):
    @pl.loop(0, SIDE // 2, unroll=8)
    def _(t):
        x = buf[pl.ds(1 + 2 * t, 2), :, :, C:2 * C].reshape(256, C)
        R.xt[:, pl.ds(pl.multiple_of(t * 256, 256), 256)] = x.T
    for r in range(3):
        for s in range(3):
            d = R.dbuf[2 - r:18 - r, :, :, 256 * (2 - s):256 * (3 - s)].reshape(NIMG * POS, C)
            at = row + (3 * r + s) * 256
            st(R.ga, at, dot(R.xt[...], d))


def conv_back(R, kt):
    @pl.loop(0, SIDE // TY, unroll=U["cback"])
    def _(t):
        acc = conv_mm(R.dbuf, kt, t * TY).reshape(TY, NIMG, 16, C)
        for yy in range(TY):
            R.da[:, pl.ds(pl.multiple_of((t * TY + yy) * 16, 16), 16), :] = acc[yy]


def swish_back(R, k, load, vg, vc, keep):
    R.s1[...] = jnp.zeros_like(R.s1)
    R.s2[...] = jnp.zeros_like(R.s2)

    def one(i, r0):
        x = normed(R, k, i, load(i, r0))
        a = x * vec(R, vg) + vec(R, vc)
        sg = sigm(a)
        da = R.da[i, r0:r0 + CH, :] * (sg * (1.0 + a * (1.0 - sg)))
        if keep:
            R.da[i, r0:r0 + CH, :] = da
        R.s1[pl.ds(i, 1), :] += rowsum(da)
        R.s2[pl.ds(i, 1), :] += rowsum(da * x)
    each_chunk(one)


def step_dh1(R):
    R.sh[...] = jnp.zeros_like(R.sh)

    def one(i, r0):
        at = slice(r0, r0 + CH)
        x = normed(R, 2, i, R.h1[i, at, :])
        d = (R.dh[i, at, :] + (R.inv[2, pl.ds(i, 1), :] * vec(R, V_G3)) * R.da[i, at, :]
             - R.m1[pl.ds(i, 1), :] - x * R.m2[pl.ds(i, 1), :])
        R.sh[...] += rowsum(d)
        put_shifts(R.dbuf, i, r0, d)
    each_chunk(one)
    st(R.ga, A_B2, R.sh[...])


def step_dk2(R):
    kernel_grad(R, R.buf2, A_K2)


def step_dx2(R):
    conv_back(R, R.k2t)


def step_da2(R):
    swish_back(R, 1, lambda i, r0: R.c1[i, r0:r0 + CH, :], V_G2, V_C2, True)
    dg, db = norm_sums(R, 1, vec(R, V_G2))
    st(R.ga, A_N2, dg)
    st(R.ga, A_N2 + 1, db)


def step_dc1(R):
    R.tmp[...] = jnp.zeros_like(R.tmp)

    def two(i, r0):
        at = slice(r0, r0 + CH)
        x = normed(R, 1, i, R.c1[i, at, :])
        d = ((R.inv[1, pl.ds(i, 1), :] * vec(R, V_G2)) * R.da[i, at, :]
             - R.m1[pl.ds(i, 1), :] - x * R.m2[pl.ds(i, 1), :])
        R.tmp[pl.ds(i, 1), :] += rowsum(d)
        put_shifts(R.dbuf, i, r0, d)
    each_chunk(two)


def step_dk1(R):
    kernel_grad(R, R.buf1, A_K1)


def step_dx1(R):
    conv_back(R, R.k1t)


def step_da1(R):
    swish_back(R, 0, lambda i, r0: R.img[i, r0:r0 + CH, :].astype(f32), V_G1, V_C1, False)
    st(R.ga, A_N1, rowsum(R.s2[...]))
    st(R.ga, A_N1 + 1, rowsum(R.s1[...]))


def swish_slope(v):
    s = sigm(v)
    return s * (1.0 + v * (1.0 - s))


def time_backward(R):
    d_add = R.tmp[0:8, :]
    total = rowsum(d_add)
    st(R.ga, A_B1, total)
    st(R.ga, A_PB, total)
    te = R.te[...]
    st(R.ga, A_PT, outer_sum(te * sigm(te), d_add))
    d_te = wide_dot(d_add, R.pt[...], nt=True) * swish_slope(te)
    lab = column_of(R.labels, (NIMG, TE))
    for j in range(NCLS):
        row = rowsum(jnp.where(lab == j, d_te, 0.0))
        for h in range(2):
            st(R.ga, A_CT + 2 * j + h, row[:, 256 * h:256 * h + 256])
    row = rowsum(d_te)
    u = R.pre[...]
    dw2 = outer_sum(u * sigm(u), d_te)
    d_u = wide_dot(d_te, R.tw2[...], nt=True) * swish_slope(u)
    row1 = rowsum(d_u)
    dw1 = outer_sum(R.emb[...], d_u)
    for h in range(2):
        st(R.ga, A_TB2 + h, row[:, 256 * h:256 * h + 256])
        st(R.ga, A_TB1 + h, row1[:, 256 * h:256 * h + 256])
        st(R.ga, A_W2 + h, dw2[:, 256 * h:256 * h + 256], 2)
        st(R.ga, A_W1 + h, dw1[:, 256 * h:256 * h + 256], 2)


STEPS = [step_x1, step_conv1, step_stats1, step_x2, step_conv2, step_stats2, step_triple, step_attn, step_stats3,
         step_head, step_head_grads, step_attn_back, step_out_grads, step_dx3, step_triple_grads, step_dh1, step_dk2,
         step_dx2, step_da2, step_dc1, time_backward, step_dx1, step_da1, step_dk1]


SCRATCH = dict(
    k1=((2304, C), bf), k1t=((2304, C), bf), k2=((2304, C), bf), k2t=((2304, C), bf),
    tw1=((SIN, TE), bf), tw2=((TE, TE), bf), pt=((TE, C), bf),
    wt=((C, 3 * C), bf), wtt=((3 * C, C), bf), wo=((C, C), bf), wot=((C, C), bf), wh=((C, C), bf), wht=((C, C), bf),
    vec=((24, C), f32), ct=((24, C), f32),
    gm=((C, C), bf), tab3=((NT, 3 * C), bf), target=((NIMG, POS, C), f32),
    tmp=((8, C), f32), mean=((4, 8, C), f32), inv=((4, 8, C), f32),
    s1=((8, C), f32), s2=((8, C), f32), m1=((8, C), f32), m2=((8, C), f32),
    sh=((1, C), f32), scale_row=((1, C), f32), sq=((1, 2 * C), f32),
    emb=((8, SIN), f32), pre=((8, TE), f32), te=((8, TE), f32), addb=((8, 16, C), f32),
    buf1=((18, 8, 16, 3 * C), bf), buf2=((18, 8, 16, 3 * C), bf), dbuf=((18, 8, 16, 3 * C), bf),
    c1=((8, POS, C), f32), h1=((8, POS, C), f32), h2=((8, POS, C), f32), da=((8, POS, C), f32), dh=((8, POS, C), f32),
    p=((8, POS, POS), f32), o=((8, POS, C), bf), low=((8, POS, C), bf),
    tri=((8, POS, 3 * C), bf),
    x3t=((C, 8 * POS), bf), xt=((C, 8 * POS), bf),
)


def main_kernel(names_in, *refs):
    R = Refs()
    n_in = len(names_in)
    for name, r in zip(names_in, refs):
        setattr(R, name, r)
    R.ga, R.gb, R.loss = refs[n_in:n_in + 3]
    for name, r in zip(list(SCRATCH), refs[n_in + 3:]):
        setattr(R, name, r)
    fa, fb = R.ga, R.gb
    for c in range(0, A_ROWS, 402):
        st(fa, c, R.wa[c:c + 402, :].astype(f32))
    st(fb, 0, R.wb[...].astype(f32))
    R.scale_row[...] = jnp.full((1, C), R.scale[0])
    first_setup(R)
    unpack_weights(R, fa, fb)
    time_forward(R)
    for step in STEPS:
        step(R)


def compute(img, steps, labels, valid, scale, nidx, table, wa, wb):
    smem = pl.BlockSpec(memory_space=pltpu.SMEM)
    vmem = pl.BlockSpec(memory_space=pltpu.VMEM)
    names = ("img", "steps", "labels", "valid", "scale", "nidx", "table", "wa", "wb")
    return pl.pallas_call(
        functools.partial(main_kernel, names),
        out_shape=(jax.ShapeDtypeStruct((2, A_ROWS, 128), f32), jax.ShapeDtypeStruct((2, B_ROWS, 128), f32),
                   jax.ShapeDtypeStruct((1, C), f32)),
        in_specs=[vmem, smem, smem, smem, smem, vmem, vmem, vmem, vmem],
        out_specs=(vmem, vmem, vmem),
        scratch_shapes=[pltpu.VMEM(s, d) for s, d in SCRATCH.values()],
        compiler_params=pltpu.CompilerParams(vmem_limit_bytes=63 * 1024 * 1024),
    )(img, steps, labels, valid, scale, nidx, table, wa, wb)


beta_one = 0.5
beta_two = 0.5
learn_rate = 0.1
decay_rate = 0.01
adam_eps = 1e-08
clip_level = 0.01
STEP = 5
PA = A_ROWS * C
PB = B_ROWS * C
MESH = pl.DeviceIdType.MESH
ORDER = (0, 1, 3, 2)
HALF_A, HALF_B, PIECE = 201, 48, 256
B_AT = 208


class Place:
    def __init__(self, chips):
        self.me = lax.axis_index("fsdp")
        self.core = lax.axis_index("dp")
        self.depth = chips // 4

    def z(self, k, d):
        return lax.rem(lax.div(k, 4) + d + self.depth, self.depth) * 4 + lax.rem(k, 4)

    def flip_x(self, k):
        return k + 1 - 2 * lax.rem(k, 2)

    def flip_y(self, k):
        return k + 2 - 4 * lax.rem(lax.div(k, 2), 2)

    def s(self, k):
        return self.core * self.flip_x(k) + (1 - self.core) * self.flip_y(k)

    def t(self, k):
        return self.core * self.flip_y(k) + (1 - self.core) * self.flip_x(k)

    def pieces(self):
        line = [self.z(self.me, -j) for j in range(4)]
        near = line + [self.s(k) for k in line]
        return near + [self.t(k) for k in near]


def send(src, dst, sems, at, core, chip):
    copy = pltpu.make_async_remote_copy(
        src_ref=src, dst_ref=dst, send_sem=sems[0].at[at], recv_sem=sems[1].at[at],
        device_id=(core, chip), device_id_type=MESH)
    copy.start()
    return copy


def greet(R, place, chips):
    barrier = pltpu.get_barrier_semaphore()
    for d in range(1, chips):
        pl.semaphore_signal(barrier, inc=1, device_id=(place.core, lax.rem(place.me + d, chips)), device_id_type=MESH)
    pl.semaphore_signal(barrier, inc=1, device_id=(1 - place.core, place.me), device_id_type=MESH)
    return barrier


def own_piece(R, place):
    count = R.valid[0]
    for i in range(1, NIMG):
        count = count + R.valid[i]
    count = count.astype(f32)
    odd = lax.rem(place.me, 2) == 1
    R.flat[0:8, :] = jnp.zeros((8, 128), f32)
    R.flat[168:184, :] = jnp.zeros((16, 128), f32)
    R.flat[8:169, :] = R.pb[...]
    for h in range(2):
        for lane in range(2):
            R.piece[lane, 0:201, :] = R.pa[pl.ds(402 * h + lane, 201, stride=2), :]
            even_rows = R.flat[pl.ds(8 + lane + 96 * h, 48 - 8 * h, stride=2), :]
            odd_rows = R.flat[pl.ds(7 + lane + 96 * h, 48 - 8 * h, stride=2), :]
            R.piece[lane, 208:256 - 8 * h, :] = jnp.where(odd, odd_rows, even_rows)
        R.piece[:, 201:208, :] = jnp.full((2, 7, 128), count)

        @pl.when(place.core == h)
        def _():
            R.w[place.me, h] = jnp.concatenate([R.piece[0], R.piece[1]], axis=1).astype(bf)


def gather_weights(R, place, meanwhile):
    me, core = place.me, place.core
    got = place.pieces()
    put = lambda k: R.w.at[k, core]
    over_s, over_t = place.s(me), place.t(me)
    zc = {d: send(put(me), put(me), R.zsem, d - 1, core, place.z(me, d)) for d in (1, 3, 2)}
    sc, tc, sib = {}, {}, {}
    for j in ORDER:
        if j == 1:
            meanwhile()
        if j:
            zc[j].wait_recv()
        sc[j] = send(put(got[j]), put(got[j]), R.ssem, j, core, over_s)
        tc[j] = send(put(got[j]), put(got[j]), R.tsem, j, core, over_t)
        sib[j] = send(put(got[j]), put(got[j]), R.csem, j, 1 - core, me)
    for j in ORDER:
        sc[j].wait_recv()
        q = 4 + j
        tc[q] = send(put(got[q]), put(got[q]), R.tsem, q, core, over_t)
        sib[q] = send(put(got[q]), put(got[q]), R.csem, q, 1 - core, me)
    for half in (0, 4):
        for j in ORDER:
            q = half + j
            tc[q].wait_recv()
            sib[8 + q] = send(put(got[8 + q]), put(got[8 + q]), R.csem, 8 + q, 1 - core, me)
    for c in sib.values():
        c.wait_recv()
    for group in (zc, sc, tc, sib):
        for c in group.values():
            c.wait_send()


def spread_rows(R, chips):
    count = jnp.zeros((1, 128), f32)
    for k in range(chips):
        base = (161 * k) // 2
        odd = k % 2
        for h in range(2):
            a = R.w[k, h, 0:208, :].astype(f32)
            row = 402 * k + 201 * h
            R.ga[0, row:row + 208, :] = a[:, :128]
            R.ga[1, row:row + 208, :] = a[:, 128:]
            count = count + a[201:202, :128]
            b = R.w[k, h, 208:256, :].astype(f32)
            if h == 0:
                R.gb[0, base + odd:base + 48, :] = b[odd:, :128]
                R.gb[1, base:base + 48, :] = b[:, 128:]
            else:
                R.gb[0, base + 48:base + 81, :] = b[:33, :128]
                R.gb[1, base + 48:base + 80 + odd, :] = b[:32 + odd, 128:]
    return count


def pack_gradients(R, chips):
    for k in range(chips):
        base = (161 * k) // 2
        for h in range(2):
            R.w[k, h, 0:208, :] = ld(R.ga, 402 * k + 201 * h, 208).astype(bf)
            R.w[k, h, 208:256, :] = ld(R.gb, base + 48 * h, 48).astype(bf)


def reduce_gradients(R, place):
    me, core = place.me, place.core
    got = place.pieces()
    over_s, over_t = place.s(me), place.t(me)
    order = [12 + j for j in ORDER] + [8 + j for j in ORDER]
    sib = {}
    for q in order[:4] + [4 + j for j in ORDER] + order[4:] + [1, 3, 2, 0]:
        there = q + 4 if 4 <= q < 8 else q - 4 if 8 <= q < 12 else q
        copy = pltpu.make_async_remote_copy(
            src_ref=R.w.at[got[q], 1 - core], dst_ref=R.r1.at[there], send_sem=R.gcsem[0].at[q],
            recv_sem=R.gcsem[1].at[there], device_id=(1 - core, me), device_id_type=MESH)
        copy.start()
        sib[there] = copy

    def total(q):
        return R.w[got[q], core].astype(f32) + R.r1[q].astype(f32)
    tc, sc, zc = {}, {}, {}
    for q in order:
        sib[q].wait_recv()
        R.t2[q - 8] = total(q).astype(bf)
        tc[q - 8] = send(R.t2.at[q - 8], R.r2.at[q - 8], R.gtsem, q - 8, core, over_t)
    for j in ORDER:
        q = 4 + j
        sib[q].wait_recv()
        tc[q].wait_recv()
        R.t3[j] = (total(q) + R.r2[q].astype(f32)).astype(bf)
        sc[j] = send(R.t3.at[j], R.r3.at[j], R.gssem, j, core, over_s)
    for j in (1, 3, 2):
        sib[j].wait_recv()
        tc[j].wait_recv()
        sc[j].wait_recv()
        R.t4[j - 1] = (total(j) + R.r2[j].astype(f32) + R.r3[j].astype(f32)).astype(bf)
        zc[j] = send(R.t4.at[j - 1], R.r4.at[j - 1], R.gzsem, j - 1, core, place.z(me, -j))
    sib[0].wait_recv()
    tc[0].wait_recv()
    sc[0].wait_recv()
    own = total(0) + R.r2[0].astype(f32) + R.r3[0].astype(f32)
    for j in (1, 3, 2):
        zc[j].wait_recv()
        own = own + R.r4[j - 1].astype(f32)
    R.half[core, 0] = own[:, :128]
    R.half[core, 1] = own[:, 128:]
    for group in (sib, tc, sc, zc):
        for c in group.values():
            c.wait_send()


def finish(R, place, chips):
    me, core = place.me, place.core
    loss = jnp.sum(R.loss[...], axis=1, keepdims=True)
    R.half[core, :, 201:208, :] = jnp.broadcast_to(loss, (2, 7, 128))
    both = send(R.half.at[core], R.half.at[core], R.hsem, 0, 1 - core, me)
    both.wait_recv()
    odd = lax.rem(me, 2)
    row = lax.broadcasted_iota(jnp.int32, (256, 128), 0)
    squares = jnp.zeros((1, 128), f32)
    for h in range(2):
        for lane in range(2):
            g = R.half[h, lane]
            keep = row < 201
            if h == 0:
                b_in = row >= 208 + (odd if lane == 0 else 0)
            else:
                b_in = jnp.logical_and(row >= 208, row < 208 + (33 if lane == 0 else 32 + odd))
            g = jnp.where(jnp.logical_or(keep, b_in), g, 0.0)
            squares = squares + rowsum(g * g)
    R.msg[0] = jnp.broadcast_to(jnp.sum(squares, axis=1, keepdims=True), (8, 128))
    R.msg[1] = R.half[0, 0, 200:208, :] + R.half[1, 0, 200:208, :]
    R.news[0] = R.msg[...]
    sent = []
    for d in range(1, chips):
        sent.append(send(R.msg, R.news.at[d], R.nsem, d - 1, core, lax.rem(me + d, chips)))
    for lane in range(2):
        for h in range(2):
            R.out_a[pl.ds(402 * h + lane, 201, stride=2), :] = R.half[h, lane, 0:201, :]
            R.flat[pl.ds(8 + 96 * h + lane, 48 - 8 * h, stride=2), :] = R.half[h, lane, 208:256 - 8 * h, :]
    grad_b = jnp.where(odd == 1, R.flat[9:170, :], R.flat[8:169, :])
    R.out_b[...] = jnp.where(odd == 1, R.flat[9:170, :], R.flat[8:169, :])
    for c in sent:
        c.wait_recv()
    total = R.news[0]
    for d in range(1, chips):
        total = total + R.news[d]
    norm = jnp.sqrt(total[0, 0:1, :])
    R.scalars[0:1, :] = total[1, 7:8, :]
    R.scalars[2:3, :] = norm
    for c in sent:
        c.wait_send()
    both.wait_send()


def update_kernel(grad_a, grad_b, scalars, pa, pb, ma, va, mb, vb, *outs):
    clip = jnp.minimum(1.0, clip_level / (scalars[2:3, :] + 1e-06))
    for grad, p, m, v, out in ((grad_a, pa, ma, va, outs[:4]), (grad_b, pb, mb, vb, outs[4:8])):
        g = grad[...] * clip
        first = beta_one * m[...] + (1.0 - beta_one) * g
        second = beta_two * v[...] + (1.0 - beta_two) * g * g
        step = (first * (1.0 / (1.0 - beta_one ** STEP))) / (
            jnp.sqrt(second * (1.0 / (1.0 - beta_two ** STEP))) + adam_eps)
        old = p[...]
        new = old - learn_rate * (step + decay_rate * old)
        out[0][...] = new
        out[1][...] = first
        out[2][...] = second
        out[3][...] = new.astype(bf)
    for k in range(3):
        outs[8 + k][0] = scalars[k, 0]


IN_ALL = ("img", "steps", "labels", "valid", "nidx", "table", "pa", "pb")


def comm_scratch(chips):
    return dict(
        w=((chips, 2, PIECE, C), bf), flat=((184, 128), f32), piece=((2, PIECE, 128), f32),
        ga=((2, A_ROWS + 16, 128), f32), gb=((2, B_ROWS + 16, 128), f32), loss=((1, C), f32),
        r1=((chips, PIECE, C), bf), r2=((8, PIECE, C), bf), r3=((4, PIECE, C), bf), r4=((3, PIECE, C), bf),
        t2=((8, PIECE, C), bf), t3=((4, PIECE, C), bf), t4=((3, PIECE, C), bf),
        half=((2, 2, PIECE, 128), f32), msg=((2, 8, 128), f32), news=((chips, 2, 8, 128), f32))


def sem_counts(chips):
    return dict(zsem=3, ssem=4, tsem=8, csem=16, gcsem=16, gtsem=8, gssem=4, gzsem=3, hsem=1, nsem=chips - 1)


def whole_kernel(chips, *refs):
    R = Refs()
    refs = list(refs)
    for name in IN_ALL:
        setattr(R, name, refs.pop(0))
    R.out_a, R.out_b, R.scalars = refs.pop(0), refs.pop(0), refs.pop(0)
    for name in list(SCRATCH) + list(comm_scratch(chips)):
        setattr(R, name, refs.pop(0))
    for name in sem_counts(chips):
        setattr(R, name, (refs.pop(0), refs.pop(0)))
    place = Place(chips)
    barrier = greet(R, place, chips)
    own_piece(R, place)
    pl.semaphore_wait(barrier, chips)
    gather_weights(R, place, lambda: first_setup(R))
    count = spread_rows(R, chips) * POS
    R.scalars[...] = jnp.zeros((8, 128), f32)
    R.scalars[1:2, :] = count
    unpack_weights(R, R.ga, R.gb)
    time_forward(R)
    R.scale_row[...] = 2.0 / jnp.concatenate([count, count], axis=1)
    for step in STEPS:
        step(R)
    st(R.ga, A_ROWS - 1, jnp.zeros((1, C), f32))
    pack_gradients(R, chips)
    reduce_gradients(R, place)
    finish(R, place, chips)


def whole_step(chips, images, timesteps, labels, valid_slot, noise_idx, noise_table,
               params_a, params_b, first_a, second_a, first_b, second_b):
    smem = pl.BlockSpec(memory_space=pltpu.SMEM)
    vmem = pl.BlockSpec(memory_space=pltpu.VMEM)
    rows = lambda v: v.reshape(-1, 128)
    scratch = [pltpu.VMEM(s, d) for s, d in SCRATCH.values()] + [pltpu.VMEM(s, d) for s, d in comm_scratch(chips).values()]
    for n in sem_counts(chips).values():
        scratch += [pltpu.SemaphoreType.DMA((n,)), pltpu.SemaphoreType.DMA((n,))]
    pa, pb = rows(params_a), rows(params_b)
    grad_a, grad_b, scalars = pl.pallas_call(
        functools.partial(whole_kernel, chips),
        out_shape=[jax.ShapeDtypeStruct((n, 128), f32) for n in (804, 161, 8)],
        in_specs=[vmem, smem, smem, smem] + [vmem] * 4,
        out_specs=[vmem] * 3,
        scratch_shapes=scratch,
        compiler_params=pltpu.CompilerParams(
            collective_id=0, has_side_effects=True, vmem_limit_bytes=63 * 1024 * 1024),
    )(images, timesteps, labels, valid_slot, noise_idx, noise_table, pa, pb)
    shapes = [jax.ShapeDtypeStruct((n, 128), d) for n in (804, 161) for d in (f32, f32, f32, bf)]
    outs = pl.pallas_call(
        update_kernel,
        out_shape=shapes + [jax.ShapeDtypeStruct((1,), f32)] * 3,
        in_specs=[vmem] * 9,
        out_specs=[vmem] * 8 + [smem] * 3,
        compiler_params=pltpu.CompilerParams(vmem_limit_bytes=32 * 1024 * 1024),
    )(grad_a, grad_b, scalars, pa, pb, rows(first_a), rows(second_a), rows(first_b), rows(second_b))
    return (*(v.reshape(-1) for v in outs[:8]), *(v.reshape(()) for v in outs[8:]))


def adam_update(master, grad_in, first_mom, second, clip_scale):
    clipped = grad_in * clip_scale
    first_new = beta_one * first_mom + (1.0 - beta_one) * clipped
    second_new = beta_two * second + (1.0 - beta_two) * clipped * clipped
    first_hat = first_new / (1.0 - beta_one**STEP)
    second_hat = second_new / (1.0 - beta_two**STEP)
    master_new = master - learn_rate * (
        first_hat / (jnp.sqrt(second_hat) + adam_eps) + decay_rate * master
    )
    return (master_new, first_new, second_new)


def plain_step(images, timesteps, labels, valid_slot, noise_idx, noise_table,
               params_a, params_b, first_a, second_a, first_b, second_b):
    gather = lambda v: lax.all_gather(v.astype(bf), "fsdp", axis=0, tiled=True).reshape(-1, C)
    count = lax.psum(jnp.sum(valid_slot).astype(f32) * POS, ("dp", "fsdp"))
    ga, gb, loss = compute(images, timesteps, labels, valid_slot, (2.0 / count).reshape(1), noise_idx, noise_table,
                           gather(params_a), gather(params_b))
    flat = lambda g: jnp.concatenate([g[0], g[1]], axis=1).reshape(-1)
    shard = lambda g: lax.psum_scatter(flat(g), "fsdp", scatter_dimension=0, tiled=True)
    part_a, part_b, loss = lax.psum((shard(ga), shard(gb), jnp.sum(loss)), "dp")
    loss, squares = lax.psum((loss, jnp.sum(part_a * part_a) + jnp.sum(part_b * part_b)), "fsdp")
    norm = jnp.sqrt(squares)
    clip = jnp.minimum(1.0, clip_level / (norm + 1e-06))
    new_a = adam_update(params_a, part_a, first_a, second_a, clip)
    new_b = adam_update(params_b, part_b, first_b, second_b, clip)
    return (*new_a, new_a[0].astype(bf), *new_b, new_b[0].astype(bf), loss, count, norm)


def solution(mesh):
    chips = mesh.shape["fsdp"]
    if chips == 16 and mesh.shape["dp"] == 2:
        step = functools.partial(whole_step, chips)
    else:
        step = plain_step
    both = P(("dp", "fsdp"))
    return jax.shard_map(
        step, mesh=mesh,
        in_specs=(both, both, both, both, both, P()) + (P("fsdp"),) * 6,
        out_specs=(P("fsdp"),) * 8 + (P(),) * 3,
        check_vma=False)
```

```python
import functools
import math
import jax
import jax.numpy as jnp
import numpy as np
from jax import lax
from jax.experimental import pallas as pl
from jax.experimental.pallas import tpu as pltpu
from jax.sharding import PartitionSpec as P

C = 256
SIDE = 16
POS = 256
TE = 512
SIN = 128
NCLS = 10
NT = 256
NIMG = 8
bf = jnp.bfloat16
f32 = jnp.float32
eps_norm = 1e-05
CH = 64
TY = 2
U = dict(conv=8, cback=8, triple=8, attn=8, head=8, aback=8, dx3=8, chunk=8, setup=8)

A_N1, A_K1, A_B1, A_W1, A_TB1, A_W2, A_TB2, A_CT, A_PT, A_PB, A_N2, A_K2, A_B2 = (
    0, 2, 2306, 2307, 2563, 2565, 3589, 3591, 3611, 4123, 4124, 4126, 6430)
A_ROWS = 6432
B_N3, B_W, B_QV, B_WO, B_BO, B_N4, B_WH, B_BH = (0, 2, 770, 772, 1028, 1029, 1031, 1287)
B_ROWS = 1288


def dot(a, b):
    return jnp.dot(a, b, preferred_element_type=f32)


def dot_nt(a, b):
    return lax.dot_general(a, b, (((1,), (1,)), ((), ())), preferred_element_type=f32)


def dot_tn(a, b):
    return lax.dot_general(a, b, (((0,), (0,)), ((), ())), preferred_element_type=f32)


def split3(x):
    hi = x.astype(bf).astype(f32)
    rest = x - hi
    mid = rest.astype(bf).astype(f32)
    return hi, mid, rest - mid


def wide_dot(x, w, nt=False):
    n = x.shape[0]
    stacked = jnp.concatenate(split3(x), axis=0).astype(bf)
    out = dot_nt(stacked, w) if nt else dot(stacked, w)
    return out[:n] + out[n:2 * n] + out[2 * n:]


def outer_sum(a, b):
    a0, a1, _ = split3(a)
    b0, b1, _ = split3(b)
    return dot_tn(jnp.concatenate([a0, a0, a1], axis=0).astype(bf),
                  jnp.concatenate([b0, b1, b0], axis=0).astype(bf))


def sigm(v):
    return 0.5 * jnp.tanh(0.5 * v) + 0.5


def rowsum(x):
    return jnp.sum(x, axis=0, keepdims=True)


def put_shifts(buf, i, r0, x):
    n = x.shape[0]
    col = lax.broadcasted_iota(jnp.int32, x.shape, 0) & 15
    left = jnp.where(col == 0, 0.0, pltpu.roll(x, 1, 0))
    right = jnp.where(col == 15, 0.0, pltpu.roll(x, n - 1, 0))
    y = n // 16
    for s, v in enumerate((left, x, right)):
        buf[pl.ds(1 + r0 // 16, y), i, :, 256 * s:256 * s + 256] = v.astype(bf).reshape(y, 16, C)


def conv_mm(buf, kmat, y):
    ty = TY
    parts = [buf[pl.ds(y + r, ty)].reshape(ty * 128, 3 * C) for r in range(3)]
    return dot(jnp.concatenate(parts, axis=1), kmat[...])


class Refs:
    pass


def ld(f, row, n, stride=1):
    at = pl.ds(row, n, stride=stride) if stride > 1 else pl.ds(row, n)
    return jnp.concatenate([f[0, at, :], f[1, at, :]], axis=1)


def st(f, row, value, stride=1):
    n = value.shape[0]
    at = pl.ds(row, n, stride=stride) if stride > 1 else pl.ds(row, n)
    f[0, at, :] = value[:, :128]
    f[1, at, :] = value[:, 128:]


def unpack_weights(R, fa, fb):
    for kmat, kt, base in ((R.k1, R.k1t, A_K1), (R.k2, R.k2t, A_K2)):
        for t in range(9):
            w = ld(fa, base + 256 * t, 256)
            kmat[256 * t:256 * t + 256, :] = w.astype(bf)
            kt[256 * (8 - t):256 * (8 - t) + 256, :] = w.T.astype(bf)
    for h in range(2):
        R.tw1[:, 256 * h:256 * h + 256] = ld(fa, A_W1 + h, SIN, 2).astype(bf)
        R.tw2[:, 256 * h:256 * h + 256] = ld(fa, A_W2 + h, TE, 2).astype(bf)
    R.pt[...] = ld(fa, A_PT, TE).astype(bf)
    for h in range(3):
        w = ld(fb, B_W + h, C, 3)
        R.wt[:, 256 * h:256 * h + 256] = w.astype(bf)
        R.wtt[256 * h:256 * h + 256, :] = w.T.astype(bf)
    w = ld(fb, B_WO, C)
    R.wo[...] = w.astype(bf)
    R.wot[...] = w.T.astype(bf)
    w = ld(fb, B_WH, C)
    R.wh[...] = w.astype(bf)
    R.wht[...] = w.T.astype(bf)
    for k, row in enumerate((A_N1, A_N1 + 1, A_B1, A_TB1, A_TB1 + 1, A_TB2, A_TB2 + 1, A_PB, A_N2, A_N2 + 1, A_B2)):
        R.vec[k:k + 1, :] = ld(fa, row, 1)
    for k, row in enumerate((B_N3, B_N3 + 1, B_QV, B_QV + 1, B_BO, B_N4, B_N4 + 1, B_BH)):
        R.vec[11 + k:12 + k, :] = ld(fb, row, 1)
    R.ct[0:20, :] = ld(fa, A_CT, 20)


(V_G1, V_C1, V_B1, V_TB1, V_TB1B, V_TB2, V_TB2B, V_PB, V_G2, V_C2, V_B2,
 V_G3, V_C3, V_QB, V_VB, V_BO, V_G4, V_C4, V_BH) = range(19)


def vec(R, k):
    return R.vec[k:k + 1, :]


def group_mean(R, s):
    return wide_dot(s, R.gm[...])


def stats(R, k, load):
    for i in range(NIMG):
        R.tmp[i:i + 1, :] = rowsum(load(i))
    mean = group_mean(R, R.tmp[0:8, :])
    R.mean[k] = mean
    for i in range(NIMG):
        x = load(i) - mean[i:i + 1, :]
        R.tmp[i:i + 1, :] = rowsum(x * x)
    R.inv[k] = lax.rsqrt(group_mean(R, R.tmp[0:8, :]) + eps_norm)


def norm_sums(R, k, gain):
    s1, s2 = R.s1[...], R.s2[...]
    m = group_mean(R, jnp.concatenate([s1 * gain, s2 * gain], axis=0))
    R.m1[...] = m[:8] * R.inv[k]
    R.m2[...] = m[8:] * R.inv[k]
    return rowsum(s2), rowsum(s1)


def first_setup(R):
    row = lax.broadcasted_iota(jnp.int32, (C, C), 0) >> 3
    col = lax.broadcasted_iota(jnp.int32, (C, C), 1) >> 3
    R.gm[...] = jnp.where(row == col, 1.0 / 2048.0, 0.0).astype(bf)
    zero = jnp.zeros((1, NIMG, 16, 3 * C), bf)
    for buf in (R.buf1, R.buf2, R.dbuf):
        buf[0:1] = zero
        buf[17:18] = zero
    hi, mid, lo = split3(R.table[...])
    R.tab3[...] = jnp.concatenate([hi, mid, lo], axis=1).astype(bf)

    @pl.loop(0, NIMG, unroll=U["setup"])
    def _(i):
        rows = lax.broadcasted_iota(jnp.int32, (NT, POS), 0)
        hot = jnp.where(rows == R.nidx[pl.ds(i, 1), :], 1.0, 0.0)
        out = dot(hot.T.astype(bf), R.tab3[...])
        R.target[i] = out[:, :C] + out[:, C:2 * C] + out[:, 2 * C:]
    stats(R, 0, lambda i: R.img[i].astype(f32))


def column_of(smem, shape):
    row = lax.broadcasted_iota(jnp.int32, shape, 0)
    out = jnp.zeros(shape, jnp.int32)
    for i in range(NIMG):
        out = jnp.where(row == i, smem[i], out)
    return out


def time_forward(R):
    lane = lax.broadcasted_iota(jnp.int32, (NIMG, SIN), 1)
    factor = math.log(10000.0) / (SIN // 2 - 1)
    freq = jnp.exp((lane & 63).astype(f32) * -factor)
    angle = column_of(R.steps, (NIMG, SIN)).astype(f32) * freq
    e = jnp.where(lane < 64, jnp.sin(angle), jnp.cos(angle))
    R.emb[...] = e
    u = wide_dot(e, R.tw1[...]) + jnp.concatenate([vec(R, V_TB1), vec(R, V_TB1B)], axis=1)
    R.pre[...] = u
    lab = column_of(R.labels, (NIMG, TE))
    te = wide_dot(u * sigm(u), R.tw2[...]) + jnp.concatenate([vec(R, V_TB2), vec(R, V_TB2B)], axis=1)
    for j in range(NCLS):
        row = jnp.concatenate([R.ct[2 * j:2 * j + 1, :], R.ct[2 * j + 1:2 * j + 2, :]], axis=1)
        te = te + jnp.where(lab == j, row, 0.0)
    R.te[...] = te
    add = wide_dot(te * sigm(te), R.pt[...]) + vec(R, V_PB) + vec(R, V_B1)
    for i in range(NIMG):
        R.addb[i] = jnp.broadcast_to(add[i:i + 1, :], (16, C))


def each_chunk(fn):
    @pl.loop(0, NIMG, unroll=U["chunk"])
    def _(i):
        for c in range(POS // CH):
            fn(i, c * CH)


def normed(R, k, i, x):
    return (x - R.mean[k, pl.ds(i, 1), :]) * R.inv[k, pl.ds(i, 1), :]


def step_x1(R):
    def one(i, r0):
        x = normed(R, 0, i, R.img[i, r0:r0 + CH, :].astype(f32))
        a = x * vec(R, V_G1) + vec(R, V_C1)
        put_shifts(R.buf1, i, r0, a * sigm(a))
    each_chunk(one)


def step_conv1(R):
    @pl.loop(0, SIDE // TY, unroll=U["conv"])
    def _(t):
        acc = conv_mm(R.buf1, R.k1, t * TY).reshape(TY, NIMG, 16, C)
        for yy in range(TY):
            R.c1[:, pl.ds(pl.multiple_of((t * TY + yy) * 16, 16), 16), :] = acc[yy] + R.addb[...]


def step_stats1(R):
    stats(R, 1, lambda i: R.c1[i])


def step_x2(R):
    def two(i, r0):
        x = normed(R, 1, i, R.c1[i, r0:r0 + CH, :])
        a = x * vec(R, V_G2) + vec(R, V_C2)
        put_shifts(R.buf2, i, r0, a * sigm(a))
    each_chunk(two)


def step_conv2(R):
    @pl.loop(0, SIDE // TY, unroll=U["conv"])
    def _(t):
        acc = conv_mm(R.buf2, R.k2, t * TY).reshape(TY, NIMG, 16, C)
        for yy in range(TY):
            at = pl.ds(pl.multiple_of((t * TY + yy) * 16, 16), 16)
            R.h1[:, at, :] = acc[yy] + R.img[:, at, :].astype(f32) + vec(R, V_B2)


def step_stats2(R):
    stats(R, 2, lambda i: R.h1[i])


def step_triple(R):
    bias = jnp.concatenate([vec(R, V_QB), jnp.zeros((1, C), f32), vec(R, V_VB)], axis=1)

    @pl.loop(0, NIMG, unroll=U["triple"])
    def _(i):
        x = (normed(R, 2, i, R.h1[i]) * vec(R, V_G3) + vec(R, V_C3)).astype(bf)
        R.x3t[:, pl.ds(pl.multiple_of(i * POS, POS), POS)] = x.T
        R.tri[i] = (dot(x, R.wt[...]) + bias).astype(bf)


def step_attn(R):
    @pl.loop(0, NIMG, unroll=U["attn"])
    def _(i):
        k = R.tri[i, :, C:2 * C]
        v = R.tri[i, :, 2 * C:]
        for h in range(2):
            at = slice(128 * h, 128 * h + 128)
            s = dot_nt(R.tri[i, at, 0:C], k) * C ** (-0.5)
            e = jnp.exp(s - jnp.max(s, axis=1, keepdims=True))
            p = e * (1.0 / jnp.sum(e, axis=1, keepdims=True))
            R.p[i, at, :] = p
            o = dot(p.astype(bf), v).astype(bf)
            R.o[i, at, :] = o
            R.h2[i, at, :] = R.h1[i, at, :] + dot(o, R.wo[...]) + vec(R, V_BO)


def step_stats3(R):
    stats(R, 3, lambda i: R.h2[i])


def step_head(R):
    scale = R.scale_row[...]
    R.loss[...] = jnp.zeros_like(R.loss)
    R.sh[...] = jnp.zeros_like(R.sh)

    @pl.loop(0, NIMG, unroll=U["head"])
    def _(i):
        valid = R.valid[i].astype(f32)
        s1 = jnp.zeros((1, C), f32)
        s2 = jnp.zeros((1, C), f32)
        for h in range(2):
            at = slice(128 * h, 128 * h + 128)
            x = normed(R, 3, i, R.h2[i, at, :])
            a = x * vec(R, V_G4) + vec(R, V_C4)
            sg = sigm(a)
            x4 = (a * sg).astype(bf)
            R.xt[:, pl.ds(pl.multiple_of(i * POS + 128 * h, 128), 128)] = x4.T
            differ = dot(x4, R.wh[...]) + vec(R, V_BH) - R.target[i, at, :]
            dv = valid * differ
            R.loss[...] += rowsum(dv * differ)
            dp = dv * scale
            R.sh[...] += rowsum(dp)
            low = dp.astype(bf)
            R.low[i, at, :] = low
            da = dot(low, R.wht[...]) * (sg * (1.0 + a * (1.0 - sg)))
            R.da[i, at, :] = da
            s1 += rowsum(da)
            s2 += rowsum(da * x)
        R.s1[pl.ds(i, 1), :] = s1
        R.s2[pl.ds(i, 1), :] = s2


def step_head_grads(R):
    st(R.gb, B_BH, R.sh[...])
    st(R.gb, B_WH, dot(R.xt[...], R.low[...].reshape(NIMG * POS, C)))
    dg, db = norm_sums(R, 3, vec(R, V_G4))
    st(R.gb, B_N4, dg)
    st(R.gb, B_N4 + 1, db)


def step_attn_back(R):
    R.sh[...] = jnp.zeros_like(R.sh)
    R.sq[...] = jnp.zeros_like(R.sq)

    @pl.loop(0, NIMG, unroll=U["aback"])
    def _(i):
        x = normed(R, 3, i, R.h2[i])
        d = (R.inv[3, pl.ds(i, 1), :] * vec(R, V_G4)) * R.da[i] - R.m1[pl.ds(i, 1), :] - x * R.m2[pl.ds(i, 1), :]
        R.dh[i] = d
        R.sh[...] += rowsum(d)
        low = d.astype(bf)
        R.low[i] = low
        R.xt[:, pl.ds(pl.multiple_of(i * POS, POS), POS)] = R.o[i].T
        dm = dot(low, R.wot[...]).astype(bf)
        p = R.p[i]
        q = R.tri[i, :, 0:C]
        k = R.tri[i, :, C:2 * C]
        v = R.tri[i, :, 2 * C:]
        dv = dot_tn(p.astype(bf), dm).astype(bf)
        dpr = dot_nt(dm, v)
        ds = (p * (dpr - jnp.sum(dpr * p, axis=1, keepdims=True))).astype(bf)
        dq = (dot(ds, k) * C ** (-0.5)).astype(bf)
        dk = (dot_tn(ds, q) * C ** (-0.5)).astype(bf)
        R.tri[i, :, 0:C] = dq
        R.tri[i, :, C:2 * C] = dk
        R.tri[i, :, 2 * C:] = dv
        R.sq[:, 0:C] += rowsum(dq.astype(f32))
        R.sq[:, C:2 * C] += rowsum(dv.astype(f32))
    st(R.gb, B_BO, R.sh[...])
    st(R.gb, B_QV, R.sq[:, 0:C])
    st(R.gb, B_QV + 1, R.sq[:, C:2 * C])


def step_out_grads(R):
    st(R.gb, B_WO, dot(R.xt[...], R.low[...].reshape(NIMG * POS, C)))


def step_dx3(R):
    @pl.loop(0, NIMG, unroll=U["dx3"])
    def _(i):
        da = dot(R.tri[i], R.wtt[...])
        R.da[i] = da
        R.s1[pl.ds(i, 1), :] = rowsum(da)
        R.s2[pl.ds(i, 1), :] = rowsum(da * normed(R, 2, i, R.h1[i]))


def step_triple_grads(R):
    for h in range(3):
        st(R.gb, B_W + h, dot(
            R.x3t[...], R.tri[:, :, 256 * h:256 * h + 256].reshape(NIMG * POS, C)), 3)
    dg, db = norm_sums(R, 2, vec(R, V_G3))
    st(R.gb, B_N3, dg)
    st(R.gb, B_N3 + 1, db)


def kernel_lhs(R, buf):
    @pl.loop(0, SIDE // 2, unroll=8)
    def _(t):
        x = buf[pl.ds(1 + 2 * t, 2), :, :, C:2 * C].reshape(256, C)
        R.xt[:, pl.ds(pl.multiple_of(t * 256, 256), 256)] = x.T


def kernel_taps(R, row, taps):
    for tap in taps:
        r, s = divmod(tap, 3)
        d = R.dbuf[2 - r:18 - r, :, :, 256 * (2 - s):256 * (3 - s)].reshape(NIMG * POS, C)
        st(R.ga, row + tap * 256, dot(R.xt[...], d))


def conv_back(R, kt, rows=(0, SIDE // TY)):
    @pl.loop(rows[0], rows[1], unroll=8)
    def _(t):
        acc = conv_mm(R.dbuf, kt, t * TY).reshape(TY, NIMG, 16, C)
        for yy in range(TY):
            R.da[:, pl.ds(pl.multiple_of((t * TY + yy) * 16, 16), 16), :] = acc[yy]


def swish_back(R, k, load, vg, vc, keep):
    R.s1[...] = jnp.zeros_like(R.s1)
    R.s2[...] = jnp.zeros_like(R.s2)

    def one(i, r0):
        x = normed(R, k, i, load(i, r0))
        a = x * vec(R, vg) + vec(R, vc)
        sg = sigm(a)
        da = R.da[i, r0:r0 + CH, :] * (sg * (1.0 + a * (1.0 - sg)))
        if keep:
            R.da[i, r0:r0 + CH, :] = da
        R.s1[pl.ds(i, 1), :] += rowsum(da)
        R.s2[pl.ds(i, 1), :] += rowsum(da * x)
    each_chunk(one)


def step_dh1(R):
    R.sh[...] = jnp.zeros_like(R.sh)

    def one(i, r0):
        at = slice(r0, r0 + CH)
        x = normed(R, 2, i, R.h1[i, at, :])
        d = (R.dh[i, at, :] + (R.inv[2, pl.ds(i, 1), :] * vec(R, V_G3)) * R.da[i, at, :]
             - R.m1[pl.ds(i, 1), :] - x * R.m2[pl.ds(i, 1), :])
        R.sh[...] += rowsum(d)
        put_shifts(R.dbuf, i, r0, d)
    each_chunk(one)
    st(R.ga, A_B2, R.sh[...])


def step_dk2(R):
    kernel_lhs(R, R.buf2)
    kernel_taps(R, A_K2, range(9))


def step_dx2_high(R):
    conv_back(R, R.k2t, (0, 4))


def step_dx2_low(R):
    conv_back(R, R.k2t, (4, 8))


def step_da2(R):
    swish_back(R, 1, lambda i, r0: R.c1[i, r0:r0 + CH, :], V_G2, V_C2, True)
    dg, db = norm_sums(R, 1, vec(R, V_G2))
    st(R.ga, A_N2, dg)
    st(R.ga, A_N2 + 1, db)


def step_dc1(R):
    R.tmp[...] = jnp.zeros_like(R.tmp)

    def two(i, r0):
        at = slice(r0, r0 + CH)
        x = normed(R, 1, i, R.c1[i, at, :])
        d = ((R.inv[1, pl.ds(i, 1), :] * vec(R, V_G2)) * R.da[i, at, :]
             - R.m1[pl.ds(i, 1), :] - x * R.m2[pl.ds(i, 1), :])
        R.tmp[pl.ds(i, 1), :] += rowsum(d)
        put_shifts(R.dbuf, i, r0, d)
    each_chunk(two)


def step_dk1_high(R):
    kernel_lhs(R, R.buf1)
    kernel_taps(R, A_K1, (6, 7, 8))


def step_dk1_mid(R):
    kernel_taps(R, A_K1, (3, 4, 5))


def step_dk1_low(R):
    kernel_taps(R, A_K1, (0, 1, 2))


def step_dx1_high(R):
    conv_back(R, R.k1t, (0, 4))


def step_dx1_low(R):
    conv_back(R, R.k1t, (4, 8))


def step_da1(R):
    swish_back(R, 0, lambda i, r0: R.img[i, r0:r0 + CH, :].astype(f32), V_G1, V_C1, False)
    R.n1[0:1, :] = rowsum(R.s2[...])
    R.n1[1:2, :] = rowsum(R.s1[...])


def swish_slope(v):
    s = sigm(v)
    return s * (1.0 + v * (1.0 - s))


def time_backward(R):
    d_add = R.tmp[0:8, :]
    total = rowsum(d_add)
    st(R.ga, A_B1, total)
    st(R.ga, A_PB, total)
    te = R.te[...]
    st(R.ga, A_PT, outer_sum(te * sigm(te), d_add))
    d_te = wide_dot(d_add, R.pt[...], nt=True) * swish_slope(te)
    lab = column_of(R.labels, (NIMG, TE))
    for j in range(NCLS):
        row = rowsum(jnp.where(lab == j, d_te, 0.0))
        for h in range(2):
            st(R.ga, A_CT + 2 * j + h, row[:, 256 * h:256 * h + 256])
    row = rowsum(d_te)
    u = R.pre[...]
    dw2 = outer_sum(u * sigm(u), d_te)
    d_u = wide_dot(d_te, R.tw2[...], nt=True) * swish_slope(u)
    row1 = rowsum(d_u)
    dw1 = outer_sum(R.emb[...], d_u)
    for h in range(2):
        st(R.ga, A_TB2 + h, row[:, 256 * h:256 * h + 256])
        st(R.ga, A_TB1 + h, row1[:, 256 * h:256 * h + 256])
        st(R.ga, A_W2 + h, dw2[:, 256 * h:256 * h + 256], 2)
        st(R.ga, A_W1 + h, dw1[:, 256 * h:256 * h + 256], 2)


FORWARD = (step_x1, step_conv1, step_stats1, step_x2, step_conv2, step_stats2, step_triple, step_attn, step_stats3,
           step_head, step_head_grads, step_attn_back, step_out_grads, step_dx3, step_triple_grads)
BACKWARD = (step_dh1, step_dk2, step_dx2_high, step_dx2_low, step_da2, step_dc1, time_backward, step_dk1_high, step_dk1_mid, step_dk1_low,
            step_dx1_high, step_dx1_low, step_da1)
STEPS = FORWARD + BACKWARD


SCRATCH = dict(
    k1=((2304, C), bf), k1t=((2304, C), bf), k2=((2304, C), bf), k2t=((2304, C), bf),
    tw1=((SIN, TE), bf), tw2=((TE, TE), bf), pt=((TE, C), bf),
    wt=((C, 3 * C), bf), wtt=((3 * C, C), bf), wo=((C, C), bf), wot=((C, C), bf), wh=((C, C), bf), wht=((C, C), bf),
    vec=((24, C), f32), ct=((24, C), f32),
    gm=((C, C), bf), tab3=((NT, 3 * C), bf), target=((NIMG, POS, C), f32),
    tmp=((8, C), f32), mean=((4, 8, C), f32), inv=((4, 8, C), f32),
    s1=((8, C), f32), s2=((8, C), f32), m1=((8, C), f32), m2=((8, C), f32),
    sh=((1, C), f32), scale_row=((1, C), f32), n1=((8, C), f32), sq=((1, 2 * C), f32),
    emb=((8, SIN), f32), pre=((8, TE), f32), te=((8, TE), f32), addb=((8, 16, C), f32),
    buf1=((18, 8, 16, 3 * C), bf), buf2=((18, 8, 16, 3 * C), bf), dbuf=((18, 8, 16, 3 * C), bf),
    c1=((8, POS, C), f32), h1=((8, POS, C), f32), h2=((8, POS, C), f32), da=((8, POS, C), f32), dh=((8, POS, C), f32),
    p=((8, POS, POS), f32), o=((8, POS, C), bf), low=((8, POS, C), bf),
    tri=((8, POS, 3 * C), bf),
    x3t=((C, 8 * POS), bf), xt=((C, 8 * POS), bf),
)


def main_kernel(names_in, *refs):
    R = Refs()
    n_in = len(names_in)
    for name, r in zip(names_in, refs):
        setattr(R, name, r)
    R.ga, R.gb, R.loss = refs[n_in:n_in + 3]
    for name, r in zip(list(SCRATCH), refs[n_in + 3:]):
        setattr(R, name, r)
    fa, fb = R.ga, R.gb
    for c in range(0, A_ROWS, 402):
        st(fa, c, R.wa[c:c + 402, :].astype(f32))
    st(fb, 0, R.wb[...].astype(f32))
    R.scale_row[...] = jnp.full((1, C), R.scale[0])
    first_setup(R)
    unpack_weights(R, fa, fb)
    time_forward(R)
    for step in STEPS:
        step(R)
    st(R.ga, A_N1, R.n1[0:2, :])
    st(R.ga, A_ROWS - 1, jnp.zeros((1, C), f32))


def compute(img, steps, labels, valid, scale, nidx, table, wa, wb):
    smem = pl.BlockSpec(memory_space=pltpu.SMEM)
    vmem = pl.BlockSpec(memory_space=pltpu.VMEM)
    names = ("img", "steps", "labels", "valid", "scale", "nidx", "table", "wa", "wb")
    return pl.pallas_call(
        functools.partial(main_kernel, names),
        out_shape=(jax.ShapeDtypeStruct((2, A_ROWS, 128), f32), jax.ShapeDtypeStruct((2, B_ROWS, 128), f32),
                   jax.ShapeDtypeStruct((1, C), f32)),
        in_specs=[vmem, smem, smem, smem, smem, vmem, vmem, vmem, vmem],
        out_specs=(vmem, vmem, vmem),
        scratch_shapes=[pltpu.VMEM(s, d) for s, d in SCRATCH.values()],
        compiler_params=pltpu.CompilerParams(vmem_limit_bytes=63 * 1024 * 1024),
    )(img, steps, labels, valid, scale, nidx, table, wa, wb)


beta_one = 0.5
beta_two = 0.5
learn_rate = 0.1
decay_rate = 0.01
adam_eps = 1e-08
clip_level = 0.01
STEP = 5
PA = A_ROWS * C
PB = B_ROWS * C
MESH = pl.DeviceIdType.MESH
ORDER = (0, 1, 3, 2)
HALF_A, HALF_B, PIECE = 201, 48, 256
B_AT = 208


class Place:
    def __init__(self, chips):
        self.me = lax.axis_index("fsdp")
        self.core = lax.axis_index("dp")
        self.depth = chips // 4

    def z(self, k, d):
        return lax.rem(lax.div(k, 4) + d + self.depth, self.depth) * 4 + lax.rem(k, 4)

    def flip_x(self, k):
        return k + 1 - 2 * lax.rem(k, 2)

    def flip_y(self, k):
        return k + 2 - 4 * lax.rem(lax.div(k, 2), 2)

    def s(self, k):
        return self.core * self.flip_x(k) + (1 - self.core) * self.flip_y(k)

    def t(self, k):
        return self.core * self.flip_y(k) + (1 - self.core) * self.flip_x(k)

    def pieces(self):
        line = [self.z(self.me, -j) for j in range(4)]
        near = line + [self.s(k) for k in line]
        return near + [self.t(k) for k in near]


def send(src, dst, sems, at, core, chip):
    copy = pltpu.make_async_remote_copy(
        src_ref=src, dst_ref=dst, send_sem=sems[0].at[at], recv_sem=sems[1].at[at],
        device_id=(core, chip), device_id_type=MESH)
    copy.start()
    return copy


def greet(R, place, chips):
    barrier = pltpu.get_barrier_semaphore()
    for d in range(1, chips):
        pl.semaphore_signal(barrier, inc=1, device_id=(place.core, lax.rem(place.me + d, chips)), device_id_type=MESH)
    pl.semaphore_signal(barrier, inc=1, device_id=(1 - place.core, place.me), device_id_type=MESH)
    return barrier


def own_piece(R, place):
    count = R.valid[0]
    for i in range(1, NIMG):
        count = count + R.valid[i]
    count = count.astype(f32)
    odd = lax.rem(place.me, 2) == 1
    R.flat[0:8, :] = jnp.zeros((8, 128), f32)
    R.flat[168:184, :] = jnp.zeros((16, 128), f32)
    R.flat[8:169, :] = R.pb[...]
    for h in range(2):
        for lane in range(2):
            R.piece[lane, 0:201, :] = R.pa[pl.ds(402 * h + lane, 201, stride=2), :]
            even_rows = R.flat[pl.ds(8 + lane + 96 * h, 48 - 8 * h, stride=2), :]
            odd_rows = R.flat[pl.ds(7 + lane + 96 * h, 48 - 8 * h, stride=2), :]
            R.piece[lane, 208:256 - 8 * h, :] = jnp.where(odd, odd_rows, even_rows)
        R.piece[:, 201:208, :] = jnp.full((2, 7, 128), count)

        @pl.when(place.core == h)
        def _():
            R.w[place.me, h] = jnp.concatenate([R.piece[0], R.piece[1]], axis=1).astype(bf)


def gather_weights(R, place, meanwhile):
    me, core = place.me, place.core
    got = place.pieces()
    put = lambda k: R.w.at[k, core]
    over_s, over_t = place.s(me), place.t(me)
    zc = {d: send(put(me), put(me), R.zsem, d - 1, core, place.z(me, d)) for d in (1, 3, 2)}
    sc, tc, sib = {}, {}, {}
    for j in ORDER:
        if j == 1:
            meanwhile()
        if j:
            zc[j].wait_recv()
        sc[j] = send(put(got[j]), put(got[j]), R.ssem, j, core, over_s)
        tc[j] = send(put(got[j]), put(got[j]), R.tsem, j, core, over_t)
        sib[j] = send(put(got[j]), put(got[j]), R.csem, j, 1 - core, me)
    for j in ORDER:
        sc[j].wait_recv()
        q = 4 + j
        tc[q] = send(put(got[q]), put(got[q]), R.tsem, q, core, over_t)
        sib[q] = send(put(got[q]), put(got[q]), R.csem, q, 1 - core, me)
    for half in (0, 4):
        for j in ORDER:
            q = half + j
            tc[q].wait_recv()
            sib[8 + q] = send(put(got[8 + q]), put(got[8 + q]), R.csem, 8 + q, 1 - core, me)
    for c in sib.values():
        c.wait_recv()
    for group in (zc, sc, tc, sib):
        for c in group.values():
            c.wait_send()


def spread_rows(R, chips):
    count = jnp.zeros((1, 128), f32)
    for k in range(chips):
        base = (161 * k) // 2
        odd = k % 2
        for h in range(2):
            a = R.w[k, h, 0:208, :].astype(f32)
            row = 402 * k + 201 * h
            R.ga[0, row:row + 208, :] = a[:, :128]
            R.ga[1, row:row + 208, :] = a[:, 128:]
            count = count + a[201:202, :128]
            b = R.w[k, h, 208:256, :].astype(f32)
            if h == 0:
                R.gb[0, base + odd:base + 48, :] = b[odd:, :128]
                R.gb[1, base:base + 48, :] = b[:, 128:]
            else:
                R.gb[0, base + 48:base + 81, :] = b[:33, :128]
                R.gb[1, base + 48:base + 80 + odd, :] = b[:32 + odd, 128:]
    return count


def pack_a(R, zt):
    for k in range(4 * zt, 4 * zt + 4):
        for h in range(2):
            R.w[k, h, 0:B_AT, :] = ld(R.ga, 402 * k + 201 * h, B_AT).astype(bf)


def pack_b(R, chips):
    for k in range(chips):
        base = (161 * k) // 2
        for h in range(2):
            R.w[k, h, B_AT:PIECE, :] = ld(R.gb, base + HALF_B * h, HALF_B).astype(bf)


def late(src, dst, send_sem, recv_sem, core, chip):
    return pltpu.make_async_remote_copy(src_ref=src, dst_ref=dst, send_sem=send_sem, recv_sem=recv_sem,
                                        device_id=(core, chip), device_id_type=MESH)


class Reduction:
    def __init__(self, R, place, at):
        self.R, self.place, self.at = R, place, at
        self.planes = (at,) if at < 4 else range(4)
        self.rows = pl.ds(0, B_AT) if at < 4 else pl.ds(B_AT, HALF_B)
        me, core, rows = place.me, place.core, self.rows
        self.mine = lax.rem(me, 4)
        self.z = lax.div(me, 4)
        group = pl.ds(4 * at, 4) if at < 4 else pl.ds(0, 16)
        plane = pl.ds(at, 1) if at < 4 else pl.ds(0, 4)
        sems = lambda pair: (pair[0].at[at], pair[1].at[at])
        self.across_core = late(R.w.at[group, 1 - core, rows], R.r1.at[group, rows], *sems(R.gcsem), 1 - core, me)
        self.across_t = late(R.t2.at[plane, :, rows], R.r2.at[plane, :, rows], *sems(R.gtsem), core, place.t(me))
        self.across_s = late(R.t3.at[plane, rows], R.r3.at[plane, rows], *sems(R.gssem), core, place.s(me))
        self.along = {}
        for zt in self.planes:
            far, mid, near = (3, 2, 1 - zt) if zt < 2 else (0, 1, 5 - zt)
            base = 2 * (zt if at < 4 else 4 + zt)
            go = lambda slot, to: late(R.t4.at[zt, rows], R.r4.at[zt, slot, rows], R.gzsem[0].at[base + slot],
                                       R.gzsem[1].at[base + slot], core, 4 * to + self.mine)
            self.along[zt] = (far, mid, near, go(1, mid), go(1, zt), go(0, zt))

    def both_cores(self, k):
        R = self.R
        return R.w[k, self.place.core, self.rows].astype(f32) + R.r1[k, self.rows].astype(f32)

    def start(self):
        self.across_core.start()

    def step_t(self):
        R, place = self.R, self.place
        self.across_core.wait_recv()
        for zt in self.planes:
            k = place.t(4 * zt + self.mine)
            R.t2[zt, 0, self.rows] = self.both_cores(place.s(k)).astype(bf)
            R.t2[zt, 1, self.rows] = self.both_cores(k).astype(bf)
        self.across_t.start()

    def step_s(self):
        R = self.R
        self.across_t.wait_recv()
        for zt in self.planes:
            k = self.place.s(4 * zt + self.mine)
            R.t3[zt, self.rows] = (self.both_cores(k) + R.r2[zt, 0, self.rows].astype(f32)).astype(bf)
        self.across_s.start()

    def step_z(self):
        R = self.R
        self.across_s.wait_recv()
        for zt in self.planes:
            far, mid, near, to_mid, mid_on, near_on = self.along[zt]
            total = (self.both_cores(4 * zt + self.mine) + R.r2[zt, 1, self.rows].astype(f32)
                     + R.r3[zt, self.rows].astype(f32))

            @pl.when(self.z == zt)
            def _():
                R.half[self.place.core, 0, self.rows] = total[:, :128]
                R.half[self.place.core, 1, self.rows] = total[:, 128:]

            @pl.when(self.z != zt)
            def _():
                R.t4[zt, self.rows] = total.astype(bf)

            @pl.when(self.z == far)
            def _():
                to_mid.start()

            @pl.when(self.z == near)
            def _():
                near_on.start()

    def step_mid(self):
        R = self.R
        for zt in self.planes:
            far, mid, near, to_mid, mid_on, near_on = self.along[zt]

            @pl.when(self.z == mid)
            def _():
                to_mid.wait_recv()
                R.t4[zt, self.rows] = (R.t4[zt, self.rows].astype(f32) + R.r4[zt, 1, self.rows].astype(f32)).astype(bf)
                mid_on.start()

    def step_end(self):
        R, core = self.R, self.place.core
        for zt in self.planes:
            far, mid, near, to_mid, mid_on, near_on = self.along[zt]

            @pl.when(self.z == zt)
            def _():
                near_on.wait_recv()
                mid_on.wait_recv()
                more = R.r4[zt, 0, self.rows].astype(f32) + R.r4[zt, 1, self.rows].astype(f32)
                R.half[core, 0, self.rows] += more[:, :128]
                R.half[core, 1, self.rows] += more[:, 128:]

    def drain(self):
        for c in (self.across_core, self.across_t, self.across_s):
            c.wait_send()
        for zt in self.planes:
            far, mid, near, to_mid, mid_on, near_on = self.along[zt]

            @pl.when(self.z == far)
            def _():
                to_mid.wait_send()

            @pl.when(self.z == mid)
            def _():
                mid_on.wait_send()

            @pl.when(self.z == near)
            def _():
                near_on.wait_send()


class NormOne:
    def __init__(self, R, place, chips):
        self.R, self.me, self.core, self.chips = R, place.me, place.core, chips
        self.cross = late(R.n1, R.n1_in.at[0], R.n1sem[0].at[0], R.n1sem[1].at[0], 1 - place.core, place.me)
        self.home = [late(R.n1_out, R.n1_in.at[d], R.n1sem[0].at[d], R.n1sem[1].at[d], place.core,
                          lax.rem(place.me + chips - d, chips)) for d in range(1, chips)]

    def start(self):
        @pl.when(self.core == 1)
        def _():
            self.cross.start()

    def to_home(self):
        R = self.R

        @pl.when(self.core == 0)
        def _():
            self.cross.wait_recv()
            R.n1_out[...] = R.n1[...] + R.n1_in[0]
        for d in range(1, self.chips):
            @pl.when(jnp.logical_and(self.core == 0, self.me == d))
            def _():
                self.home[d - 1].start()

    def end(self):
        R = self.R

        @pl.when(jnp.logical_and(self.core == 0, self.me == 0))
        def _():
            total = R.n1_out[...]
            for d in range(1, self.chips):
                self.home[d - 1].wait_recv()
                total = total + R.n1_in[d]
            R.half[0, 0, 0:2, :] = total[0:2, :128]
            R.half[0, 1, 0:2, :] = total[0:2, 128:]

    def drain(self):
        @pl.when(self.core == 1)
        def _():
            self.cross.wait_send()
        for d in range(1, self.chips):
            @pl.when(jnp.logical_and(self.core == 0, self.me == d))
            def _():
                self.home[d - 1].wait_send()


def backward_and_reduce(R, place, chips):
    r0, r1, r2, r3, rb = (Reduction(R, place, at) for at in range(5))
    n1 = NormOne(R, place, chips)
    R.n1[...] = jnp.zeros((8, C), f32)
    st(R.ga, A_N1, jnp.zeros((2, C), f32))
    st(R.ga, A_ROWS - 1, jnp.zeros((1, C), f32))
    pack_b(R, chips)
    rb.start()
    step_dh1(R)
    rb.step_t()
    step_dk2(R)
    pack_a(R, 3)
    r3.start()
    rb.step_s()
    step_dx2_high(R)
    r3.step_t()
    step_dx2_low(R)
    rb.step_z()
    step_da2(R)
    step_dc1(R)
    r3.step_s()
    time_backward(R)
    pack_a(R, 2)
    r2.start()
    rb.step_mid()
    step_dk1_high(R)
    pack_a(R, 1)
    r1.start()
    r2.step_t()
    step_dk1_mid(R)
    r3.step_z()
    step_dk1_low(R)
    pack_a(R, 0)
    r0.start()
    r1.step_t()
    step_dx1_high(R)
    r0.step_t()
    r2.step_s()
    step_dx1_low(R)
    r3.step_mid()
    rb.step_end()
    step_da1(R)
    n1.start()
    r1.step_s()
    r2.step_z()
    r0.step_s()
    n1.to_home()
    r1.step_z()
    r2.step_mid()
    r3.step_end()
    r0.step_z()
    r1.step_mid()
    r0.step_mid()
    r2.step_end()
    r1.step_end()
    r0.step_end()
    n1.end()
    for c in (rb, r3, r2, r1, r0, n1):
        c.drain()


def finish(R, place, chips):
    me, core = place.me, place.core
    loss = jnp.sum(R.loss[...], axis=1, keepdims=True)
    R.half[core, :, 201:208, :] = jnp.broadcast_to(loss, (2, 7, 128))
    both = send(R.half.at[core], R.half.at[core], R.hsem, 0, 1 - core, me)
    both.wait_recv()
    odd = lax.rem(me, 2)
    row = lax.broadcasted_iota(jnp.int32, (256, 128), 0)
    squares = jnp.zeros((1, 128), f32)
    for h in range(2):
        for lane in range(2):
            g = R.half[h, lane]
            keep = row < 201
            if h == 0:
                b_in = row >= 208 + (odd if lane == 0 else 0)
            else:
                b_in = jnp.logical_and(row >= 208, row < 208 + (33 if lane == 0 else 32 + odd))
            g = jnp.where(jnp.logical_or(keep, b_in), g, 0.0)
            squares = squares + rowsum(g * g)
    R.msg[0] = jnp.broadcast_to(jnp.sum(squares, axis=1, keepdims=True), (8, 128))
    R.msg[1] = R.half[0, 0, 200:208, :] + R.half[1, 0, 200:208, :]
    R.news[0] = R.msg[...]
    sent = []
    for d in range(1, chips):
        sent.append(send(R.msg, R.news.at[d], R.nsem, d - 1, core, lax.rem(me + d, chips)))
    for lane in range(2):
        for h in range(2):
            R.flat_a[pl.ds(402 * h + lane, 201, stride=2), :] = R.half[h, lane, 0:201, :]
            R.flat[pl.ds(8 + 96 * h + lane, 48 - 8 * h, stride=2), :] = R.half[h, lane, 208:256 - 8 * h, :]
    grad_b = jnp.where(odd == 1, R.flat[9:170, :], R.flat[8:169, :])
    R.flat_b[0:161, :] = jnp.where(odd == 1, R.flat[9:170, :], R.flat[8:169, :])
    outs = [pltpu.make_async_copy(R.flat_a, R.out_a, R.osem.at[0]), pltpu.make_async_copy(R.flat_b, R.out_b, R.osem.at[1])]
    for c in outs:
        c.start()
    for c in sent:
        c.wait_recv()
    total = R.news[0]
    for d in range(1, chips):
        total = total + R.news[d]
    norm = jnp.sqrt(total[0, 0:1, :])
    R.scalars[0:1, :] = total[1, 7:8, :]
    R.scalars[2:3, :] = norm
    for c in sent:
        c.wait_send()
    both.wait_send()
    for c in outs:
        c.wait()


def update_kernel(*refs):
    ins, scalars, outs, refs = refs[:8], refs[8], refs[9:20], refs[20:]
    bufs, news, in_sem, out_sem = refs[:8], refs[8:16], refs[16], refs[17]
    loads = [pltpu.make_async_copy(a, b, in_sem.at[k]) for k, (a, b) in enumerate(zip(ins, bufs))]
    for c in loads:
        c.start()
    clip = jnp.minimum(1.0, clip_level / (scalars[2:3, :] + 1e-06))
    for k in range(3):
        outs[8 + k][0] = scalars[k, 0]
    stores = []
    for part, rows in ((1, 161), (0, 804)):
        grad, p, m, v = bufs[4 * part:4 * part + 4]
        for c in loads[4 * part:4 * part + 4]:
            c.wait()
        g = grad[0:rows, :] * clip
        first = beta_one * m[...] + (1.0 - beta_one) * g
        second = beta_two * v[...] + (1.0 - beta_two) * g * g
        step = (first * (1.0 / (1.0 - beta_one ** STEP))) / (
            jnp.sqrt(second * (1.0 / (1.0 - beta_two ** STEP))) + adam_eps)
        old = p[...]
        new = old - learn_rate * (step + decay_rate * old)
        for k, value in enumerate((new, first, second, new.astype(bf))):
            news[4 * part + k][...] = value
            c = pltpu.make_async_copy(news[4 * part + k], outs[4 * part + k], out_sem.at[4 * part + k])
            c.start()
            stores.append(c)
    for c in stores:
        c.wait()


IN_ALL = ("img", "steps", "labels", "valid", "nidx", "table", "pa", "pb")


def comm_scratch(chips):
    return dict(
        w=((chips, 2, PIECE, C), bf), flat=((184, 128), f32), piece=((2, PIECE, 128), f32),
        ga=((2, A_ROWS + 16, 128), f32), gb=((2, B_ROWS + 16, 128), f32), loss=((1, C), f32),
        r1=((chips, PIECE, C), bf), r2=((4, 2, PIECE, C), bf), r3=((4, PIECE, C), bf), r4=((4, 2, PIECE, C), bf),
        t2=((4, 2, PIECE, C), bf), t3=((4, PIECE, C), bf), t4=((4, PIECE, C), bf),
        n1_in=((chips, 8, C), f32), n1_out=((8, C), f32),
        half=((2, 2, PIECE, 128), f32), flat_a=((808, 128), f32), flat_b=((168, 128), f32), msg=((2, 8, 128), f32), news=((chips, 2, 8, 128), f32))


def sem_counts(chips):
    return dict(zsem=3, ssem=4, tsem=8, csem=16, gcsem=5, gtsem=5, gssem=5, gzsem=16, n1sem=chips, hsem=1, nsem=chips - 1)


def whole_kernel(chips, *refs):
    R = Refs()
    refs = list(refs)
    for name in IN_ALL:
        setattr(R, name, refs.pop(0))
    R.out_a, R.out_b, R.scalars = refs.pop(0), refs.pop(0), refs.pop(0)
    for name in list(SCRATCH) + list(comm_scratch(chips)):
        setattr(R, name, refs.pop(0))
    for name in sem_counts(chips):
        setattr(R, name, (refs.pop(0), refs.pop(0)))
    R.osem = refs.pop(0)
    place = Place(chips)
    barrier = greet(R, place, chips)
    own_piece(R, place)
    pl.semaphore_wait(barrier, chips)
    gather_weights(R, place, lambda: first_setup(R))
    count = spread_rows(R, chips) * POS
    R.scalars[...] = jnp.zeros((8, 128), f32)
    R.scalars[1:2, :] = count
    unpack_weights(R, R.ga, R.gb)
    time_forward(R)
    R.scale_row[...] = 2.0 / jnp.concatenate([count, count], axis=1)
    for step in FORWARD:
        step(R)
    backward_and_reduce(R, place, chips)
    finish(R, place, chips)


def whole_step(chips, images, timesteps, labels, valid_slot, noise_idx, noise_table,
               params_a, params_b, first_a, second_a, first_b, second_b):
    smem = pl.BlockSpec(memory_space=pltpu.SMEM)
    vmem = pl.BlockSpec(memory_space=pltpu.VMEM)
    hbm = pl.BlockSpec(memory_space=pl.ANY)
    rows = lambda v: v.reshape(-1, 128)
    scratch = [pltpu.VMEM(s, d) for s, d in SCRATCH.values()] + [pltpu.VMEM(s, d) for s, d in comm_scratch(chips).values()]
    for n in sem_counts(chips).values():
        scratch += [pltpu.SemaphoreType.DMA((n,)), pltpu.SemaphoreType.DMA((n,))]
    scratch.append(pltpu.SemaphoreType.DMA((2,)))
    pa, pb = rows(params_a), rows(params_b)
    grad_a, grad_b, scalars = pl.pallas_call(
        functools.partial(whole_kernel, chips),
        out_shape=[jax.ShapeDtypeStruct((n, 128), f32) for n in (808, 168, 8)],
        in_specs=[vmem, smem, smem, smem] + [vmem] * 4,
        out_specs=[hbm, hbm, vmem],
        scratch_shapes=scratch,
        compiler_params=pltpu.CompilerParams(
            collective_id=0, has_side_effects=True, vmem_limit_bytes=63 * 1024 * 1024),
    )(images, timesteps, labels, valid_slot, noise_idx, noise_table, pa, pb)
    shapes = [jax.ShapeDtypeStruct((n, 128), d) for n in (804, 161) for d in (f32, f32, f32, bf)]
    buffers = [pltpu.VMEM((n + extra, 128), f32) for n, pad in ((804, 4), (161, 7)) for extra in (pad, 0, 0, 0)]
    outs = pl.pallas_call(
        update_kernel,
        out_shape=shapes + [jax.ShapeDtypeStruct((1,), f32)] * 3,
        in_specs=[hbm] * 8 + [vmem],
        out_specs=[hbm] * 8 + [smem] * 3,
        scratch_shapes=buffers + [pltpu.VMEM(s.shape, s.dtype) for s in shapes] + [pltpu.SemaphoreType.DMA((8,))] * 2,
        compiler_params=pltpu.CompilerParams(vmem_limit_bytes=63 * 1024 * 1024),
    )(grad_a, pa, rows(first_a), rows(second_a), grad_b, pb, rows(first_b), rows(second_b), scalars)
    return (*(v.reshape(-1) for v in outs[:8]), *(v.reshape(()) for v in outs[8:]))


def adam_update(master, grad_in, first_mom, second, clip_scale):
    clipped = grad_in * clip_scale
    first_new = beta_one * first_mom + (1.0 - beta_one) * clipped
    second_new = beta_two * second + (1.0 - beta_two) * clipped * clipped
    first_hat = first_new / (1.0 - beta_one**STEP)
    second_hat = second_new / (1.0 - beta_two**STEP)
    master_new = master - learn_rate * (
        first_hat / (jnp.sqrt(second_hat) + adam_eps) + decay_rate * master
    )
    return (master_new, first_new, second_new)


def plain_step(images, timesteps, labels, valid_slot, noise_idx, noise_table,
               params_a, params_b, first_a, second_a, first_b, second_b):
    gather = lambda v: lax.all_gather(v.astype(bf), "fsdp", axis=0, tiled=True).reshape(-1, C)
    count = lax.psum(jnp.sum(valid_slot).astype(f32) * POS, ("dp", "fsdp"))
    ga, gb, loss = compute(images, timesteps, labels, valid_slot, (2.0 / count).reshape(1), noise_idx, noise_table,
                           gather(params_a), gather(params_b))
    flat = lambda g: jnp.concatenate([g[0], g[1]], axis=1).reshape(-1)
    shard = lambda g: lax.psum_scatter(flat(g), "fsdp", scatter_dimension=0, tiled=True)
    part_a, part_b, loss = lax.psum((shard(ga), shard(gb), jnp.sum(loss)), "dp")
    loss, squares = lax.psum((loss, jnp.sum(part_a * part_a) + jnp.sum(part_b * part_b)), "fsdp")
    norm = jnp.sqrt(squares)
    clip = jnp.minimum(1.0, clip_level / (norm + 1e-06))
    new_a = adam_update(params_a, part_a, first_a, second_a, clip)
    new_b = adam_update(params_b, part_b, first_b, second_b, clip)
    return (*new_a, new_a[0].astype(bf), *new_b, new_b[0].astype(bf), loss, count, norm)


def solution(mesh):
    chips = mesh.shape["fsdp"]
    if chips == 16 and mesh.shape["dp"] == 2:
        step = functools.partial(whole_step, chips)
    else:
        step = plain_step
    both = P(("dp", "fsdp"))
    return jax.shard_map(
        step, mesh=mesh,
        in_specs=(both, both, both, both, both, P()) + (P("fsdp"),) * 6,
        out_specs=(P("fsdp"),) * 8 + (P(),) * 3,
        check_vma=False)
```

```python
import functools
import math
import jax
import jax.numpy as jnp
import numpy as np
from jax import lax
from jax.experimental import pallas as pl
from jax.experimental.pallas import tpu as pltpu
from jax.sharding import PartitionSpec as P

C = 256
SIDE = 16
POS = 256
TE = 512
SIN = 128
NCLS = 10
NT = 256
NIMG = 8
bf = jnp.bfloat16
f32 = jnp.float32
eps_norm = 1e-05
CH = 64
TY = 2
U = dict(conv=8, cback=8, triple=8, attn=8, head=8, aback=8, dx3=8, chunk=8, setup=8)

A_N1, A_K1, A_B1, A_W1, A_TB1, A_W2, A_TB2, A_CT, A_PT, A_PB, A_N2, A_K2, A_B2 = (
    0, 2, 2306, 2307, 2563, 2565, 3589, 3591, 3611, 4123, 4124, 4126, 6430)
A_ROWS = 6432
B_N3, B_W, B_QV, B_WO, B_BO, B_N4, B_WH, B_BH = (0, 2, 770, 772, 1028, 1029, 1031, 1287)
B_ROWS = 1288


def dot(a, b):
    return jnp.dot(a, b, preferred_element_type=f32)


def dot_nt(a, b):
    return lax.dot_general(a, b, (((1,), (1,)), ((), ())), preferred_element_type=f32)


def dot_tn(a, b):
    return lax.dot_general(a, b, (((0,), (0,)), ((), ())), preferred_element_type=f32)


def split3(x):
    hi = x.astype(bf).astype(f32)
    rest = x - hi
    mid = rest.astype(bf).astype(f32)
    return hi, mid, rest - mid


def wide_dot(x, w, nt=False):
    n = x.shape[0]
    stacked = jnp.concatenate(split3(x), axis=0).astype(bf)
    out = dot_nt(stacked, w) if nt else dot(stacked, w)
    return out[:n] + out[n:2 * n] + out[2 * n:]


def outer_sum(a, b):
    a0, a1, _ = split3(a)
    b0, b1, _ = split3(b)
    return dot_tn(jnp.concatenate([a0, a0, a1], axis=0).astype(bf),
                  jnp.concatenate([b0, b1, b0], axis=0).astype(bf))


def sigm(v):
    return 0.5 * jnp.tanh(0.5 * v) + 0.5


def rowsum(x):
    return jnp.sum(x, axis=0, keepdims=True)


def put_shifts(buf, i, r0, x):
    n = x.shape[0]
    col = lax.broadcasted_iota(jnp.int32, x.shape, 0) & 15
    left = jnp.where(col == 0, 0.0, pltpu.roll(x, 1, 0))
    right = jnp.where(col == 15, 0.0, pltpu.roll(x, n - 1, 0))
    y = n // 16
    for s, v in enumerate((left, x, right)):
        buf[pl.ds(1 + r0 // 16, y), i, :, 256 * s:256 * s + 256] = v.astype(bf).reshape(y, 16, C)


def conv_mm(buf, kmat, y, nt=False):
    ty = TY
    parts = [buf[pl.ds(y + r, ty)].reshape(ty * 128, 3 * C) for r in range(3)]
    rows = jnp.concatenate(parts, axis=1)
    return dot_nt(rows, kmat[...]) if nt else dot(rows, kmat[...])


class Refs:
    pass


def ld(f, row, n, stride=1):
    at = pl.ds(row, n, stride=stride) if stride > 1 else pl.ds(row, n)
    return jnp.concatenate([f[0, at, :], f[1, at, :]], axis=1)


def st(f, row, value, stride=1):
    n = value.shape[0]
    at = pl.ds(row, n, stride=stride) if stride > 1 else pl.ds(row, n)
    f[0, at, :] = value[:, :128]
    f[1, at, :] = value[:, 128:]


def unpack_kernel(kmat, kt, fa, base):
    for t in range(9):
        w = ld(fa, base + 256 * t, 256)
        kmat[256 * t:256 * t + 256, :] = w.astype(bf)
        kt[:, 256 * (8 - t):256 * (8 - t) + 256] = w.astype(bf)


def unpack_norm_one(R, fa):
    R.vec[0:2, :] = ld(fa, A_N1, 2)


def unpack_time(R, fa):
    for h in range(2):
        R.tw1[:, 256 * h:256 * h + 256] = ld(fa, A_W1 + h, SIN, 2).astype(bf)
        R.tw2[:, 256 * h:256 * h + 256] = ld(fa, A_W2 + h, TE, 2).astype(bf)
    R.pt[...] = ld(fa, A_PT, TE).astype(bf)
    for k, row in enumerate((A_B1, A_TB1, A_TB1 + 1, A_TB2, A_TB2 + 1, A_PB, A_N2, A_N2 + 1)):
        R.vec[2 + k:3 + k, :] = ld(fa, row, 1)
    R.ct[0:20, :] = ld(fa, A_CT, 20)


def unpack_second_kernel(R, fa):
    unpack_kernel(R.k2, R.k2t, fa, A_K2)
    R.vec[10:11, :] = ld(fa, A_B2, 1)


def unpack_b(R, fb):
    for h in range(3):
        w = ld(fb, B_W + h, C, 3)
        R.wt[:, 256 * h:256 * h + 256] = w.astype(bf)
        R.wtt[256 * h:256 * h + 256, :] = w.T.astype(bf)
    for base, mat, turned in ((B_WO, R.wo, R.wot), (B_WH, R.wh, R.wht)):
        w = ld(fb, base, C)
        mat[...] = w.astype(bf)
        turned[...] = w.T.astype(bf)
    for k, row in enumerate((B_N3, B_N3 + 1, B_QV, B_QV + 1, B_BO, B_N4, B_N4 + 1, B_BH)):
        R.vec[11 + k:12 + k, :] = ld(fb, row, 1)


def unpack_weights(R, fa, fb):
    unpack_norm_one(R, fa)
    unpack_kernel(R.k1, R.k1t, fa, A_K1)
    unpack_time(R, fa)
    unpack_second_kernel(R, fa)
    unpack_b(R, fb)


(V_G1, V_C1, V_B1, V_TB1, V_TB1B, V_TB2, V_TB2B, V_PB, V_G2, V_C2, V_B2,
 V_G3, V_C3, V_QB, V_VB, V_BO, V_G4, V_C4, V_BH) = range(19)


def vec(R, k):
    return R.vec[k:k + 1, :]


def group_mean(R, s):
    return wide_dot(s, R.gm[...])


def stats(R, k, load, add=None):
    for i in range(NIMG):
        R.tmp[i:i + 1, :] = rowsum(load(i))
    mean = group_mean(R, R.tmp[0:8, :]) if add is None else group_mean(R, R.tmp[0:8, :] + POS * add) - add
    R.mean[k] = mean
    for i in range(NIMG):
        x = load(i) - mean[i:i + 1, :]
        R.tmp[i:i + 1, :] = rowsum(x * x)
    R.inv[k] = lax.rsqrt(group_mean(R, R.tmp[0:8, :]) + eps_norm)


def norm_sums(R, k, gain):
    s1, s2 = R.s1[...], R.s2[...]
    m = group_mean(R, jnp.concatenate([s1 * gain, s2 * gain], axis=0))
    R.m1[...] = m[:8] * R.inv[k]
    R.m2[...] = m[8:] * R.inv[k]
    return rowsum(s2), rowsum(s1)


def first_setup(R):
    row = lax.broadcasted_iota(jnp.int32, (C, C), 0) >> 3
    col = lax.broadcasted_iota(jnp.int32, (C, C), 1) >> 3
    R.gm[...] = jnp.where(row == col, 1.0 / 2048.0, 0.0).astype(bf)
    zero = jnp.zeros((1, NIMG, 16, 3 * C), bf)
    for buf in (R.buf1, R.buf2, R.dbuf):
        buf[0:1] = zero
        buf[17:18] = zero
    hi, mid, lo = split3(R.table[...])
    R.tab3[...] = jnp.concatenate([hi, mid, lo], axis=1).astype(bf)

    @pl.loop(0, NIMG, unroll=U["setup"])
    def _(i):
        rows = lax.broadcasted_iota(jnp.int32, (NT, POS), 0)
        hot = jnp.where(rows == R.nidx[pl.ds(i, 1), :], 1.0, 0.0)
        out = dot(hot.T.astype(bf), R.tab3[...])
        R.target[i] = out[:, :C] + out[:, C:2 * C] + out[:, 2 * C:]
    stats(R, 0, lambda i: R.img[i].astype(f32))


def column_of(smem, shape):
    row = lax.broadcasted_iota(jnp.int32, shape, 0)
    out = jnp.zeros(shape, jnp.int32)
    for i in range(NIMG):
        out = jnp.where(row == i, smem[i], out)
    return out


def time_forward(R):
    lane = lax.broadcasted_iota(jnp.int32, (NIMG, SIN), 1)
    factor = math.log(10000.0) / (SIN // 2 - 1)
    freq = jnp.exp((lane & 63).astype(f32) * -factor)
    angle = column_of(R.steps, (NIMG, SIN)).astype(f32) * freq
    e = jnp.where(lane < 64, jnp.sin(angle), jnp.cos(angle))
    R.emb[...] = e
    u = wide_dot(e, R.tw1[...]) + jnp.concatenate([vec(R, V_TB1), vec(R, V_TB1B)], axis=1)
    R.pre[...] = u
    lab = column_of(R.labels, (NIMG, TE))
    te = wide_dot(u * sigm(u), R.tw2[...]) + jnp.concatenate([vec(R, V_TB2), vec(R, V_TB2B)], axis=1)
    for j in range(NCLS):
        row = jnp.concatenate([R.ct[2 * j:2 * j + 1, :], R.ct[2 * j + 1:2 * j + 2, :]], axis=1)
        te = te + jnp.where(lab == j, row, 0.0)
    R.te[...] = te
    add = wide_dot(te * sigm(te), R.pt[...]) + vec(R, V_PB) + vec(R, V_B1)
    R.add[...] = add


def each_chunk(fn):
    @pl.loop(0, NIMG, unroll=U["chunk"])
    def _(i):
        for c in range(POS // CH):
            fn(i, c * CH)


def normed(R, k, i, x):
    return (x - R.mean[k, pl.ds(i, 1), :]) * R.inv[k, pl.ds(i, 1), :]


def step_x1(R):
    def one(i, r0):
        x = normed(R, 0, i, R.img[i, r0:r0 + CH, :].astype(f32))
        a = x * vec(R, V_G1) + vec(R, V_C1)
        put_shifts(R.buf1, i, r0, a * sigm(a))
    each_chunk(one)


def conv_one(R, lo, hi):
    @pl.loop(lo, hi, unroll=hi - lo)
    def _(t):
        acc = conv_mm(R.buf1, R.k1, t * TY).reshape(TY, NIMG, 16, C)
        for yy in range(TY):
            R.c1[:, pl.ds(pl.multiple_of((t * TY + yy) * 16, 16), 16), :] = acc[yy]


def step_conv1(R):
    conv_one(R, 0, SIDE // TY)


def step_stats1(R):
    stats(R, 1, lambda i: R.c1[i], R.add[...])


def step_x2(R):
    def two(i, r0):
        x = normed(R, 1, i, R.c1[i, r0:r0 + CH, :])
        a = x * vec(R, V_G2) + vec(R, V_C2)
        put_shifts(R.buf2, i, r0, a * sigm(a))
    each_chunk(two)


def step_conv2(R):
    @pl.loop(0, SIDE // TY, unroll=U["conv"])
    def _(t):
        acc = conv_mm(R.buf2, R.k2, t * TY).reshape(TY, NIMG, 16, C)
        for yy in range(TY):
            at = pl.ds(pl.multiple_of((t * TY + yy) * 16, 16), 16)
            R.h1[:, at, :] = acc[yy] + R.img[:, at, :].astype(f32) + vec(R, V_B2)


def step_stats2(R):
    stats(R, 2, lambda i: R.h1[i])


def step_triple(R):
    bias = jnp.concatenate([vec(R, V_QB), jnp.zeros((1, C), f32), vec(R, V_VB)], axis=1)

    @pl.loop(0, NIMG, unroll=U["triple"])
    def _(i):
        x = (normed(R, 2, i, R.h1[i]) * vec(R, V_G3) + vec(R, V_C3)).astype(bf)
        R.x3t[:, pl.ds(pl.multiple_of(i * POS, POS), POS)] = x.T
        R.tri[i] = (dot(x, R.wt[...]) + bias).astype(bf)


def step_attn(R):
    for g in range(0, NIMG, 4):
        for i in range(g, g + 4):
            R.p[i] = dot_nt(R.tri[i, :, 0:C], R.tri[i, :, C:2 * C])
        for i in range(g, g + 4):
            for r in range(0, POS, CH):
                s = R.p[i, r:r + CH, :] * C ** (-0.5)
                e = jnp.exp(s - jnp.max(s, axis=1, keepdims=True))
                R.p[i, r:r + CH, :] = e * (1.0 / jnp.sum(e, axis=1, keepdims=True))
        for i in range(g, g + 4):
            R.o[i] = dot(R.p[i].astype(bf), R.tri[i, :, 2 * C:]).astype(bf)
        for i in range(g, g + 4):
            R.h2[i] = R.h1[i] + dot(R.o[i], R.wo[...]) + vec(R, V_BO)


def step_stats3(R):
    stats(R, 3, lambda i: R.h2[i])


def step_head(R):
    scale = R.scale_row[...]
    loss = jnp.zeros((8, C), f32)
    bias = jnp.zeros((8, C), f32)
    for g in range(0, NIMG, 4):
        for i in range(g, g + 4):
            for r in range(0, POS, CH):
                a = normed(R, 3, i, R.h2[i, r:r + CH, :]) * vec(R, V_G4) + vec(R, V_C4)
                R.low[i, r:r + CH, :] = (a * sigm(a)).astype(bf)
        for i in range(g, g + 4):
            R.da[i] = dot(R.low[i], R.wh[...])
            R.xt[:, i * POS:(i + 1) * POS] = R.low[i].T
        for i in range(g, g + 4):
            valid = R.valid[i].astype(f32)
            for r in range(0, POS, CH):
                differ = R.da[i, r:r + CH, :] + vec(R, V_BH) - R.target[i, r:r + CH, :]
                dv = valid * differ
                loss += fold(dv * differ)
                dp = dv * scale
                bias += fold(dp)
                R.low[i, r:r + CH, :] = dp.astype(bf)
        for i in range(g, g + 4):
            R.da[i] = dot(R.low[i], R.wht[...])
        for i in range(g, g + 4):
            s1 = jnp.zeros((8, C), f32)
            s2 = jnp.zeros((8, C), f32)
            for r in range(0, POS, CH):
                x = normed(R, 3, i, R.h2[i, r:r + CH, :])
                a = x * vec(R, V_G4) + vec(R, V_C4)
                sg = sigm(a)
                da = R.da[i, r:r + CH, :] * (sg * (1.0 + a * (1.0 - sg)))
                R.da[i, r:r + CH, :] = da
                s1 += fold(da)
                s2 += fold(da * x)
            R.s1[i:i + 1, :] = rowsum(s1)
            R.s2[i:i + 1, :] = rowsum(s2)
    R.loss[...] = rowsum(loss)
    R.sh[...] = rowsum(bias)


def step_head_grads(R):
    st(R.gb, B_BH, R.sh[...])
    st(R.gb, B_WH, dot(R.xt[...], R.low[...].reshape(NIMG * POS, C)))
    dg, db = norm_sums(R, 3, vec(R, V_G4))
    st(R.gb, B_N4, dg)
    st(R.gb, B_N4 + 1, db)


def step_attn_back(R):
    out_bias = jnp.zeros((8, C), f32)
    q_bias = jnp.zeros((8, C), f32)
    v_bias = jnp.zeros((8, C), f32)
    for g in range(0, NIMG, 4):
        four = range(g, g + 4)
        for i in four:
            for r in range(0, POS, CH):
                x = normed(R, 3, i, R.h2[i, r:r + CH, :])
                d = ((R.inv[3, i:i + 1, :] * vec(R, V_G4)) * R.da[i, r:r + CH, :]
                     - R.m1[i:i + 1, :] - x * R.m2[i:i + 1, :])
                R.dh[i, r:r + CH, :] = d
                out_bias += fold(d)
                R.low[i, r:r + CH, :] = d.astype(bf)
            R.xt[:, i * POS:(i + 1) * POS] = R.o[i].T
        for i in four:
            R.o[i] = dot(R.low[i], R.wot[...]).astype(bf)
        for i in four:
            R.da[i] = dot_nt(R.o[i], R.tri[i, :, 2 * C:])
            dv = dot_tn(R.p[i].astype(bf), R.o[i]).astype(bf)
            R.tri[i, :, 2 * C:] = dv
            v_bias += fold(dv.astype(f32))
        for i in four:
            for r in range(0, POS, CH):
                p = R.p[i, r:r + CH, :]
                dpr = R.da[i, r:r + CH, :]
                R.p[i, r:r + CH, :] = p * (dpr - jnp.sum(dpr * p, axis=1, keepdims=True))
        for i in four:
            ds = R.p[i].astype(bf)
            dq = (dot(ds, R.tri[i, :, C:2 * C]) * C ** (-0.5)).astype(bf)
            dk = (dot_tn(ds, R.tri[i, :, 0:C]) * C ** (-0.5)).astype(bf)
            R.tri[i, :, 0:C] = dq
            R.tri[i, :, C:2 * C] = dk
            q_bias += fold(dq.astype(f32))
    st(R.gb, B_BO, rowsum(out_bias))
    st(R.gb, B_QV, rowsum(q_bias))
    st(R.gb, B_QV + 1, rowsum(v_bias))


def step_out_grads(R):
    st(R.gb, B_WO, dot(R.xt[...], R.low[...].reshape(NIMG * POS, C)))


def step_dx3(R):
    @pl.loop(0, NIMG, unroll=U["dx3"])
    def _(i):
        da = dot(R.tri[i], R.wtt[...])
        R.da[i] = da
        R.s1[pl.ds(i, 1), :] = rowsum(da)
        R.s2[pl.ds(i, 1), :] = rowsum(da * normed(R, 2, i, R.h1[i]))


def step_triple_grads(R):
    for h in range(3):
        st(R.gb, B_W + h, dot(
            R.x3t[...], R.tri[:, :, 256 * h:256 * h + 256].reshape(NIMG * POS, C)), 3)
    dg, db = norm_sums(R, 2, vec(R, V_G3))
    st(R.gb, B_N3, dg)
    st(R.gb, B_N3 + 1, db)


def kernel_lhs(R, buf):
    @pl.loop(0, SIDE // 2, unroll=8)
    def _(t):
        x = buf[pl.ds(1 + 2 * t, 2), :, :, C:2 * C].reshape(256, C)
        R.xt[:, pl.ds(pl.multiple_of(t * 256, 256), 256)] = x.T


def kernel_taps(R, row, taps):
    for tap in taps:
        r, s = divmod(tap, 3)
        d = R.dbuf[2 - r:18 - r, :, :, 256 * (2 - s):256 * (3 - s)].reshape(NIMG * POS, C)
        st(R.ga, row + tap * 256, dot(R.xt[...], d))


def conv_back(R, kt, rows=(0, SIDE // TY)):
    @pl.loop(rows[0], rows[1], unroll=rows[1] - rows[0])
    def _(t):
        acc = conv_mm(R.dbuf, kt, t * TY, True).reshape(TY, NIMG, 16, C)
        for yy in range(TY):
            R.da[:, pl.ds(pl.multiple_of((t * TY + yy) * 16, 16), 16), :] = acc[yy]


def fold(x):
    return jnp.sum(x.reshape(x.shape[0] // 8, 8, x.shape[1]), axis=0)


def swish_back(R, k, load, vg, vc, keep):
    for i in range(NIMG):
        s1 = jnp.zeros((8, C), f32)
        s2 = jnp.zeros((8, C), f32)
        for r0 in range(0, POS, CH):
            x = normed(R, k, i, load(i, r0))
            a = x * vec(R, vg) + vec(R, vc)
            sg = sigm(a)
            da = R.da[i, r0:r0 + CH, :] * (sg * (1.0 + a * (1.0 - sg)))
            if keep:
                R.da[i, r0:r0 + CH, :] = da
            s1 += fold(da)
            s2 += fold(da * x)
        R.s1[i:i + 1, :] = rowsum(s1)
        R.s2[i:i + 1, :] = rowsum(s2)


def step_dh1(R):
    R.sums8[...] = jnp.zeros_like(R.sums8)

    def one(i, r0):
        at = slice(r0, r0 + CH)
        x = normed(R, 2, i, R.h1[i, at, :])
        d = (R.dh[i, at, :] + (R.inv[2, pl.ds(i, 1), :] * vec(R, V_G3)) * R.da[i, at, :]
             - R.m1[pl.ds(i, 1), :] - x * R.m2[pl.ds(i, 1), :])
        R.sums8[...] += fold(d)
        put_shifts(R.dbuf, i, r0, d)
    each_chunk(one)
    st(R.ga, A_B2, rowsum(R.sums8[...]))


def step_dk2(R):
    kernel_lhs(R, R.buf2)
    kernel_taps(R, A_K2, range(9))


def step_dx2_high(R):
    conv_back(R, R.k2t, (0, 4))


def step_dx2_low(R):
    conv_back(R, R.k2t, (4, 8))


def step_da2(R):
    swish_back(R, 1, lambda i, r0: R.c1[i, r0:r0 + CH, :], V_G2, V_C2, True)
    dg, db = norm_sums(R, 1, vec(R, V_G2))
    st(R.ga, A_N2, dg)
    st(R.ga, A_N2 + 1, db)


def step_dc1(R):
    R.tmp[...] = jnp.zeros_like(R.tmp)

    def two(i, r0):
        at = slice(r0, r0 + CH)
        x = normed(R, 1, i, R.c1[i, at, :])
        d = ((R.inv[1, pl.ds(i, 1), :] * vec(R, V_G2)) * R.da[i, at, :]
             - R.m1[pl.ds(i, 1), :] - x * R.m2[pl.ds(i, 1), :])
        R.tmp[pl.ds(i, 1), :] += rowsum(d)
        put_shifts(R.dbuf, i, r0, d)
    each_chunk(two)


def step_dk1_high(R):
    kernel_lhs(R, R.buf1)
    kernel_taps(R, A_K1, (6, 7, 8))


def step_dk1_mid(R):
    kernel_taps(R, A_K1, (3, 4, 5))


def step_dk1_low(R):
    kernel_taps(R, A_K1, (0, 1, 2))


def step_dx1_high(R):
    conv_back(R, R.k1t, (0, 4))


def step_dx1_low(R):
    conv_back(R, R.k1t, (4, 8))


def step_da1(R):
    swish_back(R, 0, lambda i, r0: R.img[i, r0:r0 + CH, :].astype(f32), V_G1, V_C1, False)
    R.n1[0:1, :] = rowsum(R.s2[...])
    R.n1[1:2, :] = rowsum(R.s1[...])


def swish_slope(v):
    s = sigm(v)
    return s * (1.0 + v * (1.0 - s))


def time_backward(R):
    d_add = R.tmp[0:8, :]
    total = rowsum(d_add)
    st(R.ga, A_B1, total)
    st(R.ga, A_PB, total)
    te = R.te[...]
    st(R.ga, A_PT, outer_sum(te * sigm(te), d_add))
    d_te = wide_dot(d_add, R.pt[...], nt=True) * swish_slope(te)
    lab = column_of(R.labels, (NIMG, TE))
    for j in range(NCLS):
        row = rowsum(jnp.where(lab == j, d_te, 0.0))
        for h in range(2):
            st(R.ga, A_CT + 2 * j + h, row[:, 256 * h:256 * h + 256])
    row = rowsum(d_te)
    u = R.pre[...]
    dw2 = outer_sum(u * sigm(u), d_te)
    d_u = wide_dot(d_te, R.tw2[...], nt=True) * swish_slope(u)
    row1 = rowsum(d_u)
    dw1 = outer_sum(R.emb[...], d_u)
    for h in range(2):
        st(R.ga, A_TB2 + h, row[:, 256 * h:256 * h + 256])
        st(R.ga, A_TB1 + h, row1[:, 256 * h:256 * h + 256])
        st(R.ga, A_W2 + h, dw2[:, 256 * h:256 * h + 256], 2)
        st(R.ga, A_W1 + h, dw1[:, 256 * h:256 * h + 256], 2)


FORWARD_A = (step_x1, step_conv1, step_stats1, step_x2, step_conv2, step_stats2)
FORWARD_B = (step_triple, step_attn, step_stats3, step_head, step_head_grads, step_attn_back, step_out_grads, step_dx3, step_triple_grads)
BACKWARD = (step_dh1, step_dk2, step_dx2_high, step_dx2_low, step_da2, step_dc1, time_backward, step_dk1_high, step_dk1_mid, step_dk1_low,
            step_dx1_high, step_dx1_low, step_da1)
STEPS = FORWARD_A + FORWARD_B + BACKWARD


SCRATCH = dict(
    k1=((2304, C), bf), k1t=((C, 2304), bf), k2=((2304, C), bf), k2t=((C, 2304), bf),
    tw1=((SIN, TE), bf), tw2=((TE, TE), bf), pt=((TE, C), bf),
    wt=((C, 3 * C), bf), wtt=((3 * C, C), bf), wo=((C, C), bf), wot=((C, C), bf), wh=((C, C), bf), wht=((C, C), bf),
    vec=((24, C), f32), ct=((24, C), f32),
    gm=((C, C), bf), tab3=((NT, 3 * C), bf), target=((NIMG, POS, C), f32),
    tmp=((8, C), f32), mean=((4, 8, C), f32), inv=((4, 8, C), f32),
    s1=((8, C), f32), s2=((8, C), f32), m1=((8, C), f32), m2=((8, C), f32),
    sh=((1, C), f32), sums8=((8, C), f32), scale_row=((1, C), f32), n1=((8, C), f32), sq=((1, 2 * C), f32),
    emb=((8, SIN), f32), pre=((8, TE), f32), te=((8, TE), f32), add=((8, C), f32),
    buf1=((18, 8, 16, 3 * C), bf), buf2=((18, 8, 16, 3 * C), bf), dbuf=((18, 8, 16, 3 * C), bf),
    c1=((8, POS, C), f32), h1=((8, POS, C), f32), h2=((8, POS, C), f32), da=((8, POS, C), f32), dh=((8, POS, C), f32),
    p=((8, POS, POS), f32), o=((8, POS, C), bf), low=((8, POS, C), bf),
    tri=((8, POS, 3 * C), bf),
    x3t=((C, 8 * POS), bf), xt=((C, 8 * POS), bf),
)


def main_kernel(names_in, *refs):
    R = Refs()
    n_in = len(names_in)
    for name, r in zip(names_in, refs):
        setattr(R, name, r)
    R.ga, R.gb, R.loss = refs[n_in:n_in + 3]
    for name, r in zip(list(SCRATCH), refs[n_in + 3:]):
        setattr(R, name, r)
    fa, fb = R.ga, R.gb
    for c in range(0, A_ROWS, 402):
        st(fa, c, R.wa[c:c + 402, :].astype(f32))
    st(fb, 0, R.wb[...].astype(f32))
    R.scale_row[...] = jnp.full((1, C), R.scale[0])
    first_setup(R)
    unpack_weights(R, fa, fb)
    time_forward(R)
    for step in STEPS:
        step(R)
    st(R.ga, A_N1, R.n1[0:2, :])
    st(R.ga, A_ROWS - 1, jnp.zeros((1, C), f32))


def compute(img, steps, labels, valid, scale, nidx, table, wa, wb):
    smem = pl.BlockSpec(memory_space=pltpu.SMEM)
    vmem = pl.BlockSpec(memory_space=pltpu.VMEM)
    names = ("img", "steps", "labels", "valid", "scale", "nidx", "table", "wa", "wb")
    return pl.pallas_call(
        functools.partial(main_kernel, names),
        out_shape=(jax.ShapeDtypeStruct((2, A_ROWS, 128), f32), jax.ShapeDtypeStruct((2, B_ROWS, 128), f32),
                   jax.ShapeDtypeStruct((1, C), f32)),
        in_specs=[vmem, smem, smem, smem, smem, vmem, vmem, vmem, vmem],
        out_specs=(vmem, vmem, vmem),
        scratch_shapes=[pltpu.VMEM(s, d) for s, d in SCRATCH.values()],
        compiler_params=pltpu.CompilerParams(vmem_limit_bytes=63 * 1024 * 1024),
    )(img, steps, labels, valid, scale, nidx, table, wa, wb)


beta_one = 0.5
beta_two = 0.5
learn_rate = 0.1
decay_rate = 0.01
adam_eps = 1e-08
clip_level = 0.01
STEP = 5
PA = A_ROWS * C
PB = B_ROWS * C
MESH = pl.DeviceIdType.MESH
ORDER = (0, 1, 3, 2)
HALF_A, HALF_B, PIECE = 201, 48, 256
B_AT = 208


class Place:
    def __init__(self, chips):
        self.me = lax.axis_index("fsdp")
        self.core = lax.axis_index("dp")
        self.depth = chips // 4

    def z(self, k, d):
        return lax.rem(lax.div(k, 4) + d + self.depth, self.depth) * 4 + lax.rem(k, 4)

    def flip_x(self, k):
        return k + 1 - 2 * lax.rem(k, 2)

    def flip_y(self, k):
        return k + 2 - 4 * lax.rem(lax.div(k, 2), 2)

    def s(self, k):
        return self.core * self.flip_x(k) + (1 - self.core) * self.flip_y(k)

    def t(self, k):
        return self.core * self.flip_y(k) + (1 - self.core) * self.flip_x(k)

    def pieces(self):
        line = [self.z(self.me, -j) for j in range(4)]
        near = line + [self.s(k) for k in line]
        return near + [self.t(k) for k in near]


def send(src, dst, sems, at, core, chip):
    copy = pltpu.make_async_remote_copy(
        src_ref=src, dst_ref=dst, send_sem=sems[0].at[at], recv_sem=sems[1].at[at],
        device_id=(core, chip), device_id_type=MESH)
    copy.start()
    return copy


def greet(R, place, chips):
    barrier = pltpu.get_barrier_semaphore()
    for d in range(1, chips):
        pl.semaphore_signal(barrier, inc=1, device_id=(place.core, lax.rem(place.me + d, chips)), device_id_type=MESH)
    pl.semaphore_signal(barrier, inc=1, device_id=(1 - place.core, place.me), device_id_type=MESH)
    return barrier


def own_piece(R, place):
    count = R.valid[0]
    for i in range(1, NIMG):
        count = count + R.valid[i]
    count = count.astype(f32)
    odd = lax.rem(place.me, 2) == 1
    R.flat[0:8, :] = jnp.zeros((8, 128), f32)
    R.flat[168:184, :] = jnp.zeros((16, 128), f32)
    R.flat[8:169, :] = R.pb[...]
    for h in range(2):
        for lane in range(2):
            R.piece[lane, 0:201, :] = R.pa[pl.ds(402 * h + lane, 201, stride=2), :]
            even_rows = R.flat[pl.ds(8 + lane + 96 * h, 48 - 8 * h, stride=2), :]
            odd_rows = R.flat[pl.ds(7 + lane + 96 * h, 48 - 8 * h, stride=2), :]
            R.piece[lane, 208:256 - 8 * h, :] = jnp.where(odd, odd_rows, even_rows)
        R.piece[:, 201:208, :] = jnp.full((2, 7, 128), count)

        @pl.when(place.core == h)
        def _():
            R.w[place.me, h] = jnp.concatenate([R.piece[0], R.piece[1]], axis=1).astype(bf)


def gather_weights(R, place, meanwhile):
    me, core = place.me, place.core
    got = place.pieces()
    put = lambda k: R.w.at[k, core]
    over_s, over_t = place.s(me), place.t(me)
    zc = {d: send(put(me), put(me), R.zsem, d - 1, core, place.z(me, d)) for d in (1, 3, 2)}
    sc, tc, sib = {}, {}, {}
    for j in ORDER:
        if j == 1:
            meanwhile()
        if j:
            zc[j].wait_recv()
        sc[j] = send(put(got[j]), put(got[j]), R.ssem, j, core, over_s)
        tc[j] = send(put(got[j]), put(got[j]), R.tsem, j, core, over_t)
        sib[j] = send(put(got[j]), put(got[j]), R.csem, j, 1 - core, me)
    for j in ORDER:
        sc[j].wait_recv()
        q = 4 + j
        tc[q] = send(put(got[q]), put(got[q]), R.tsem, q, core, over_t)
        sib[q] = send(put(got[q]), put(got[q]), R.csem, q, 1 - core, me)
    for half in (0, 4):
        for j in ORDER:
            q = half + j
            tc[q].wait_recv()
            sib[8 + q] = send(put(got[8 + q]), put(got[8 + q]), R.csem, 8 + q, 1 - core, me)
    for c in sib.values():
        c.wait_recv()
    for group in (zc, sc, tc, sib):
        for c in group.values():
            c.wait_send()


def spread_rows(R, chips):
    count = jnp.zeros((1, 128), f32)
    for k in range(chips):
        base = (161 * k) // 2
        odd = k % 2
        for h in range(2):
            a = R.w[k, h, 0:208, :].astype(f32)
            row = 402 * k + 201 * h
            R.ga[0, row:row + 208, :] = a[:, :128]
            R.ga[1, row:row + 208, :] = a[:, 128:]
            count = count + a[201:202, :128]
            b = R.w[k, h, 208:256, :].astype(f32)
            if h == 0:
                R.gb[0, base + odd:base + 48, :] = b[odd:, :128]
                R.gb[1, base:base + 48, :] = b[:, 128:]
            else:
                R.gb[0, base + 48:base + 81, :] = b[:33, :128]
                R.gb[1, base + 48:base + 80 + odd, :] = b[:32 + odd, 128:]
    return count


def pack_a(R, zt):
    for k in range(4 * zt, 4 * zt + 4):
        for h in range(2):
            R.w[k, h, 0:B_AT, :] = ld(R.ga, 402 * k + 201 * h, B_AT).astype(bf)


def pack_b(R, chips):
    for k in range(chips):
        base = (161 * k) // 2
        for h in range(2):
            R.w[k, h, B_AT:PIECE, :] = ld(R.gb, base + HALF_B * h, HALF_B).astype(bf)


def late(src, dst, send_sem, recv_sem, core, chip):
    return pltpu.make_async_remote_copy(src_ref=src, dst_ref=dst, send_sem=send_sem, recv_sem=recv_sem,
                                        device_id=(core, chip), device_id_type=MESH)


class Reduction:
    def __init__(self, R, place, at):
        self.R, self.place, self.at = R, place, at
        self.planes = (at,) if at < 4 else range(4)
        self.rows = pl.ds(0, B_AT) if at < 4 else pl.ds(B_AT, HALF_B)
        me, core, rows = place.me, place.core, self.rows
        self.mine = lax.rem(me, 4)
        self.z = lax.div(me, 4)
        group = pl.ds(4 * at, 4) if at < 4 else pl.ds(0, 16)
        plane = pl.ds(at, 1) if at < 4 else pl.ds(0, 4)
        sems = lambda pair: (pair[0].at[at], pair[1].at[at])
        self.across_core = late(R.w.at[group, 1 - core, rows], R.r1.at[group, rows], *sems(R.gcsem), 1 - core, me)
        self.across_t = late(R.t2.at[plane, :, rows], R.r2.at[plane, :, rows], *sems(R.gtsem), core, place.t(me))
        self.across_s = late(R.t3.at[plane, rows], R.r3.at[plane, rows], *sems(R.gssem), core, place.s(me))
        self.along = {}
        for zt in self.planes:
            far, mid, near = (3, 2, 1 - zt) if zt < 2 else (0, 1, 5 - zt)
            base = 2 * (zt if at < 4 else 4 + zt)
            go = lambda slot, to: late(R.t4.at[zt, rows], R.r4.at[zt, slot, rows], R.gzsem[0].at[base + slot],
                                       R.gzsem[1].at[base + slot], core, 4 * to + self.mine)
            self.along[zt] = (far, mid, near, go(1, mid), go(1, zt), go(0, zt))

    def both_cores(self, k):
        R = self.R
        return R.w[k, self.place.core, self.rows].astype(f32) + R.r1[k, self.rows].astype(f32)

    def start(self):
        self.across_core.start()

    def step_t(self):
        R, place = self.R, self.place
        self.across_core.wait_recv()
        for zt in self.planes:
            k = place.t(4 * zt + self.mine)
            R.t2[zt, 0, self.rows] = self.both_cores(place.s(k)).astype(bf)
            R.t2[zt, 1, self.rows] = self.both_cores(k).astype(bf)
        self.across_t.start()

    def step_s(self):
        R = self.R
        self.across_t.wait_recv()
        for zt in self.planes:
            k = self.place.s(4 * zt + self.mine)
            R.t3[zt, self.rows] = (self.both_cores(k) + R.r2[zt, 0, self.rows].astype(f32)).astype(bf)
        self.across_s.start()

    def step_z(self):
        R = self.R
        self.across_s.wait_recv()
        for zt in self.planes:
            far, mid, near, to_mid, mid_on, near_on = self.along[zt]
            total = (self.both_cores(4 * zt + self.mine) + R.r2[zt, 1, self.rows].astype(f32)
                     + R.r3[zt, self.rows].astype(f32))

            @pl.when(self.z == zt)
            def _():
                R.half[self.place.core, 0, self.rows] = total[:, :128]
                R.half[self.place.core, 1, self.rows] = total[:, 128:]

            @pl.when(self.z != zt)
            def _():
                R.t4[zt, self.rows] = total.astype(bf)

            @pl.when(self.z == far)
            def _():
                to_mid.start()

            @pl.when(self.z == near)
            def _():
                near_on.start()

    def step_mid(self):
        R = self.R
        for zt in self.planes:
            far, mid, near, to_mid, mid_on, near_on = self.along[zt]

            @pl.when(self.z == mid)
            def _():
                to_mid.wait_recv()
                R.t4[zt, self.rows] = (R.t4[zt, self.rows].astype(f32) + R.r4[zt, 1, self.rows].astype(f32)).astype(bf)
                mid_on.start()

    def step_end(self):
        R, core = self.R, self.place.core
        for zt in self.planes:
            far, mid, near, to_mid, mid_on, near_on = self.along[zt]

            @pl.when(self.z == zt)
            def _():
                near_on.wait_recv()
                mid_on.wait_recv()
                more = R.r4[zt, 0, self.rows].astype(f32) + R.r4[zt, 1, self.rows].astype(f32)
                R.half[core, 0, self.rows] += more[:, :128]
                R.half[core, 1, self.rows] += more[:, 128:]

    def drain(self):
        for c in (self.across_core, self.across_t, self.across_s):
            c.wait_send()
        for zt in self.planes:
            far, mid, near, to_mid, mid_on, near_on = self.along[zt]

            @pl.when(self.z == far)
            def _():
                to_mid.wait_send()

            @pl.when(self.z == mid)
            def _():
                mid_on.wait_send()

            @pl.when(self.z == near)
            def _():
                near_on.wait_send()


class NormOne:
    def __init__(self, R, place, chips):
        self.R, self.me, self.core, self.chips = R, place.me, place.core, chips
        self.cross = late(R.n1, R.n1_in.at[0], R.n1sem[0].at[0], R.n1sem[1].at[0], 1 - place.core, place.me)
        self.home = [late(R.n1_out, R.n1_in.at[d], R.n1sem[0].at[d], R.n1sem[1].at[d], place.core,
                          lax.rem(place.me + chips - d, chips)) for d in range(1, chips)]

    def start(self):
        @pl.when(self.core == 1)
        def _():
            self.cross.start()

    def to_home(self):
        R = self.R

        @pl.when(self.core == 0)
        def _():
            self.cross.wait_recv()
            R.n1_out[...] = R.n1[...] + R.n1_in[0]
        for d in range(1, self.chips):
            @pl.when(jnp.logical_and(self.core == 0, self.me == d))
            def _():
                self.home[d - 1].start()

    def end(self):
        R = self.R

        @pl.when(jnp.logical_and(self.core == 0, self.me == 0))
        def _():
            total = R.n1_out[...]
            for d in range(1, self.chips):
                self.home[d - 1].wait_recv()
                total = total + R.n1_in[d]
            R.half[0, 0, 0:2, :] = total[0:2, :128]
            R.half[0, 1, 0:2, :] = total[0:2, 128:]

    def drain(self):
        @pl.when(self.core == 1)
        def _():
            self.cross.wait_send()
        for d in range(1, self.chips):
            @pl.when(jnp.logical_and(self.core == 0, self.me == d))
            def _():
                self.home[d - 1].wait_send()


def backward_and_reduce(R, place, chips):
    r0, r1, r2, r3, rb = (Reduction(R, place, at) for at in range(5))
    n1 = NormOne(R, place, chips)
    R.n1[...] = jnp.zeros((8, C), f32)
    st(R.ga, A_N1, jnp.zeros((2, C), f32))
    st(R.ga, A_ROWS - 1, jnp.zeros((1, C), f32))
    pack_b(R, chips)
    rb.start()
    step_dh1(R)
    rb.step_t()
    step_dk2(R)
    pack_a(R, 3)
    r3.start()
    rb.step_s()
    step_dx2_high(R)
    r3.step_t()
    step_dx2_low(R)
    step_da2(R)
    rb.step_z()
    step_dc1(R)
    r3.step_s()
    time_backward(R)
    pack_a(R, 2)
    r2.start()
    rb.step_mid()
    step_dk1_high(R)
    pack_a(R, 1)
    r1.start()
    r2.step_t()
    step_dk1_mid(R)
    step_dk1_low(R)
    r3.step_z()
    pack_a(R, 0)
    r0.start()
    r1.step_t()
    r0.step_t()
    step_dx1_high(R)
    step_dx1_low(R)
    r2.step_s()
    r1.step_s()
    r0.step_s()
    step_da1(R)
    n1.start()
    r3.step_mid()
    r2.step_z()
    r1.step_z()
    r0.step_z()
    n1.to_home()
    r2.step_mid()
    r1.step_mid()
    r0.step_mid()
    rb.step_end()
    r3.step_end()
    r2.step_end()
    r1.step_end()
    r0.step_end()
    n1.end()
    for c in (rb, r3, r2, r1, r0, n1):
        c.drain()


def finish(R, place, chips):
    me, core = place.me, place.core
    loss = jnp.sum(R.loss[...], axis=1, keepdims=True)
    R.half[core, :, 201:208, :] = jnp.broadcast_to(loss, (2, 7, 128))
    both = send(R.half.at[core], R.half.at[core], R.hsem, 0, 1 - core, me)
    both.wait_recv()
    odd = lax.rem(me, 2)
    row = lax.broadcasted_iota(jnp.int32, (256, 128), 0)
    squares = jnp.zeros((1, 128), f32)
    for h in range(2):
        for lane in range(2):
            g = R.half[h, lane]
            keep = row < 201
            if h == 0:
                b_in = row >= 208 + (odd if lane == 0 else 0)
            else:
                b_in = jnp.logical_and(row >= 208, row < 208 + (33 if lane == 0 else 32 + odd))
            g = jnp.where(jnp.logical_or(keep, b_in), g, 0.0)
            squares = squares + rowsum(g * g)
    R.msg[0] = jnp.broadcast_to(jnp.sum(squares, axis=1, keepdims=True), (8, 128))
    R.msg[1] = R.half[0, 0, 200:208, :] + R.half[1, 0, 200:208, :]
    R.news[0] = R.msg[...]
    sent = []
    for d in range(1, chips):
        sent.append(send(R.msg, R.news.at[d], R.nsem, d - 1, core, lax.rem(me + d, chips)))
    for lane in range(2):
        for h in range(2):
            R.flat_a[pl.ds(402 * h + lane, 201, stride=2), :] = R.half[h, lane, 0:201, :]
            R.flat[pl.ds(8 + 96 * h + lane, 48 - 8 * h, stride=2), :] = R.half[h, lane, 208:256 - 8 * h, :]
    grad_b = jnp.where(odd == 1, R.flat[9:170, :], R.flat[8:169, :])
    R.flat_b[0:161, :] = jnp.where(odd == 1, R.flat[9:170, :], R.flat[8:169, :])
    outs = [pltpu.make_async_copy(R.flat_a, R.out_a, R.osem.at[0]), pltpu.make_async_copy(R.flat_b, R.out_b, R.osem.at[1])]
    for c in outs:
        c.start()
    for c in sent:
        c.wait_recv()
    total = R.news[0]
    for d in range(1, chips):
        total = total + R.news[d]
    norm = jnp.sqrt(total[0, 0:1, :])
    R.scalars[0:1, :] = total[1, 7:8, :]
    R.scalars[2:3, :] = norm
    for c in sent:
        c.wait_send()
    both.wait_send()
    for c in outs:
        c.wait()


def update_kernel(*refs):
    ins, scalars, outs, refs = refs[:8], refs[8], refs[9:20], refs[20:]
    bufs, news, in_sem, out_sem = refs[:8], refs[8:16], refs[16], refs[17]
    loads = [pltpu.make_async_copy(a, b, in_sem.at[k]) for k, (a, b) in enumerate(zip(ins, bufs))]
    for c in loads:
        c.start()
    clip = jnp.minimum(1.0, clip_level / (scalars[2:3, :] + 1e-06))
    for k in range(3):
        outs[8 + k][0] = scalars[k, 0]
    stores = []
    for part, rows in ((1, 161), (0, 804)):
        grad, p, m, v = bufs[4 * part:4 * part + 4]
        for c in loads[4 * part:4 * part + 4]:
            c.wait()
        g = grad[0:rows, :] * clip
        first = beta_one * m[...] + (1.0 - beta_one) * g
        second = beta_two * v[...] + (1.0 - beta_two) * g * g
        step = (first * (1.0 / (1.0 - beta_one ** STEP))) / (
            jnp.sqrt(second * (1.0 / (1.0 - beta_two ** STEP))) + adam_eps)
        old = p[...]
        new = old - learn_rate * (step + decay_rate * old)
        for k, value in enumerate((new, first, second, new.astype(bf))):
            news[4 * part + k][...] = value
            c = pltpu.make_async_copy(news[4 * part + k], outs[4 * part + k], out_sem.at[4 * part + k])
            c.start()
            stores.append(c)
    for c in stores:
        c.wait()


IN_ALL = ("steps", "labels", "valid")
LOADED = ("pa", "pb", "img", "nidx", "table")


def comm_scratch(chips):
    return dict(
        pa=((804, 128), f32), pb=((161, 128), f32), img=((NIMG, POS, C), bf), nidx=((NIMG, POS), jnp.int32),
        table=((NT, C), f32),
        w=((chips, 2, PIECE, C), bf), flat=((184, 128), f32), piece=((2, PIECE, 128), f32),
        ga=((2, A_ROWS + 16, 128), f32), gb=((2, B_ROWS + 16, 128), f32), loss=((1, C), f32),
        r1=((chips, PIECE, C), bf), r2=((4, 2, PIECE, C), bf), r3=((4, PIECE, C), bf), r4=((4, 2, PIECE, C), bf),
        t2=((4, 2, PIECE, C), bf), t3=((4, PIECE, C), bf), t4=((4, PIECE, C), bf),
        n1_in=((chips, 8, C), f32), n1_out=((8, C), f32),
        half=((2, 2, PIECE, 128), f32), flat_a=((808, 128), f32), flat_b=((168, 128), f32), msg=((2, 8, 128), f32), news=((chips, 2, 8, 128), f32))


def sem_counts(chips):
    return dict(zsem=3, ssem=4, tsem=8, csem=16, gcsem=5, gtsem=5, gssem=5, gzsem=16, n1sem=chips, hsem=1, nsem=chips - 1)


def whole_kernel(chips, *refs):
    R = Refs()
    refs = list(refs)
    for name in IN_ALL:
        setattr(R, name, refs.pop(0))
    R.sources = [refs.pop(0) for _ in LOADED]
    R.out_a, R.out_b, R.scalars = refs.pop(0), refs.pop(0), refs.pop(0)
    for name in list(SCRATCH) + list(comm_scratch(chips)):
        setattr(R, name, refs.pop(0))
    for name in sem_counts(chips):
        setattr(R, name, (refs.pop(0), refs.pop(0)))
    R.osem, R.isem = refs.pop(0), refs.pop(0)
    place = Place(chips)
    barrier = greet(R, place, chips)
    R.loads = []
    for n, (name, src) in enumerate(zip(LOADED, R.sources)):
        R.loads.append(pltpu.make_async_copy(src, getattr(R, name), R.isem.at[n]))
        R.loads[-1].start()
    for c in R.loads[:2]:
        c.wait()
    own_piece(R, place)
    pl.semaphore_wait(barrier, chips)

    def meanwhile():
        for c in R.loads[2:]:
            c.wait()
        first_setup(R)
    gather_weights(R, place, meanwhile)
    count = spread_rows(R, chips) * POS
    R.scalars[...] = jnp.zeros((8, 128), f32)
    R.scalars[1:2, :] = count
    unpack_weights(R, R.ga, R.gb)
    time_forward(R)
    R.scale_row[...] = 2.0 / jnp.concatenate([count, count], axis=1)
    for step in FORWARD_A + FORWARD_B:
        step(R)
    backward_and_reduce(R, place, chips)
    finish(R, place, chips)


def whole_step(chips, images, timesteps, labels, valid_slot, noise_idx, noise_table,
               params_a, params_b, first_a, second_a, first_b, second_b):
    smem = pl.BlockSpec(memory_space=pltpu.SMEM)
    vmem = pl.BlockSpec(memory_space=pltpu.VMEM)
    hbm = pl.BlockSpec(memory_space=pl.ANY)
    rows = lambda v: v.reshape(-1, 128)
    scratch = [pltpu.VMEM(s, d) for s, d in SCRATCH.values()] + [pltpu.VMEM(s, d) for s, d in comm_scratch(chips).values()]
    for n in sem_counts(chips).values():
        scratch += [pltpu.SemaphoreType.DMA((n,)), pltpu.SemaphoreType.DMA((n,))]
    scratch += [pltpu.SemaphoreType.DMA((2,)), pltpu.SemaphoreType.DMA((5,))]
    pa, pb = rows(params_a), rows(params_b)
    grad_a, grad_b, scalars = pl.pallas_call(
        functools.partial(whole_kernel, chips),
        out_shape=[jax.ShapeDtypeStruct((n, 128), f32) for n in (808, 168, 8)],
        in_specs=[smem] * 3 + [hbm] * 5,
        out_specs=[hbm, hbm, vmem],
        scratch_shapes=scratch,
        compiler_params=pltpu.CompilerParams(
            collective_id=0, has_side_effects=True, vmem_limit_bytes=63 * 1024 * 1024),
    )(timesteps, labels, valid_slot, pa, pb, images, noise_idx, noise_table)
    shapes = [jax.ShapeDtypeStruct((n, 128), d) for n in (804, 161) for d in (f32, f32, f32, bf)]
    buffers = [pltpu.VMEM((n + extra, 128), f32) for n, pad in ((804, 4), (161, 7)) for extra in (pad, 0, 0, 0)]
    outs = pl.pallas_call(
        update_kernel,
        out_shape=shapes + [jax.ShapeDtypeStruct((1,), f32)] * 3,
        in_specs=[hbm] * 8 + [vmem],
        out_specs=[hbm] * 8 + [smem] * 3,
        scratch_shapes=buffers + [pltpu.VMEM(s.shape, s.dtype) for s in shapes] + [pltpu.SemaphoreType.DMA((8,))] * 2,
        compiler_params=pltpu.CompilerParams(vmem_limit_bytes=63 * 1024 * 1024),
    )(grad_a, pa, rows(first_a), rows(second_a), grad_b, pb, rows(first_b), rows(second_b), scalars)
    return (*(v.reshape(-1) for v in outs[:8]), *(v.reshape(()) for v in outs[8:]))


def adam_update(master, grad_in, first_mom, second, clip_scale):
    clipped = grad_in * clip_scale
    first_new = beta_one * first_mom + (1.0 - beta_one) * clipped
    second_new = beta_two * second + (1.0 - beta_two) * clipped * clipped
    first_hat = first_new / (1.0 - beta_one**STEP)
    second_hat = second_new / (1.0 - beta_two**STEP)
    master_new = master - learn_rate * (
        first_hat / (jnp.sqrt(second_hat) + adam_eps) + decay_rate * master
    )
    return (master_new, first_new, second_new)


def plain_step(images, timesteps, labels, valid_slot, noise_idx, noise_table,
               params_a, params_b, first_a, second_a, first_b, second_b):
    gather = lambda v: lax.all_gather(v.astype(bf), "fsdp", axis=0, tiled=True).reshape(-1, C)
    count = lax.psum(jnp.sum(valid_slot).astype(f32) * POS, ("dp", "fsdp"))
    ga, gb, loss = compute(images, timesteps, labels, valid_slot, (2.0 / count).reshape(1), noise_idx, noise_table,
                           gather(params_a), gather(params_b))
    flat = lambda g: jnp.concatenate([g[0], g[1]], axis=1).reshape(-1)
    shard = lambda g: lax.psum_scatter(flat(g), "fsdp", scatter_dimension=0, tiled=True)
    part_a, part_b, loss = lax.psum((shard(ga), shard(gb), jnp.sum(loss)), "dp")
    loss, squares = lax.psum((loss, jnp.sum(part_a * part_a) + jnp.sum(part_b * part_b)), "fsdp")
    norm = jnp.sqrt(squares)
    clip = jnp.minimum(1.0, clip_level / (norm + 1e-06))
    new_a = adam_update(params_a, part_a, first_a, second_a, clip)
    new_b = adam_update(params_b, part_b, first_b, second_b, clip)
    return (*new_a, new_a[0].astype(bf), *new_b, new_b[0].astype(bf), loss, count, norm)


def solution(mesh):
    chips = mesh.shape["fsdp"]
    if chips == 16 and mesh.shape["dp"] == 2:
        step = functools.partial(whole_step, chips)
    else:
        step = plain_step
    both = P(("dp", "fsdp"))
    return jax.shard_map(
        step, mesh=mesh,
        in_specs=(both, both, both, both, both, P()) + (P("fsdp"),) * 6,
        out_specs=(P("fsdp"),) * 8 + (P(),) * 3,
        check_vma=False)
```

```python
import functools
import math
import jax
import jax.numpy as jnp
import numpy as np
from jax import lax
from jax.experimental import pallas as pl
from jax.experimental.pallas import tpu as pltpu
from jax.sharding import PartitionSpec as P

C = 256
SIDE = 16
POS = 256
TE = 512
SIN = 128
NCLS = 10
NT = 256
NIMG = 8
bf = jnp.bfloat16
f32 = jnp.float32
eps_norm = 1e-05
CH = 64
TY = 2
U = dict(conv=8, cback=8, triple=8, attn=8, head=8, aback=8, dx3=8, chunk=8, setup=8)

A_N1, A_K1, A_B1, A_W1, A_TB1, A_W2, A_TB2, A_CT, A_PT, A_PB, A_N2, A_K2, A_B2 = (
    0, 2, 2306, 2307, 2563, 2565, 3589, 3591, 3611, 4123, 4124, 4126, 6430)
A_ROWS = 6432
B_N3, B_W, B_QV, B_WO, B_BO, B_N4, B_WH, B_BH = (0, 2, 770, 772, 1028, 1029, 1031, 1287)
B_ROWS = 1288


def dot(a, b):
    return jnp.dot(a, b, preferred_element_type=f32)


def dot_nt(a, b):
    return lax.dot_general(a, b, (((1,), (1,)), ((), ())), preferred_element_type=f32)


def dot_tn(a, b):
    return lax.dot_general(a, b, (((0,), (0,)), ((), ())), preferred_element_type=f32)


def split3(x):
    hi = x.astype(bf).astype(f32)
    rest = x - hi
    mid = rest.astype(bf).astype(f32)
    return hi, mid, rest - mid


def wide_dot(x, w, nt=False):
    n = x.shape[0]
    stacked = jnp.concatenate(split3(x), axis=0).astype(bf)
    out = dot_nt(stacked, w) if nt else dot(stacked, w)
    return out[:n] + out[n:2 * n] + out[2 * n:]


def outer_sum(a, b):
    a0, a1, _ = split3(a)
    b0, b1, _ = split3(b)
    return dot_tn(jnp.concatenate([a0, a0, a1], axis=0).astype(bf),
                  jnp.concatenate([b0, b1, b0], axis=0).astype(bf))


def sigm(v):
    return 0.5 * jnp.tanh(0.5 * v) + 0.5


def rowsum(x):
    return jnp.sum(x, axis=0, keepdims=True)


def put_shifts(buf, i, r0, x):
    n = x.shape[0]
    col = lax.broadcasted_iota(jnp.int32, x.shape, 0) & 15
    left = jnp.where(col == 0, 0.0, pltpu.roll(x, 1, 0))
    right = jnp.where(col == 15, 0.0, pltpu.roll(x, n - 1, 0))
    y = n // 16
    for s, v in enumerate((left, x, right)):
        buf[pl.ds(1 + r0 // 16, y), i, :, 256 * s:256 * s + 256] = v.astype(bf).reshape(y, 16, C)


def conv_mm(buf, kmat, y, nt=False):
    ty = TY
    parts = [buf[pl.ds(y + r, ty)].reshape(ty * 128, 3 * C) for r in range(3)]
    rows = jnp.concatenate(parts, axis=1)
    return dot_nt(rows, kmat[...]) if nt else dot(rows, kmat[...])


class Refs:
    pass


def ld(f, row, n, stride=1):
    at = pl.ds(row, n, stride=stride) if stride > 1 else pl.ds(row, n)
    return jnp.concatenate([f[0, at, :], f[1, at, :]], axis=1)


def st(f, row, value, stride=1):
    n = value.shape[0]
    at = pl.ds(row, n, stride=stride) if stride > 1 else pl.ds(row, n)
    f[0, at, :] = value[:, :128]
    f[1, at, :] = value[:, 128:]


def unpack_kernel(kmat, kt, fa, base):
    for t in range(9):
        w = ld(fa, base + 256 * t, 256)
        kmat[256 * t:256 * t + 256, :] = w.astype(bf)
        kt[:, 256 * (8 - t):256 * (8 - t) + 256] = w.astype(bf)


def unpack_norm_one(R, fa):
    R.vec[0:2, :] = ld(fa, A_N1, 2)


def unpack_time(R, fa):
    for h in range(2):
        R.tw1[:, 256 * h:256 * h + 256] = ld(fa, A_W1 + h, SIN, 2).astype(bf)
        R.tw2[:, 256 * h:256 * h + 256] = ld(fa, A_W2 + h, TE, 2).astype(bf)
    R.pt[...] = ld(fa, A_PT, TE).astype(bf)
    for k, row in enumerate((A_B1, A_TB1, A_TB1 + 1, A_TB2, A_TB2 + 1, A_PB, A_N2, A_N2 + 1)):
        R.vec[2 + k:3 + k, :] = ld(fa, row, 1)
    R.ct[0:20, :] = ld(fa, A_CT, 20)


def unpack_second_kernel(R, fa):
    unpack_kernel(R.k2, R.k2t, fa, A_K2)
    R.vec[10:11, :] = ld(fa, A_B2, 1)


def unpack_b(R, fb):
    for h in range(3):
        w = ld(fb, B_W + h, C, 3)
        R.wt[:, 256 * h:256 * h + 256] = w.astype(bf)
        R.wtt[256 * h:256 * h + 256, :] = w.T.astype(bf)
    for base, mat, turned in ((B_WO, R.wo, R.wot), (B_WH, R.wh, R.wht)):
        w = ld(fb, base, C)
        mat[...] = w.astype(bf)
        turned[...] = w.T.astype(bf)
    for k, row in enumerate((B_N3, B_N3 + 1, B_QV, B_QV + 1, B_BO, B_N4, B_N4 + 1, B_BH)):
        R.vec[11 + k:12 + k, :] = ld(fb, row, 1)


def unpack_weights(R, fa, fb):
    unpack_norm_one(R, fa)
    unpack_kernel(R.k1, R.k1t, fa, A_K1)
    unpack_time(R, fa)
    unpack_second_kernel(R, fa)
    unpack_b(R, fb)


(V_G1, V_C1, V_B1, V_TB1, V_TB1B, V_TB2, V_TB2B, V_PB, V_G2, V_C2, V_B2,
 V_G3, V_C3, V_QB, V_VB, V_BO, V_G4, V_C4, V_BH) = range(19)


def vec(R, k):
    return R.vec[k:k + 1, :]


def group_mean(R, s):
    return wide_dot(s, R.gm[...])


def stats(R, k, load, add=None):
    for i in range(NIMG):
        R.tmp[i:i + 1, :] = rowsum(load(i))
    mean = group_mean(R, R.tmp[0:8, :]) if add is None else group_mean(R, R.tmp[0:8, :] + POS * add) - add
    R.mean[k] = mean
    for i in range(NIMG):
        x = load(i) - mean[i:i + 1, :]
        R.tmp[i:i + 1, :] = rowsum(x * x)
    R.inv[k] = lax.rsqrt(group_mean(R, R.tmp[0:8, :]) + eps_norm)


def norm_sums(R, k, gain):
    s1, s2 = R.s1[...], R.s2[...]
    m = group_mean(R, jnp.concatenate([s1 * gain, s2 * gain], axis=0))
    R.m1[...] = m[:8] * R.inv[k]
    R.m2[...] = m[8:] * R.inv[k]
    return rowsum(s2), rowsum(s1)


def first_setup(R):
    row = lax.broadcasted_iota(jnp.int32, (C, C), 0) >> 3
    col = lax.broadcasted_iota(jnp.int32, (C, C), 1) >> 3
    R.gm[...] = jnp.where(row == col, 1.0 / 2048.0, 0.0).astype(bf)
    zero = jnp.zeros((1, NIMG, 16, 3 * C), bf)
    for buf in (R.buf1, R.buf2, R.dbuf):
        buf[0:1] = zero
        buf[17:18] = zero
    hi, mid, lo = split3(R.table[...])
    R.tab3[...] = jnp.concatenate([hi, mid, lo], axis=1).astype(bf)

    @pl.loop(0, NIMG, unroll=U["setup"])
    def _(i):
        rows = lax.broadcasted_iota(jnp.int32, (NT, POS), 0)
        hot = jnp.where(rows == R.nidx[pl.ds(i, 1), :], 1.0, 0.0)
        out = dot(hot.T.astype(bf), R.tab3[...])
        R.target[i] = out[:, :C] + out[:, C:2 * C] + out[:, 2 * C:]
    stats(R, 0, lambda i: R.img[i].astype(f32))


def column_of(smem, shape):
    row = lax.broadcasted_iota(jnp.int32, shape, 0)
    out = jnp.zeros(shape, jnp.int32)
    for i in range(NIMG):
        out = jnp.where(row == i, smem[i], out)
    return out


def time_forward(R):
    lane = lax.broadcasted_iota(jnp.int32, (NIMG, SIN), 1)
    factor = math.log(10000.0) / (SIN // 2 - 1)
    freq = jnp.exp((lane & 63).astype(f32) * -factor)
    angle = column_of(R.steps, (NIMG, SIN)).astype(f32) * freq
    e = jnp.where(lane < 64, jnp.sin(angle), jnp.cos(angle))
    R.emb[...] = e
    u = wide_dot(e, R.tw1[...]) + jnp.concatenate([vec(R, V_TB1), vec(R, V_TB1B)], axis=1)
    R.pre[...] = u
    lab = column_of(R.labels, (NIMG, TE))
    te = wide_dot(u * sigm(u), R.tw2[...]) + jnp.concatenate([vec(R, V_TB2), vec(R, V_TB2B)], axis=1)
    for j in range(NCLS):
        row = jnp.concatenate([R.ct[2 * j:2 * j + 1, :], R.ct[2 * j + 1:2 * j + 2, :]], axis=1)
        te = te + jnp.where(lab == j, row, 0.0)
    R.te[...] = te
    add = wide_dot(te * sigm(te), R.pt[...]) + vec(R, V_PB) + vec(R, V_B1)
    R.add[...] = add


def each_chunk(fn):
    @pl.loop(0, NIMG, unroll=U["chunk"])
    def _(i):
        for c in range(POS // CH):
            fn(i, c * CH)


def normed(R, k, i, x):
    return (x - R.mean[k, pl.ds(i, 1), :]) * R.inv[k, pl.ds(i, 1), :]


def step_x1(R):
    def one(i, r0):
        x = normed(R, 0, i, R.img[i, r0:r0 + CH, :].astype(f32))
        a = x * vec(R, V_G1) + vec(R, V_C1)
        put_shifts(R.buf1, i, r0, a * sigm(a))
    each_chunk(one)


def conv_one(R, lo, hi):
    @pl.loop(lo, hi, unroll=hi - lo)
    def _(t):
        acc = conv_mm(R.buf1, R.k1, t * TY).reshape(TY, NIMG, 16, C)
        for yy in range(TY):
            R.c1[:, pl.ds(pl.multiple_of((t * TY + yy) * 16, 16), 16), :] = acc[yy]


def step_conv1(R):
    conv_one(R, 0, SIDE // TY)


def step_stats1(R):
    stats(R, 1, lambda i: R.c1[i], R.add[...])


def step_x2(R):
    def two(i, r0):
        x = normed(R, 1, i, R.c1[i, r0:r0 + CH, :])
        a = x * vec(R, V_G2) + vec(R, V_C2)
        put_shifts(R.buf2, i, r0, a * sigm(a))
    each_chunk(two)


def step_conv2(R):
    @pl.loop(0, SIDE // TY, unroll=U["conv"])
    def _(t):
        acc = conv_mm(R.buf2, R.k2, t * TY).reshape(TY, NIMG, 16, C)
        for yy in range(TY):
            at = pl.ds(pl.multiple_of((t * TY + yy) * 16, 16), 16)
            R.h1[:, at, :] = acc[yy] + R.img[:, at, :].astype(f32) + vec(R, V_B2)


def step_stats2(R):
    stats(R, 2, lambda i: R.h1[i])


def step_triple(R):
    bias = jnp.concatenate([vec(R, V_QB), jnp.zeros((1, C), f32), vec(R, V_VB)], axis=1)

    @pl.loop(0, NIMG, unroll=U["triple"])
    def _(i):
        x = (normed(R, 2, i, R.h1[i]) * vec(R, V_G3) + vec(R, V_C3)).astype(bf)
        R.x3t[:, pl.ds(pl.multiple_of(i * POS, POS), POS)] = x.T
        R.tri[i] = (dot(x, R.wt[...]) + bias).astype(bf)


def step_attn(R):
    for g in range(0, NIMG, 8):
        for i in range(g, g + 8):
            R.p[i] = dot_nt(R.tri[i, :, 0:C], R.tri[i, :, C:2 * C])
        for i in range(g, g + 8):
            for r in range(0, POS, CH):
                s = R.p[i, r:r + CH, :] * C ** (-0.5)
                e = jnp.exp(s - jnp.max(s, axis=1, keepdims=True))
                R.p[i, r:r + CH, :] = e * (1.0 / jnp.sum(e, axis=1, keepdims=True))
        for i in range(g, g + 8):
            R.o[i] = dot(R.p[i].astype(bf), R.tri[i, :, 2 * C:]).astype(bf)
        for i in range(g, g + 8):
            R.h2[i] = R.h1[i] + dot(R.o[i], R.wo[...]) + vec(R, V_BO)


def step_stats3(R):
    stats(R, 3, lambda i: R.h2[i])


def step_head(R):
    scale = R.scale_row[...]
    loss = jnp.zeros((8, C), f32)
    bias = jnp.zeros((8, C), f32)
    for g in range(0, NIMG, 8):
        for i in range(g, g + 8):
            for r in range(0, POS, CH):
                a = normed(R, 3, i, R.h2[i, r:r + CH, :]) * vec(R, V_G4) + vec(R, V_C4)
                sg = sigm(a)
                R.low[i, r:r + CH, :] = (a * sg).astype(bf)
                R.dh[i, r:r + CH, :] = sg * (1.0 + a * (1.0 - sg))
        for i in range(g, g + 8):
            R.da[i] = dot(R.low[i], R.wh[...])
            R.xt[:, i * POS:(i + 1) * POS] = R.low[i].T
        for i in range(g, g + 8):
            valid = R.valid[i].astype(f32)
            for r in range(0, POS, CH):
                differ = R.da[i, r:r + CH, :] + vec(R, V_BH) - R.target[i, r:r + CH, :]
                dv = valid * differ
                loss += fold(dv * differ)
                dp = dv * scale
                bias += fold(dp)
                R.low[i, r:r + CH, :] = dp.astype(bf)
        for i in range(g, g + 8):
            R.da[i] = dot(R.low[i], R.wht[...])
        for i in range(g, g + 8):
            s1 = jnp.zeros((8, C), f32)
            s2 = jnp.zeros((8, C), f32)
            for r in range(0, POS, CH):
                x = normed(R, 3, i, R.h2[i, r:r + CH, :])
                da = R.da[i, r:r + CH, :] * R.dh[i, r:r + CH, :]
                R.da[i, r:r + CH, :] = da
                s1 += fold(da)
                s2 += fold(da * x)
            R.s1[i:i + 1, :] = rowsum(s1)
            R.s2[i:i + 1, :] = rowsum(s2)
    R.loss[...] = rowsum(loss)
    R.sh[...] = rowsum(bias)


def step_head_grads(R):
    st(R.gb, B_BH, R.sh[...])
    st(R.gb, B_WH, dot(R.xt[...], R.low[...].reshape(NIMG * POS, C)))
    dg, db = norm_sums(R, 3, vec(R, V_G4))
    st(R.gb, B_N4, dg)
    st(R.gb, B_N4 + 1, db)


def step_attn_back(R):
    out_bias = jnp.zeros((8, C), f32)
    q_bias = jnp.zeros((8, C), f32)
    v_bias = jnp.zeros((8, C), f32)
    for g in range(0, NIMG, 8):
        images = range(g, g + 8)
        for i in images:
            for r in range(0, POS, CH):
                x = normed(R, 3, i, R.h2[i, r:r + CH, :])
                d = ((R.inv[3, i:i + 1, :] * vec(R, V_G4)) * R.da[i, r:r + CH, :]
                     - R.m1[i:i + 1, :] - x * R.m2[i:i + 1, :])
                R.dh[i, r:r + CH, :] = d
                out_bias += fold(d)
                R.low[i, r:r + CH, :] = d.astype(bf)
            R.xt[:, i * POS:(i + 1) * POS] = R.o[i].T
        for i in images:
            R.o[i] = dot(R.low[i], R.wot[...]).astype(bf)
        for i in images:
            R.da[i] = dot_nt(R.o[i], R.tri[i, :, 2 * C:])
            dv = dot_tn(R.p[i].astype(bf), R.o[i]).astype(bf)
            R.tri[i, :, 2 * C:] = dv
            v_bias += fold(dv.astype(f32))
        for i in images:
            for r in range(0, POS, CH):
                p = R.p[i, r:r + CH, :]
                dpr = R.da[i, r:r + CH, :]
                R.p[i, r:r + CH, :] = p * (dpr - jnp.sum(dpr * p, axis=1, keepdims=True))
        for i in images:
            ds = R.p[i].astype(bf)
            dq = (dot(ds, R.tri[i, :, C:2 * C]) * C ** (-0.5)).astype(bf)
            dk = (dot_tn(ds, R.tri[i, :, 0:C]) * C ** (-0.5)).astype(bf)
            R.tri[i, :, 0:C] = dq
            R.tri[i, :, C:2 * C] = dk
            q_bias += fold(dq.astype(f32))
    st(R.gb, B_BO, rowsum(out_bias))
    st(R.gb, B_QV, rowsum(q_bias))
    st(R.gb, B_QV + 1, rowsum(v_bias))


def step_out_grads(R):
    st(R.gb, B_WO, dot(R.xt[...], R.low[...].reshape(NIMG * POS, C)))


def step_dx3(R):
    @pl.loop(0, NIMG, unroll=U["dx3"])
    def _(i):
        da = dot(R.tri[i], R.wtt[...])
        R.da[i] = da
        R.s1[pl.ds(i, 1), :] = rowsum(da)
        R.s2[pl.ds(i, 1), :] = rowsum(da * normed(R, 2, i, R.h1[i]))


def step_triple_grads(R):
    for h in range(3):
        st(R.gb, B_W + h, dot(
            R.x3t[...], R.tri[:, :, 256 * h:256 * h + 256].reshape(NIMG * POS, C)), 3)
    dg, db = norm_sums(R, 2, vec(R, V_G3))
    st(R.gb, B_N3, dg)
    st(R.gb, B_N3 + 1, db)


def kernel_lhs(R, buf):
    @pl.loop(0, SIDE // 2, unroll=8)
    def _(t):
        x = buf[pl.ds(1 + 2 * t, 2), :, :, C:2 * C].reshape(256, C)
        R.xt[:, pl.ds(pl.multiple_of(t * 256, 256), 256)] = x.T


def kernel_taps(R, row, taps):
    for tap in taps:
        r, s = divmod(tap, 3)
        d = R.dbuf[2 - r:18 - r, :, :, 256 * (2 - s):256 * (3 - s)].reshape(NIMG * POS, C)
        st(R.ga, row + tap * 256, dot(R.xt[...], d))


def conv_back(R, kt, rows=(0, SIDE // TY)):
    @pl.loop(rows[0], rows[1], unroll=rows[1] - rows[0])
    def _(t):
        acc = conv_mm(R.dbuf, kt, t * TY, True).reshape(TY, NIMG, 16, C)
        for yy in range(TY):
            R.da[:, pl.ds(pl.multiple_of((t * TY + yy) * 16, 16), 16), :] = acc[yy]


def fold(x):
    return jnp.sum(x.reshape(x.shape[0] // 8, 8, x.shape[1]), axis=0)


def swish_back(R, k, load, vg, vc, keep):
    for i in range(NIMG):
        s1 = jnp.zeros((8, C), f32)
        s2 = jnp.zeros((8, C), f32)
        for r0 in range(0, POS, CH):
            x = normed(R, k, i, load(i, r0))
            a = x * vec(R, vg) + vec(R, vc)
            sg = sigm(a)
            da = R.da[i, r0:r0 + CH, :] * (sg * (1.0 + a * (1.0 - sg)))
            if keep:
                R.da[i, r0:r0 + CH, :] = da
            s1 += fold(da)
            s2 += fold(da * x)
        R.s1[i:i + 1, :] = rowsum(s1)
        R.s2[i:i + 1, :] = rowsum(s2)


def step_dh1(R):
    R.sums8[...] = jnp.zeros_like(R.sums8)

    def one(i, r0):
        at = slice(r0, r0 + CH)
        x = normed(R, 2, i, R.h1[i, at, :])
        d = (R.dh[i, at, :] + (R.inv[2, pl.ds(i, 1), :] * vec(R, V_G3)) * R.da[i, at, :]
             - R.m1[pl.ds(i, 1), :] - x * R.m2[pl.ds(i, 1), :])
        R.sums8[...] += fold(d)
        put_shifts(R.dbuf, i, r0, d)
    each_chunk(one)
    st(R.ga, A_B2, rowsum(R.sums8[...]))


def step_dk2(R):
    kernel_lhs(R, R.buf2)
    kernel_taps(R, A_K2, range(9))


def step_dx2_high(R):
    conv_back(R, R.k2t, (0, 4))


def step_dx2_low(R):
    conv_back(R, R.k2t, (4, 8))


def step_da2(R):
    swish_back(R, 1, lambda i, r0: R.c1[i, r0:r0 + CH, :], V_G2, V_C2, True)
    dg, db = norm_sums(R, 1, vec(R, V_G2))
    st(R.ga, A_N2, dg)
    st(R.ga, A_N2 + 1, db)


def step_dc1(R):
    R.tmp[...] = jnp.zeros_like(R.tmp)

    def two(i, r0):
        at = slice(r0, r0 + CH)
        x = normed(R, 1, i, R.c1[i, at, :])
        d = ((R.inv[1, pl.ds(i, 1), :] * vec(R, V_G2)) * R.da[i, at, :]
             - R.m1[pl.ds(i, 1), :] - x * R.m2[pl.ds(i, 1), :])
        R.tmp[pl.ds(i, 1), :] += rowsum(d)
        put_shifts(R.dbuf, i, r0, d)
    each_chunk(two)


def step_dk1_high(R):
    kernel_lhs(R, R.buf1)
    kernel_taps(R, A_K1, (6, 7, 8))


def step_dk1_mid(R):
    kernel_taps(R, A_K1, (3, 4, 5))


def step_dk1_low(R):
    kernel_taps(R, A_K1, (0, 1, 2))


def step_dx1_high(R):
    conv_back(R, R.k1t, (0, 4))


def step_dx1_low(R):
    conv_back(R, R.k1t, (4, 8))


def step_da1(R):
    swish_back(R, 0, lambda i, r0: R.img[i, r0:r0 + CH, :].astype(f32), V_G1, V_C1, False)
    R.n1[0:1, :] = rowsum(R.s2[...])
    R.n1[1:2, :] = rowsum(R.s1[...])


def swish_slope(v):
    s = sigm(v)
    return s * (1.0 + v * (1.0 - s))


def time_backward(R):
    d_add = R.tmp[0:8, :]
    total = rowsum(d_add)
    st(R.ga, A_B1, total)
    st(R.ga, A_PB, total)
    te = R.te[...]
    st(R.ga, A_PT, outer_sum(te * sigm(te), d_add))
    d_te = wide_dot(d_add, R.pt[...], nt=True) * swish_slope(te)
    lab = column_of(R.labels, (NIMG, TE))
    for j in range(NCLS):
        row = rowsum(jnp.where(lab == j, d_te, 0.0))
        for h in range(2):
            st(R.ga, A_CT + 2 * j + h, row[:, 256 * h:256 * h + 256])
    row = rowsum(d_te)
    u = R.pre[...]
    dw2 = outer_sum(u * sigm(u), d_te)
    d_u = wide_dot(d_te, R.tw2[...], nt=True) * swish_slope(u)
    row1 = rowsum(d_u)
    dw1 = outer_sum(R.emb[...], d_u)
    for h in range(2):
        st(R.ga, A_TB2 + h, row[:, 256 * h:256 * h + 256])
        st(R.ga, A_TB1 + h, row1[:, 256 * h:256 * h + 256])
        st(R.ga, A_W2 + h, dw2[:, 256 * h:256 * h + 256], 2)
        st(R.ga, A_W1 + h, dw1[:, 256 * h:256 * h + 256], 2)


FORWARD_A = (step_x1, step_conv1, step_stats1, step_x2, step_conv2, step_stats2)
FORWARD_B = (step_triple, step_attn, step_stats3, step_head, step_head_grads, step_attn_back, step_out_grads, step_dx3, step_triple_grads)
BACKWARD = (step_dh1, step_dk2, step_dx2_high, step_dx2_low, step_da2, step_dc1, time_backward, step_dk1_high, step_dk1_mid, step_dk1_low,
            step_dx1_high, step_dx1_low, step_da1)
STEPS = FORWARD_A + FORWARD_B + BACKWARD


SCRATCH = dict(
    k1=((2304, C), bf), k1t=((C, 2304), bf), k2=((2304, C), bf), k2t=((C, 2304), bf),
    tw1=((SIN, TE), bf), tw2=((TE, TE), bf), pt=((TE, C), bf),
    wt=((C, 3 * C), bf), wtt=((3 * C, C), bf), wo=((C, C), bf), wot=((C, C), bf), wh=((C, C), bf), wht=((C, C), bf),
    vec=((24, C), f32), ct=((24, C), f32),
    gm=((C, C), bf), tab3=((NT, 3 * C), bf), target=((NIMG, POS, C), f32),
    tmp=((8, C), f32), mean=((4, 8, C), f32), inv=((4, 8, C), f32),
    s1=((8, C), f32), s2=((8, C), f32), m1=((8, C), f32), m2=((8, C), f32),
    sh=((1, C), f32), sums8=((8, C), f32), scale_row=((1, C), f32), n1=((8, C), f32), sq=((1, 2 * C), f32),
    emb=((8, SIN), f32), pre=((8, TE), f32), te=((8, TE), f32), add=((8, C), f32),
    buf1=((18, 8, 16, 3 * C), bf), buf2=((18, 8, 16, 3 * C), bf), dbuf=((18, 8, 16, 3 * C), bf),
    c1=((8, POS, C), f32), h1=((8, POS, C), f32), h2=((8, POS, C), f32), da=((8, POS, C), f32), dh=((8, POS, C), f32),
    p=((8, POS, POS), f32), o=((8, POS, C), bf), low=((8, POS, C), bf),
    tri=((8, POS, 3 * C), bf),
    x3t=((C, 8 * POS), bf), xt=((C, 8 * POS), bf),
)


def main_kernel(names_in, *refs):
    R = Refs()
    n_in = len(names_in)
    for name, r in zip(names_in, refs):
        setattr(R, name, r)
    R.ga, R.gb, R.loss = refs[n_in:n_in + 3]
    for name, r in zip(list(SCRATCH), refs[n_in + 3:]):
        setattr(R, name, r)
    fa, fb = R.ga, R.gb
    for c in range(0, A_ROWS, 402):
        st(fa, c, R.wa[c:c + 402, :].astype(f32))
    st(fb, 0, R.wb[...].astype(f32))
    R.scale_row[...] = jnp.full((1, C), R.scale[0])
    first_setup(R)
    unpack_weights(R, fa, fb)
    time_forward(R)
    for step in STEPS:
        step(R)
    st(R.ga, A_N1, R.n1[0:2, :])
    st(R.ga, A_ROWS - 1, jnp.zeros((1, C), f32))


def compute(img, steps, labels, valid, scale, nidx, table, wa, wb):
    smem = pl.BlockSpec(memory_space=pltpu.SMEM)
    vmem = pl.BlockSpec(memory_space=pltpu.VMEM)
    names = ("img", "steps", "labels", "valid", "scale", "nidx", "table", "wa", "wb")
    return pl.pallas_call(
        functools.partial(main_kernel, names),
        out_shape=(jax.ShapeDtypeStruct((2, A_ROWS, 128), f32), jax.ShapeDtypeStruct((2, B_ROWS, 128), f32),
                   jax.ShapeDtypeStruct((1, C), f32)),
        in_specs=[vmem, smem, smem, smem, smem, vmem, vmem, vmem, vmem],
        out_specs=(vmem, vmem, vmem),
        scratch_shapes=[pltpu.VMEM(s, d) for s, d in SCRATCH.values()],
        compiler_params=pltpu.CompilerParams(vmem_limit_bytes=63 * 1024 * 1024),
    )(img, steps, labels, valid, scale, nidx, table, wa, wb)


beta_one = 0.5
beta_two = 0.5
learn_rate = 0.1
decay_rate = 0.01
adam_eps = 1e-08
clip_level = 0.01
STEP = 5
PA = A_ROWS * C
PB = B_ROWS * C
MESH = pl.DeviceIdType.MESH
ORDER = (0, 1, 3, 2)
HALF_A, HALF_B, PIECE = 201, 48, 256
B_AT = 208


class Place:
    def __init__(self, chips):
        self.me = lax.axis_index("fsdp")
        self.core = lax.axis_index("dp")
        self.depth = chips // 4

    def z(self, k, d):
        return lax.rem(lax.div(k, 4) + d + self.depth, self.depth) * 4 + lax.rem(k, 4)

    def flip_x(self, k):
        return k + 1 - 2 * lax.rem(k, 2)

    def flip_y(self, k):
        return k + 2 - 4 * lax.rem(lax.div(k, 2), 2)

    def s(self, k):
        return self.core * self.flip_x(k) + (1 - self.core) * self.flip_y(k)

    def t(self, k):
        return self.core * self.flip_y(k) + (1 - self.core) * self.flip_x(k)

    def pieces(self):
        line = [self.z(self.me, -j) for j in range(4)]
        near = line + [self.s(k) for k in line]
        return near + [self.t(k) for k in near]


def send(src, dst, sems, at, core, chip):
    copy = pltpu.make_async_remote_copy(
        src_ref=src, dst_ref=dst, send_sem=sems[0].at[at], recv_sem=sems[1].at[at],
        device_id=(core, chip), device_id_type=MESH)
    copy.start()
    return copy


def greet(R, place, chips):
    barrier = pltpu.get_barrier_semaphore()
    for d in range(1, chips):
        pl.semaphore_signal(barrier, inc=1, device_id=(place.core, lax.rem(place.me + d, chips)), device_id_type=MESH)
    pl.semaphore_signal(barrier, inc=1, device_id=(1 - place.core, place.me), device_id_type=MESH)
    return barrier


def own_piece(R, place):
    count = R.valid[0]
    for i in range(1, NIMG):
        count = count + R.valid[i]
    count = count.astype(f32)
    odd = lax.rem(place.me, 2) == 1
    R.flat[0:8, :] = jnp.zeros((8, 128), f32)
    R.flat[168:184, :] = jnp.zeros((16, 128), f32)
    R.flat[8:169, :] = R.pb[...]
    for h in range(2):
        for lane in range(2):
            R.piece[lane, 0:201, :] = R.pa[pl.ds(402 * h + lane, 201, stride=2), :]
            even_rows = R.flat[pl.ds(8 + lane + 96 * h, 48 - 8 * h, stride=2), :]
            odd_rows = R.flat[pl.ds(7 + lane + 96 * h, 48 - 8 * h, stride=2), :]
            R.piece[lane, 208:256 - 8 * h, :] = jnp.where(odd, odd_rows, even_rows)
        R.piece[:, 201:208, :] = jnp.full((2, 7, 128), count)

        @pl.when(place.core == h)
        def _():
            R.w[place.me, h] = jnp.concatenate([R.piece[0], R.piece[1]], axis=1).astype(bf)


def gather_weights(R, place, meanwhile):
    me, core = place.me, place.core
    got = place.pieces()
    put = lambda k: R.w.at[k, core]
    over_s, over_t = place.s(me), place.t(me)
    zc = {d: send(put(me), put(me), R.zsem, d - 1, core, place.z(me, d)) for d in (1, 3, 2)}
    sc, tc, sib = {}, {}, {}
    for j in ORDER:
        if j == 1:
            meanwhile()
        if j:
            zc[j].wait_recv()
        sc[j] = send(put(got[j]), put(got[j]), R.ssem, j, core, over_s)
        tc[j] = send(put(got[j]), put(got[j]), R.tsem, j, core, over_t)
        sib[j] = send(put(got[j]), put(got[j]), R.csem, j, 1 - core, me)
    for j in ORDER:
        sc[j].wait_recv()
        q = 4 + j
        tc[q] = send(put(got[q]), put(got[q]), R.tsem, q, core, over_t)
        sib[q] = send(put(got[q]), put(got[q]), R.csem, q, 1 - core, me)
    for half in (0, 4):
        for j in ORDER:
            q = half + j
            tc[q].wait_recv()
            sib[8 + q] = send(put(got[8 + q]), put(got[8 + q]), R.csem, 8 + q, 1 - core, me)
    for c in sib.values():
        c.wait_recv()
    for group in (zc, sc, tc, sib):
        for c in group.values():
            c.wait_send()


def spread_rows(R, chips):
    count = jnp.zeros((1, 128), f32)
    for k in range(chips):
        base = (161 * k) // 2
        odd = k % 2
        for h in range(2):
            a = R.w[k, h, 0:208, :].astype(f32)
            row = 402 * k + 201 * h
            R.ga[0, row:row + 208, :] = a[:, :128]
            R.ga[1, row:row + 208, :] = a[:, 128:]
            count = count + a[201:202, :128]
            b = R.w[k, h, 208:256, :].astype(f32)
            if h == 0:
                R.gb[0, base + odd:base + 48, :] = b[odd:, :128]
                R.gb[1, base:base + 48, :] = b[:, 128:]
            else:
                R.gb[0, base + 48:base + 81, :] = b[:33, :128]
                R.gb[1, base + 48:base + 80 + odd, :] = b[:32 + odd, 128:]
    return count


def pack_a(R, zt):
    for k in range(4 * zt, 4 * zt + 4):
        for h in range(2):
            R.w[k, h, 0:B_AT, :] = ld(R.ga, 402 * k + 201 * h, B_AT).astype(bf)


def pack_b(R, chips):
    for k in range(chips):
        base = (161 * k) // 2
        for h in range(2):
            R.w[k, h, B_AT:PIECE, :] = ld(R.gb, base + HALF_B * h, HALF_B).astype(bf)


def late(src, dst, send_sem, recv_sem, core, chip):
    return pltpu.make_async_remote_copy(src_ref=src, dst_ref=dst, send_sem=send_sem, recv_sem=recv_sem,
                                        device_id=(core, chip), device_id_type=MESH)


class Reduction:
    def __init__(self, R, place, at):
        self.R, self.place, self.at = R, place, at
        self.planes = (at,) if at < 4 else range(4)
        self.rows = pl.ds(0, B_AT) if at < 4 else pl.ds(B_AT, HALF_B)
        me, core, rows = place.me, place.core, self.rows
        self.mine = lax.rem(me, 4)
        self.z = lax.div(me, 4)
        group = pl.ds(4 * at, 4) if at < 4 else pl.ds(0, 16)
        plane = pl.ds(at, 1) if at < 4 else pl.ds(0, 4)
        sems = lambda pair: (pair[0].at[at], pair[1].at[at])
        self.across_core = late(R.w.at[group, 1 - core, rows], R.r1.at[group, rows], *sems(R.gcsem), 1 - core, me)
        self.across_t = late(R.t2.at[plane, :, rows], R.r2.at[plane, :, rows], *sems(R.gtsem), core, place.t(me))
        self.across_s = late(R.t3.at[plane, rows], R.r3.at[plane, rows], *sems(R.gssem), core, place.s(me))
        self.along = {}
        for zt in self.planes:
            far, mid, near = (3, 2, 1 - zt) if zt < 2 else (0, 1, 5 - zt)
            base = 2 * (zt if at < 4 else 4 + zt)
            go = lambda slot, to: late(R.t4.at[zt, rows], R.r4.at[zt, slot, rows], R.gzsem[0].at[base + slot],
                                       R.gzsem[1].at[base + slot], core, 4 * to + self.mine)
            self.along[zt] = (far, mid, near, go(1, mid), go(1, zt), go(0, zt))

    def both_cores(self, k):
        R = self.R
        return R.w[k, self.place.core, self.rows].astype(f32) + R.r1[k, self.rows].astype(f32)

    def start(self):
        self.across_core.start()

    def step_t(self):
        R, place = self.R, self.place
        self.across_core.wait_recv()
        for zt in self.planes:
            k = place.t(4 * zt + self.mine)
            R.t2[zt, 0, self.rows] = self.both_cores(place.s(k)).astype(bf)
            R.t2[zt, 1, self.rows] = self.both_cores(k).astype(bf)
        self.across_t.start()

    def step_s(self):
        R = self.R
        self.across_t.wait_recv()
        for zt in self.planes:
            k = self.place.s(4 * zt + self.mine)
            R.t3[zt, self.rows] = (self.both_cores(k) + R.r2[zt, 0, self.rows].astype(f32)).astype(bf)
        self.across_s.start()

    def step_z(self):
        R = self.R
        self.across_s.wait_recv()
        for zt in self.planes:
            far, mid, near, to_mid, mid_on, near_on = self.along[zt]
            total = (self.both_cores(4 * zt + self.mine) + R.r2[zt, 1, self.rows].astype(f32)
                     + R.r3[zt, self.rows].astype(f32))

            @pl.when(self.z == zt)
            def _():
                R.half[self.place.core, 0, self.rows] = total[:, :128]
                R.half[self.place.core, 1, self.rows] = total[:, 128:]

            @pl.when(self.z != zt)
            def _():
                R.t4[zt, self.rows] = total.astype(bf)

            @pl.when(self.z == far)
            def _():
                to_mid.start()

            @pl.when(self.z == near)
            def _():
                near_on.start()

    def step_mid(self):
        R = self.R
        for zt in self.planes:
            far, mid, near, to_mid, mid_on, near_on = self.along[zt]

            @pl.when(self.z == mid)
            def _():
                to_mid.wait_recv()
                R.t4[zt, self.rows] = (R.t4[zt, self.rows].astype(f32) + R.r4[zt, 1, self.rows].astype(f32)).astype(bf)
                mid_on.start()

    def step_end(self):
        R, core = self.R, self.place.core
        for zt in self.planes:
            far, mid, near, to_mid, mid_on, near_on = self.along[zt]

            @pl.when(self.z == zt)
            def _():
                near_on.wait_recv()
                mid_on.wait_recv()
                more = R.r4[zt, 0, self.rows].astype(f32) + R.r4[zt, 1, self.rows].astype(f32)
                R.half[core, 0, self.rows] += more[:, :128]
                R.half[core, 1, self.rows] += more[:, 128:]

    def drain(self):
        for c in (self.across_core, self.across_t, self.across_s):
            c.wait_send()
        for zt in self.planes:
            far, mid, near, to_mid, mid_on, near_on = self.along[zt]

            @pl.when(self.z == far)
            def _():
                to_mid.wait_send()

            @pl.when(self.z == mid)
            def _():
                mid_on.wait_send()

            @pl.when(self.z == near)
            def _():
                near_on.wait_send()


class NormOne:
    def __init__(self, R, place, chips):
        self.R, self.me, self.core, self.chips = R, place.me, place.core, chips
        self.cross = late(R.n1, R.n1_in.at[0], R.n1sem[0].at[0], R.n1sem[1].at[0], 1 - place.core, place.me)
        self.home = [late(R.n1_out, R.n1_in.at[d], R.n1sem[0].at[d], R.n1sem[1].at[d], place.core,
                          lax.rem(place.me + chips - d, chips)) for d in range(1, chips)]

    def start(self):
        @pl.when(self.core == 1)
        def _():
            self.cross.start()

    def to_home(self):
        R = self.R

        @pl.when(self.core == 0)
        def _():
            self.cross.wait_recv()
            R.n1_out[...] = R.n1[...] + R.n1_in[0]
        for d in range(1, self.chips):
            @pl.when(jnp.logical_and(self.core == 0, self.me == d))
            def _():
                self.home[d - 1].start()

    def end(self):
        R = self.R

        @pl.when(jnp.logical_and(self.core == 0, self.me == 0))
        def _():
            total = R.n1_out[...]
            for d in range(1, self.chips):
                self.home[d - 1].wait_recv()
                total = total + R.n1_in[d]
            R.half[0, 0, 0:2, :] = total[0:2, :128]
            R.half[0, 1, 0:2, :] = total[0:2, 128:]

    def drain(self):
        @pl.when(self.core == 1)
        def _():
            self.cross.wait_send()
        for d in range(1, self.chips):
            @pl.when(jnp.logical_and(self.core == 0, self.me == d))
            def _():
                self.home[d - 1].wait_send()


def backward_and_reduce(R, place, chips):
    r0, r1, r2, r3, rb = (Reduction(R, place, at) for at in range(5))
    n1 = NormOne(R, place, chips)
    R.n1[...] = jnp.zeros((8, C), f32)
    st(R.ga, A_N1, jnp.zeros((2, C), f32))
    st(R.ga, A_ROWS - 1, jnp.zeros((1, C), f32))
    pack_b(R, chips)
    rb.start()
    step_dh1(R)
    rb.step_t()
    step_dk2(R)
    pack_a(R, 3)
    r3.start()
    rb.step_s()
    step_dx2_high(R)
    r3.step_t()
    step_dx2_low(R)
    step_da2(R)
    rb.step_z()
    step_dc1(R)
    r3.step_s()
    time_backward(R)
    pack_a(R, 2)
    r2.start()
    rb.step_mid()
    step_dk1_high(R)
    pack_a(R, 1)
    r1.start()
    r2.step_t()
    step_dk1_mid(R)
    step_dk1_low(R)
    r3.step_z()
    pack_a(R, 0)
    r0.start()
    r1.step_t()
    r0.step_t()
    step_dx1_high(R)
    step_dx1_low(R)
    r2.step_s()
    r1.step_s()
    r0.step_s()
    step_da1(R)
    n1.start()
    r3.step_mid()
    r2.step_z()
    r1.step_z()
    r0.step_z()
    n1.to_home()
    r2.step_mid()
    r1.step_mid()
    r0.step_mid()
    rb.step_end()
    r3.step_end()
    r2.step_end()
    r1.step_end()
    r0.step_end()
    n1.end()
    for c in (rb, r3, r2, r1, r0, n1):
        c.drain()


def finish(R, place, chips):
    me, core = place.me, place.core
    loss = jnp.sum(R.loss[...], axis=1, keepdims=True)
    R.half[core, :, 201:208, :] = jnp.broadcast_to(loss, (2, 7, 128))
    both = send(R.half.at[core], R.half.at[core], R.hsem, 0, 1 - core, me)
    both.wait_recv()
    odd = lax.rem(me, 2)
    row = lax.broadcasted_iota(jnp.int32, (256, 128), 0)
    squares = jnp.zeros((1, 128), f32)
    for h in range(2):
        for lane in range(2):
            g = R.half[h, lane]
            keep = row < 201
            if h == 0:
                b_in = row >= 208 + (odd if lane == 0 else 0)
            else:
                b_in = jnp.logical_and(row >= 208, row < 208 + (33 if lane == 0 else 32 + odd))
            g = jnp.where(jnp.logical_or(keep, b_in), g, 0.0)
            squares = squares + rowsum(g * g)
    R.msg[0] = jnp.broadcast_to(jnp.sum(squares, axis=1, keepdims=True), (8, 128))
    R.msg[1] = R.half[0, 0, 200:208, :] + R.half[1, 0, 200:208, :]
    R.news[0] = R.msg[...]
    sent = []
    for d in range(1, chips):
        sent.append(send(R.msg, R.news.at[d], R.nsem, d - 1, core, lax.rem(me + d, chips)))
    for lane in range(2):
        for h in range(2):
            R.flat_a[pl.ds(402 * h + lane, 201, stride=2), :] = R.half[h, lane, 0:201, :]
            R.flat[pl.ds(8 + 96 * h + lane, 48 - 8 * h, stride=2), :] = R.half[h, lane, 208:256 - 8 * h, :]
    grad_b = jnp.where(odd == 1, R.flat[9:170, :], R.flat[8:169, :])
    R.flat_b[0:161, :] = jnp.where(odd == 1, R.flat[9:170, :], R.flat[8:169, :])
    outs = [pltpu.make_async_copy(R.flat_a, R.out_a, R.osem.at[0]), pltpu.make_async_copy(R.flat_b, R.out_b, R.osem.at[1])]
    for c in outs:
        c.start()
    for c in sent:
        c.wait_recv()
    total = R.news[0]
    for d in range(1, chips):
        total = total + R.news[d]
    norm = jnp.sqrt(total[0, 0:1, :])
    R.scalars[0:1, :] = total[1, 7:8, :]
    R.scalars[2:3, :] = norm
    for c in sent:
        c.wait_send()
    both.wait_send()
    for c in outs:
        c.wait()


def update_kernel(*refs):
    ins, scalars, outs, refs = refs[:8], refs[8], refs[9:20], refs[20:]
    bufs, news, in_sem, out_sem = refs[:8], refs[8:16], refs[16], refs[17]
    loads = [pltpu.make_async_copy(a, b, in_sem.at[k]) for k, (a, b) in enumerate(zip(ins, bufs))]
    for c in loads:
        c.start()
    clip = jnp.minimum(1.0, clip_level / (scalars[2:3, :] + 1e-06))
    for k in range(3):
        outs[8 + k][0] = scalars[k, 0]
    stores = []
    for part, rows in ((1, 161), (0, 804)):
        grad, p, m, v = bufs[4 * part:4 * part + 4]
        for c in loads[4 * part:4 * part + 4]:
            c.wait()
        g = grad[0:rows, :] * clip
        first = beta_one * m[...] + (1.0 - beta_one) * g
        second = beta_two * v[...] + (1.0 - beta_two) * g * g
        step = (first * (1.0 / (1.0 - beta_one ** STEP))) / (
            jnp.sqrt(second * (1.0 / (1.0 - beta_two ** STEP))) + adam_eps)
        old = p[...]
        new = old - learn_rate * (step + decay_rate * old)
        for k, value in enumerate((new, first, second, new.astype(bf))):
            news[4 * part + k][...] = value
            c = pltpu.make_async_copy(news[4 * part + k], outs[4 * part + k], out_sem.at[4 * part + k])
            c.start()
            stores.append(c)
    for c in stores:
        c.wait()


IN_ALL = ("steps", "labels", "valid")
LOADED = ("pa", "pb", "img", "nidx", "table")


def comm_scratch(chips):
    return dict(
        pa=((804, 128), f32), pb=((161, 128), f32), img=((NIMG, POS, C), bf), nidx=((NIMG, POS), jnp.int32),
        table=((NT, C), f32),
        w=((chips, 2, PIECE, C), bf), flat=((184, 128), f32), piece=((2, PIECE, 128), f32),
        ga=((2, A_ROWS + 16, 128), f32), gb=((2, B_ROWS + 16, 128), f32), loss=((1, C), f32),
        r1=((chips, PIECE, C), bf), r2=((4, 2, PIECE, C), bf), r3=((4, PIECE, C), bf), r4=((4, 2, PIECE, C), bf),
        t2=((4, 2, PIECE, C), bf), t3=((4, PIECE, C), bf), t4=((4, PIECE, C), bf),
        n1_in=((chips, 8, C), f32), n1_out=((8, C), f32),
        half=((2, 2, PIECE, 128), f32), flat_a=((808, 128), f32), flat_b=((168, 128), f32), msg=((2, 8, 128), f32), news=((chips, 2, 8, 128), f32))


def sem_counts(chips):
    return dict(zsem=3, ssem=4, tsem=8, csem=16, gcsem=5, gtsem=5, gssem=5, gzsem=16, n1sem=chips, hsem=1, nsem=chips - 1)


def whole_kernel(chips, *refs):
    R = Refs()
    refs = list(refs)
    for name in IN_ALL:
        setattr(R, name, refs.pop(0))
    R.sources = [refs.pop(0) for _ in LOADED]
    R.out_a, R.out_b, R.scalars = refs.pop(0), refs.pop(0), refs.pop(0)
    for name in list(SCRATCH) + list(comm_scratch(chips)):
        setattr(R, name, refs.pop(0))
    for name in sem_counts(chips):
        setattr(R, name, (refs.pop(0), refs.pop(0)))
    R.osem, R.isem = refs.pop(0), refs.pop(0)
    place = Place(chips)
    barrier = greet(R, place, chips)
    R.loads = []
    for n, (name, src) in enumerate(zip(LOADED, R.sources)):
        R.loads.append(pltpu.make_async_copy(src, getattr(R, name), R.isem.at[n]))
        R.loads[-1].start()
    for c in R.loads[:2]:
        c.wait()
    own_piece(R, place)
    pl.semaphore_wait(barrier, chips)

    def meanwhile():
        for c in R.loads[2:]:
            c.wait()
        first_setup(R)
    gather_weights(R, place, meanwhile)
    count = spread_rows(R, chips) * POS
    R.scalars[...] = jnp.zeros((8, 128), f32)
    R.scalars[1:2, :] = count
    unpack_weights(R, R.ga, R.gb)
    time_forward(R)
    R.scale_row[...] = 2.0 / jnp.concatenate([count, count], axis=1)
    for step in FORWARD_A + FORWARD_B:
        step(R)
    backward_and_reduce(R, place, chips)
    finish(R, place, chips)


def whole_step(chips, images, timesteps, labels, valid_slot, noise_idx, noise_table,
               params_a, params_b, first_a, second_a, first_b, second_b):
    smem = pl.BlockSpec(memory_space=pltpu.SMEM)
    vmem = pl.BlockSpec(memory_space=pltpu.VMEM)
    hbm = pl.BlockSpec(memory_space=pl.ANY)
    rows = lambda v: v.reshape(-1, 128)
    scratch = [pltpu.VMEM(s, d) for s, d in SCRATCH.values()] + [pltpu.VMEM(s, d) for s, d in comm_scratch(chips).values()]
    for n in sem_counts(chips).values():
        scratch += [pltpu.SemaphoreType.DMA((n,)), pltpu.SemaphoreType.DMA((n,))]
    scratch += [pltpu.SemaphoreType.DMA((2,)), pltpu.SemaphoreType.DMA((5,))]
    pa, pb = rows(params_a), rows(params_b)
    grad_a, grad_b, scalars = pl.pallas_call(
        functools.partial(whole_kernel, chips),
        out_shape=[jax.ShapeDtypeStruct((n, 128), f32) for n in (808, 168, 8)],
        in_specs=[smem] * 3 + [hbm] * 5,
        out_specs=[hbm, hbm, vmem],
        scratch_shapes=scratch,
        compiler_params=pltpu.CompilerParams(
            collective_id=0, has_side_effects=True, vmem_limit_bytes=63 * 1024 * 1024),
    )(timesteps, labels, valid_slot, pa, pb, images, noise_idx, noise_table)
    shapes = [jax.ShapeDtypeStruct((n, 128), d) for n in (804, 161) for d in (f32, f32, f32, bf)]
    buffers = [pltpu.VMEM((n + extra, 128), f32) for n, pad in ((804, 4), (161, 7)) for extra in (pad, 0, 0, 0)]
    outs = pl.pallas_call(
        update_kernel,
        out_shape=shapes + [jax.ShapeDtypeStruct((1,), f32)] * 3,
        in_specs=[hbm] * 8 + [vmem],
        out_specs=[hbm] * 8 + [smem] * 3,
        scratch_shapes=buffers + [pltpu.VMEM(s.shape, s.dtype) for s in shapes] + [pltpu.SemaphoreType.DMA((8,))] * 2,
        compiler_params=pltpu.CompilerParams(vmem_limit_bytes=63 * 1024 * 1024),
    )(grad_a, pa, rows(first_a), rows(second_a), grad_b, pb, rows(first_b), rows(second_b), scalars)
    return (*(v.reshape(-1) for v in outs[:8]), *(v.reshape(()) for v in outs[8:]))


def adam_update(master, grad_in, first_mom, second, clip_scale):
    clipped = grad_in * clip_scale
    first_new = beta_one * first_mom + (1.0 - beta_one) * clipped
    second_new = beta_two * second + (1.0 - beta_two) * clipped * clipped
    first_hat = first_new / (1.0 - beta_one**STEP)
    second_hat = second_new / (1.0 - beta_two**STEP)
    master_new = master - learn_rate * (
        first_hat / (jnp.sqrt(second_hat) + adam_eps) + decay_rate * master
    )
    return (master_new, first_new, second_new)


def plain_step(images, timesteps, labels, valid_slot, noise_idx, noise_table,
               params_a, params_b, first_a, second_a, first_b, second_b):
    gather = lambda v: lax.all_gather(v.astype(bf), "fsdp", axis=0, tiled=True).reshape(-1, C)
    count = lax.psum(jnp.sum(valid_slot).astype(f32) * POS, ("dp", "fsdp"))
    ga, gb, loss = compute(images, timesteps, labels, valid_slot, (2.0 / count).reshape(1), noise_idx, noise_table,
                           gather(params_a), gather(params_b))
    flat = lambda g: jnp.concatenate([g[0], g[1]], axis=1).reshape(-1)
    shard = lambda g: lax.psum_scatter(flat(g), "fsdp", scatter_dimension=0, tiled=True)
    part_a, part_b, loss = lax.psum((shard(ga), shard(gb), jnp.sum(loss)), "dp")
    loss, squares = lax.psum((loss, jnp.sum(part_a * part_a) + jnp.sum(part_b * part_b)), "fsdp")
    norm = jnp.sqrt(squares)
    clip = jnp.minimum(1.0, clip_level / (norm + 1e-06))
    new_a = adam_update(params_a, part_a, first_a, second_a, clip)
    new_b = adam_update(params_b, part_b, first_b, second_b, clip)
    return (*new_a, new_a[0].astype(bf), *new_b, new_b[0].astype(bf), loss, count, norm)


def solution(mesh):
    chips = mesh.shape["fsdp"]
    if chips == 16 and mesh.shape["dp"] == 2:
        step = functools.partial(whole_step, chips)
    else:
        step = plain_step
    both = P(("dp", "fsdp"))
    return jax.shard_map(
        step, mesh=mesh,
        in_specs=(both, both, both, both, both, P()) + (P("fsdp"),) * 6,
        out_specs=(P("fsdp"),) * 8 + (P(),) * 3,
        check_vma=False)
```
